32 devices in a mesh: dp: 8 (over y, x, core), seq: 4 (over z).
Axes of the slice: x: 2, y: 2, z: 4, core: 2. Of those that a mesh axis runs over, the one named last changes fastest.
Arguments:
- block_input: bfloat16 [32, 1024, 1152], P('dp', 'seq'), may hold values from -6 to 6
- modulation: bfloat16 [32, 4, 6912], P('dp'), may hold values from -3 to 3
- segment_ids: int32 [32, 1024], P('dp', 'seq'), may hold values from 0 to 3, as said below
- qkv_weight: bfloat16 [1152, 3456], P('seq'), may hold values from -0.1875 to 0.1875
- query_value_bias: bfloat16 [2304], replicated, may hold values from -3 to 3
- attn_out_weight: bfloat16 [1152, 1152], P('seq'), may hold values from -1.5 to 1.5
- attn_out_bias: bfloat16 [1152], replicated, may hold values from -3 to 3
- mlp_in_weight: bfloat16 [1152, 4608], P('seq'), may hold values from -0.1875 to 0.1875
- mlp_in_bias: bfloat16 [4608], replicated, may hold values from -3 to 3
- mlp_out_weight: bfloat16 [4608, 1152], P('seq'), may hold values from -0.1875 to 0.1875
- mlp_out_bias: bfloat16 [1152], replicated, may hold values from -3 to 3
- proj_in_weight: bfloat16 [1152, 2048], P('seq'), may hold values from -0.1875 to 0.1875
- proj_in_bias: bfloat16 [2048], replicated, may hold values from -3 to 3
- proj_mid_weight: bfloat16 [2048, 2048], P('seq'), may hold values from -0.125 to 0.125
- proj_mid_bias: bfloat16 [2048], replicated, may hold values from -3 to 3
- proj_out_weight: bfloat16 [2048, 768], P('seq'), may hold values from -0.125 to 0.125
- proj_out_bias: bfloat16 [768], replicated, may hold values from -2 to 2
- targets: bfloat16 [32, 1024, 768], P('dp', 'seq'), may hold values from -6 to 6
Outputs:
- block_out: bfloat16 [32, 1024, 1152], P('dp', 'seq')
- grad_input: float32 [32, 1024, 1152], P('dp', 'seq')
- grad_modulation: float32 [32, 4, 6912], P('dp')
- grad_qkv_weight: float32 [1152, 3456], P('seq')
- grad_query_value_bias: float32 [2304], P('seq')
- grad_attn_out_weight: float32 [1152, 1152], P('seq')
- grad_attn_out_bias: float32 [1152], P('seq')
- grad_mlp_in_weight: float32 [1152, 4608], P('seq')
- grad_mlp_in_bias: float32 [4608], P('seq')
- grad_mlp_out_weight: float32 [4608, 1152], P('seq')
- grad_mlp_out_bias: float32 [1152], P('seq')
- grad_proj_in_weight: float32 [1152, 2048], P('seq')
- grad_proj_in_bias: float32 [2048], P('seq')
- grad_proj_mid_weight: float32 [2048, 2048], P('seq')
- grad_proj_mid_bias: float32 [2048], P('seq')
- grad_proj_out_weight: float32 [2048, 768], P('seq')
- grad_proj_out_bias: float32 [768], P('seq')
The draws below stay inside these ranges and needn't reach their ends.
Inputs may be any that keep to these rules, and one draw needn't show every extreme that they name: `segment_ids`: along each row the numbers never fall and each of 0 to 3 occurs; in each row one image, which one drawn at random, takes all positions but fewer than 256.
All inputs are finite; a program needn't handle non-finite values.
Results may differ from the reference program's by a relative error of at most 0.025.
Values may be sent and summed in bfloat16 or wider, within the bound.
A program may use at most 512 MiB of HBM per device.

```python
import jax
import jax.numpy as jnp
from jax import lax

D = 1152
HEADS = 16
HEAD_DIM = 72
MLP = 4608
DH = 2048
DZ = 768
ROW_LEN = 1024
SEGS = 4
ROWS_ALL = 32
SPAN = 256


def draw_segment_ids(key, part):
    key = jax.random.fold_in(key, 7)
    subkeys = jax.random.split(key, 2)
    short_most = max((SPAN - 1) // (SEGS - 1), 1)
    lengths = jax.random.randint(subkeys[0], (ROWS_ALL, SEGS), 1, short_most + 1)
    longest = jax.random.randint(subkeys[1], (ROWS_ALL, 1), 0, SEGS)
    is_long = jnp.arange(SEGS)[None, :] == longest
    others = jnp.sum(jnp.where(is_long, 0, lengths), axis=1, keepdims=True)
    lengths = jnp.where(is_long, ROW_LEN - others, lengths)
    bounds = jnp.cumsum(lengths, axis=1)
    places = jnp.arange(ROW_LEN)
    passed = places[None, :, None] >= bounds[:, None, :SEGS - 1]
    return jnp.sum(passed.astype(jnp.int32), axis=2).astype(jnp.int32)


def shard_levels(key, extent, shards, least, high):
    def one(position, blocks):
        steps = jax.random.uniform(jax.random.fold_in(jax.random.fold_in(key, 6), position), (blocks,), jnp.float32, least / len(shards), high / len(shards))
        return jnp.repeat(jnp.exp(steps), extent[position] // blocks).reshape((-1,) + (1,) * (len(extent) - position - 1))

    level = one(*shards[0])
    for cut in shards[1:]:
        level = level * one(*cut)
    return level


def normal_values(stream_key, shape, scale, limit, cuts=(), held_as=jnp.bfloat16):
    values = jax.random.normal(stream_key, shape, jnp.float32) * scale
    if len(cuts) > 0:
        values = shard_levels(stream_key, shape, cuts, -0.22, 0.18) * values
    return jnp.clip(values, min=-limit, max=limit).astype(held_as)


def setup_inputs(seed: int = 0) -> dict:
    splits = jax.random.split(jax.random.key(seed), 19)
    block_input = normal_values(splits[0], (ROWS_ALL, ROW_LEN, D), 1.0, 6.0, ((0, 8), (1, 4)))
    modulation = normal_values(splits[1], (ROWS_ALL, SEGS, 6 * D), 0.5, 3.0, ((0, 8),))
    segment_ids = draw_segment_ids(jax.random.fold_in(splits[18], 71), 0)
    qkv_weight = normal_values(splits[3], (D, 3 * D), D ** -0.5, 0.1875, ((0, 4),))
    query_value_bias = normal_values(splits[4], (2 * D,), 0.5, 3.0)
    attn_out_weight = normal_values(splits[5], (D, D), (D // 64) ** -0.5, 1.5, ((0, 4),))
    attn_out_bias = normal_values(splits[6], (D,), 0.5, 3.0)
    mlp_in_weight = normal_values(splits[7], (D, MLP), D ** -0.5, 0.1875, ((0, 4),))
    mlp_in_bias = normal_values(splits[8], (MLP,), 0.5, 3.0)
    mlp_out_weight = normal_values(splits[9], (MLP, D), (MLP // 4) ** -0.5, 0.1875, ((0, 4),))
    mlp_out_bias = normal_values(splits[10], (D,), 0.5, 3.0)
    proj_in_weight = normal_values(splits[11], (D, DH), D ** -0.5, 0.1875, ((0, 4),))
    proj_in_bias = normal_values(splits[12], (DH,), 0.5, 3.0)
    proj_mid_weight = normal_values(splits[13], (DH, DH), DH ** -0.5, 0.125, ((0, 4),))
    proj_mid_bias = normal_values(splits[14], (DH,), 0.5, 3.0)
    proj_out_weight = normal_values(splits[15], (DH, DZ), DH ** -0.5, 0.125, ((0, 4),))
    proj_out_bias = normal_values(splits[16], (DZ,), 0.3, 2.0)
    targets = normal_values(splits[17], (ROWS_ALL, ROW_LEN, DZ), 1.0, 6.0, ((0, 8), (1, 4)))
    return {"block_input": block_input, "modulation": modulation, "segment_ids": segment_ids, "qkv_weight": qkv_weight, "query_value_bias": query_value_bias, "attn_out_weight": attn_out_weight, "attn_out_bias": attn_out_bias, "mlp_in_weight": mlp_in_weight, "mlp_in_bias": mlp_in_bias, "mlp_out_weight": mlp_out_weight, "mlp_out_bias": mlp_out_bias, "proj_in_weight": proj_in_weight, "proj_in_bias": proj_in_bias, "proj_mid_weight": proj_mid_weight, "proj_mid_bias": proj_mid_bias, "proj_out_weight": proj_out_weight, "proj_out_bias": proj_out_bias, "targets": targets}


@jax.custom_vjp
def low(v):
    return lax.optimization_barrier(v.astype(jnp.bfloat16)).astype(jnp.float32)

@jax.custom_vjp
def low_back(v):
    return v

def low_keep(v):
    return (low(v), None)

def low_pass(kept, grad):
    return (grad,)

def back_keep(v):
    return (v, None)

def back_low(kept, grad):
    return (low(grad),)
low.defvjp(low_keep, low_pass)
low_back.defvjp(back_keep, back_low)
HIGHEST = lax.Precision.HIGHEST
EPSILON = 1e-06

def matmul(left, right):
    return jnp.dot(left, right, precision=HIGHEST)

def layer_norm(values):
    centred = values - lax.optimization_barrier(jnp.mean(values, axis=-1, keepdims=True))
    return centred * lax.rsqrt(lax.optimization_barrier(jnp.mean(centred * centred, axis=-1, keepdims=True)) + EPSILON)

def attend_row(qkv_row, seg_row):
    parts = qkv_row.reshape(ROW_LEN, 3, HEADS, HEAD_DIM)
    query = parts[:, 0]
    keys = parts[:, 1]
    values = parts[:, 2]
    scores = jnp.einsum('qhd,khd->hqk', query, keys, precision=HIGHEST) * HEAD_DIM ** (-0.5)
    scores = low_back(scores)
    same = seg_row[:, None] == seg_row[None, :]
    scores = jnp.where(same[None], scores, -1e+30)
    probs = low(jax.nn.softmax(scores, axis=-1))
    return jnp.einsum('hqk,khd->qhd', probs, values, precision=HIGHEST).reshape(ROW_LEN, D)

def attend_pair(pair):
    return jax.checkpoint(attend_row)(pair[0], pair[1])

def forward(inputs, modulation, qkv_weight, query_value_bias, attn_out_weight, attn_out_bias, mlp_in_weight, mlp_in_bias, mlp_out_weight, mlp_out_bias, proj_in_weight, proj_in_bias, proj_mid_weight, proj_mid_bias, proj_out_weight, proj_out_bias, segment_ids, goals):
    one_hot = (segment_ids[:, :, None] == jnp.arange(SEGS, dtype=jnp.int32)[None, None, :]).astype(jnp.float32)
    mod_tok = jnp.einsum('rcs,rsd->rcd', one_hot, modulation, precision=HIGHEST)
    shift1 = mod_tok[..., :D]
    scale1 = mod_tok[..., D:2 * D]
    gate1 = mod_tok[..., 2 * D:3 * D]
    shift2 = mod_tok[..., 3 * D:4 * D]
    scale2 = mod_tok[..., 4 * D:5 * D]
    gate2 = mod_tok[..., 5 * D:]
    modulated1 = low(layer_norm(inputs) * (1.0 + scale1) + shift1)
    full_bias = jnp.concatenate([query_value_bias[:D], jnp.zeros((D,), jnp.float32), query_value_bias[D:]])
    qkv = low_back(low(matmul(modulated1.reshape(-1, D), qkv_weight) + full_bias))
    qkv = qkv.reshape(ROWS_ALL, ROW_LEN, 3 * D)
    attended = lax.map(attend_pair, (qkv, segment_ids))
    attended = low_back(low(attended))
    branch = low_back(matmul(attended.reshape(-1, D), attn_out_weight) + attn_out_bias).reshape(inputs.shape)
    middle = inputs + gate1 * branch
    modulated2 = low(layer_norm(middle) * (1.0 + scale2) + shift2)
    hmid = low_back(matmul(modulated2.reshape(-1, D), mlp_in_weight) + mlp_in_bias)
    act_mid = low(jax.nn.gelu(hmid, approximate=True))
    mlp_branch = low_back(matmul(act_mid, mlp_out_weight) + mlp_out_bias).reshape(inputs.shape)
    block_out = low(middle + gate2 * mlp_branch)
    hidden1 = low_back(matmul(block_out.reshape(-1, D), proj_in_weight) + proj_in_bias)
    act1 = low(jax.nn.silu(hidden1))
    hidden2 = low_back(matmul(act1, proj_mid_weight) + proj_mid_bias)
    act2 = low(jax.nn.silu(hidden2))
    feats = low_back(matmul(act2, proj_out_weight) + proj_out_bias)
    flat_goals = goals.reshape(-1, DZ)
    feat_unit = feats * lax.rsqrt(lax.optimization_barrier(jnp.sum(feats * feats, axis=-1, keepdims=True)) + EPSILON)
    goal_unit = flat_goals * lax.rsqrt(lax.optimization_barrier(jnp.sum(flat_goals * flat_goals, axis=-1, keepdims=True)) + EPSILON)
    cosine = lax.optimization_barrier(jnp.sum(feat_unit * goal_unit, axis=-1))
    loss = -(0.5 * DZ) * jnp.sum(cosine)
    return (loss, block_out)

def reference(block_input, modulation, segment_ids, qkv_weight, query_value_bias, attn_out_weight, attn_out_bias, mlp_in_weight, mlp_in_bias, mlp_out_weight, mlp_out_bias, proj_in_weight, proj_in_bias, proj_mid_weight, proj_mid_bias, proj_out_weight, proj_out_bias, targets):
    floats = [arr.astype(jnp.float32) for arr in (block_input, modulation, qkv_weight, query_value_bias, attn_out_weight, attn_out_bias, mlp_in_weight, mlp_in_bias, mlp_out_weight, mlp_out_bias, proj_in_weight, proj_in_bias, proj_mid_weight, proj_mid_bias, proj_out_weight, proj_out_bias)]
    goals = targets.astype(jnp.float32)

    def objective(*params):
        return forward(*params, segment_ids, goals)
    loss, pullback, block_out = jax.vjp(objective, *floats, has_aux=True)
    grads = pullback(jnp.ones_like(loss))
    return (block_out.astype(jnp.bfloat16), grads[0], grads[1], grads[2], grads[3], grads[4], grads[5], grads[6], grads[7], grads[8], grads[9], grads[10], grads[11], grads[12], grads[13], grads[14], grads[15])
```

```python
import functools
import math

import jax
import jax.numpy as jnp
from jax import lax
from jax.experimental import pallas as pl
from jax.experimental.pallas import tpu as pltpu
from jax.sharding import PartitionSpec as P

HEAD_DIM = 72
EPSILON = 1e-06
GELU_COEF = 0.044715
MASKED = -1e30
LOG2E = 1.4426950408889634
LANES = 128
BF = jnp.bfloat16
F32 = jnp.float32


def dot_nn(left, right):
    return jnp.dot(left, right, preferred_element_type=F32)


def dot_tn(left, right):
    return lax.dot_general(left, right, (((0,), (0,)), ((), ())), preferred_element_type=F32)


def dot_nt(left, right):
    return lax.dot_general(left, right, (((1,), (1,)), ((), ())), preferred_element_type=F32)


def silu_grad(value):
    sigmoid_val = jax.nn.sigmoid(value)
    return sigmoid_val * (1.0 + value * (1.0 - sigmoid_val))


def gelu_grad(value):
    factor = math.sqrt(2.0 / math.pi)
    tangent = jnp.tanh(factor * (value + GELU_COEF * value * value * value))
    return 0.5 * (1.0 + tangent) + 0.5 * value * (1.0 - tangent * tangent) * factor * (
        1.0 + 3.0 * GELU_COEF * value * value
    )


def norm_stats(values):
    centred = values - jnp.mean(values, axis=-1, keepdims=True)
    inv_std = lax.rsqrt(jnp.mean(centred * centred, axis=-1, keepdims=True) + EPSILON)
    return (centred * inv_std, inv_std)


def norm_back(grad_normed, normed, inv_std):
    return inv_std * (
        grad_normed
        - jnp.mean(grad_normed, axis=-1, keepdims=True)
        - normed * jnp.mean(grad_normed * normed, axis=-1, keepdims=True)
    )


def head_window(head, width):
    tile = jnp.minimum((head * HEAD_DIM) // LANES, width // LANES - 2)
    base = pl.multiple_of(tile * LANES, LANES)
    offset = head * HEAD_DIM - base
    lane = lax.broadcasted_iota(jnp.int32, (1, 2 * LANES), 1)
    mine = (lane >= offset) & (lane < offset + HEAD_DIM)
    spare = jnp.where(offset >= 4, 0, LANES)
    return base, mine, lane - spare, offset >= 4


def with_segments(block, mine, lane, seg, hit, miss):
    code = jnp.where(lane == seg, hit, miss)
    code = jnp.where((lane >= 0) & (lane < 4), code, 0.0)
    return jnp.where(mine, block.astype(F32), code).astype(BF)


def attend_forward_kernel(q_ref, k_ref, v_ref, segq_ref, segk_ref, out_ref, total_ref, *, block):
    head = pl.program_id(0)
    width = q_ref.shape[1]
    base, mine, lane, low = head_window(head, width)
    window = pl.ds(base, 2 * LANES)
    factor = HEAD_DIM ** (-0.5) * LOG2E
    keys = with_segments(k_ref[:, window], mine, lane, segk_ref[...], 0.0, 1.0)
    values = jnp.where(
        mine, v_ref[:, window].astype(F32), jnp.where(lane == 0, 1.0, 0.0)
    ).astype(BF)
    values_t = values.T
    for start in range(0, q_ref.shape[0], block):
        rows = pl.ds(start, block)
        query = with_segments(q_ref[rows, window], mine, lane, segq_ref[rows, :], MASKED, 0.0)
        scores = dot_nt(keys, query) * factor
        top = jnp.max(scores, axis=0, keepdims=True)
        weights = jnp.exp2(scores - top).astype(BF)
        gathered = dot_nn(values_t, weights)
        total = jnp.where(low, gathered[0:1], gathered[LANES : LANES + 1])
        result = (gathered * (1.0 / total)).T
        out_ref[rows, window] = jnp.where(
            mine, result, out_ref[rows, window].astype(F32)
        ).astype(BF)
        total_ref[pl.ds(head, 1), rows] = top + jnp.log2(total)


def whole(shape):
    return pl.BlockSpec(shape, lambda *_: (0,) * len(shape))


def attend_forward(parts, seg_query, seg_keys, heads):
    (query, qcol), (keys, kcol), (values, vcol) = parts
    count, tokens = seg_query.shape[0], seg_keys.shape[0]
    width = heads * HEAD_DIM
    return pl.pallas_call(
        functools.partial(attend_forward_kernel, block=min(256, count)),
        grid=(heads,),
        in_specs=[
            pl.BlockSpec((count, width), lambda h: (0, qcol)),
            pl.BlockSpec((tokens, width), lambda h: (0, kcol)),
            pl.BlockSpec((tokens, width), lambda h: (0, vcol)),
            whole((count, 1)),
            whole((tokens, 1)),
        ],
        out_specs=[whole((count, width)), whole((heads, count))],
        out_shape=[
            jax.ShapeDtypeStruct((count, width), BF),
            jax.ShapeDtypeStruct((heads, count), F32),
        ],
        compiler_params=pltpu.CompilerParams(vmem_limit_bytes=56 * 1024 * 1024),
        cost_estimate=pl.CostEstimate(
            flops=heads * count * tokens * 4 * 256,
            bytes_accessed=2 * width * (2 * count + 2 * tokens),
            transcendentals=heads * count * tokens,
        ),
        name="attend_forward",
    )(query, keys, values, seg_query, seg_keys)


def attend_backward_kernel(
    q_ref, k_ref, v_ref, segq_ref, segk_ref, total_ref, out_ref, grad_ref, *rest, block, columns
):
    grads, dots = rest[:-1], rest[-1]
    dq_ref, dk_ref, dv_ref = grads if len(grads) == 3 else grads * 3
    head = pl.program_id(0)
    width = q_ref.shape[1]
    count = q_ref.shape[0]
    factor = HEAD_DIM ** (-0.5) * LOG2E

    @pl.when(head == 0)
    def _():
        row = lax.broadcasted_iota(jnp.int32, dots.shape[:1] + (width,), 0)
        col = lax.broadcasted_iota(jnp.int32, dots.shape[:1] + (width,), 1)
        pick = ((col >= row * HEAD_DIM) & (col < (row + 1) * HEAD_DIM)).astype(F32).astype(BF)
        for start in range(0, count, block):
            rows = pl.ds(start, block)
            product = out_ref[rows, :].astype(F32) * grad_ref[rows, :].astype(F32)
            high = product.astype(BF)
            rest_part = (product - high.astype(F32)).astype(BF)
            dots[:, rows] = dot_nt(pick, high) + dot_nt(pick, rest_part)

    base, mine, lane, _ = head_window(head, width)
    window = pl.ds(base, 2 * LANES)
    keys = with_segments(k_ref[:, window], mine, lane, segk_ref[...], 0.0, 1.0)
    keys_t = keys.T
    values = v_ref[:, window]
    grad_keys = None
    for start in range(0, count, block):
        rows = pl.ds(start, block)
        query = with_segments(q_ref[rows, window], mine, lane, segq_ref[rows, :], MASKED, 0.0)
        grad = jnp.where(mine, grad_ref[rows, window].astype(F32), 0.0).astype(BF)
        scores = dot_nt(keys, query) * factor
        probs = jnp.exp2(scores - total_ref[pl.ds(head, 1), rows])
        grad_probs = dot_nt(values, grad)
        grad_scores = (probs * (grad_probs - dots[pl.ds(head, 1), rows])).astype(BF)
        part_v = dot_nn(probs.astype(BF), grad)
        part_k = dot_nn(grad_scores, query)
        if grad_keys is None:
            grad_keys, grad_values = part_k, part_v
        else:
            grad_keys, grad_values = grad_keys + part_k, grad_values + part_v
        grad_query = (dot_nn(keys_t, grad_scores) * HEAD_DIM ** (-0.5)).T
        put(dq_ref, rows, base + columns[0], mine, grad_query)
    every = pl.ds(0, k_ref.shape[0])
    put(dk_ref, every, base + columns[1], mine, grad_keys * HEAD_DIM ** (-0.5))
    put(dv_ref, every, base + columns[2], mine, grad_values)


def put(ref, rows, base, mine, value):
    window = pl.ds(pl.multiple_of(base, LANES), 2 * LANES)
    ref[rows, window] = jnp.where(mine, value, ref[rows, window].astype(F32)).astype(BF)


def attend_backward(parts, seg_query, seg_keys, totals, out, grad, heads):
    (query, qcol), (keys, kcol), (values, vcol) = parts
    count, tokens = seg_query.shape[0], seg_keys.shape[0]
    width = heads * HEAD_DIM
    if count == tokens:
        shapes = [(count, 3 * width)]
        columns = (0, width, 2 * width)
    else:
        shapes = [(count, width), (tokens, width), (tokens, width)]
        columns = (0, 0, 0)
    return pl.pallas_call(
        functools.partial(attend_backward_kernel, block=min(256, count), columns=columns),
        grid=(heads,),
        in_specs=[
            pl.BlockSpec((count, width), lambda h: (0, qcol)),
            pl.BlockSpec((tokens, width), lambda h: (0, kcol)),
            pl.BlockSpec((tokens, width), lambda h: (0, vcol)),
            whole((count, 1)),
            whole((tokens, 1)),
            whole((heads, count)),
            whole((count, width)),
            whole((count, width)),
        ],
        out_specs=[whole(shape) for shape in shapes],
        out_shape=[jax.ShapeDtypeStruct(shape, BF) for shape in shapes],
        scratch_shapes=[pltpu.VMEM((heads, count), F32)],
        compiler_params=pltpu.CompilerParams(vmem_limit_bytes=60 * 1024 * 1024),
        cost_estimate=pl.CostEstimate(
            flops=heads * count * tokens * 10 * 256,
            bytes_accessed=2 * width * (4 * count + 4 * tokens),
            transcendentals=heads * count * tokens,
        ),
        name="attend_backward",
    )(query, keys, values, seg_query, seg_keys, totals, out, grad)


class Rows:
    def __init__(self, seq, rows):
        self.seq, self.rows = seq, rows
        self.share = seq // rows
        here = lax.axis_index("seq")
        self.row, self.part = here // self.share, here % self.share

    def device(self, row, part):
        return (row % self.rows) * self.share + part % self.share

    def shift_rows(self, shift):
        return [
            (self.device(r, p), self.device(r + shift, p))
            for r in range(self.rows)
            for p in range(self.share)
        ]

    def shift_parts(self, shift):
        return [
            (self.device(r, p), self.device(r, p + shift))
            for r in range(self.rows)
            for p in range(self.share)
        ]

    def to_rows(self, array):
        pieces = []
        for shift in range(self.rows):
            piece = lax.dynamic_index_in_dim(
                array, (self.row + shift) % self.rows, 0, keepdims=False
            )
            if shift:
                piece = lax.ppermute(piece, "seq", self.shift_rows(shift))
            pieces.append(piece)
        return pieces

    def to_spans(self, pieces):
        result = jnp.zeros((self.rows,) + pieces[0].shape, pieces[0].dtype)
        for shift, piece in enumerate(pieces):
            if shift:
                piece = lax.ppermute(piece, "seq", self.shift_rows(-shift))
            result = lax.dynamic_update_index_in_dim(
                result, piece, (self.row + shift) % self.rows, 0
            )
        return result

    def gather_parts(self, array):
        return jnp.concatenate(
            [array]
            + [
                lax.ppermute(array, "seq", self.shift_parts(shift))
                for shift in range(1, self.share)
            ],
            axis=0,
        )

    def sum_parts(self, array):
        count = array.shape[0] // self.share
        total = array[:count].astype(F32)
        for shift in range(1, self.share):
            piece = array[shift * count : (shift + 1) * count]
            total = total + lax.ppermute(piece, "seq", self.shift_parts(-shift)).astype(F32)
        return total.astype(array.dtype)

    def all_parts(self, array):
        total = array
        for shift in range(1, self.share):
            total = total + lax.ppermute(array, "seq", self.shift_parts(shift))
        return total


def gather_bundle(bundle):
    copies = lax.axis_size("dp")
    count = bundle.shape[0] // copies
    own = lax.dynamic_slice_in_dim(bundle, lax.axis_index("dp") * count, count, 0)
    full = lax.all_gather(own, ("seq", "dp"), axis=0, tiled=True)
    return full.reshape(lax.axis_size("seq"), bundle.shape[0], bundle.shape[1])


def reduce_bundle(bundle):
    flat = bundle.reshape(-1, bundle.shape[2])
    own = lax.psum_scatter(flat, ("seq", "dp"), scatter_dimension=0, tiled=True)
    return lax.all_gather(own, "dp", axis=0, tiled=True)


def stack_columns(weight, width):
    return [weight[:, start : start + width] for start in range(0, weight.shape[1], width)]


def split_rows(full, count):
    return [
        full[:, start : start + count].reshape(-1, full.shape[2])
        for start in range(0, full.shape[1], count)
    ]


def local(
    block_input,
    modulation,
    segment_ids,
    qkv_weight,
    query_value_bias,
    attn_out_weight,
    attn_out_bias,
    mlp_in_weight,
    mlp_in_bias,
    mlp_out_weight,
    mlp_out_bias,
    proj_in_weight,
    proj_in_bias,
    proj_mid_weight,
    proj_mid_bias,
    proj_out_weight,
    proj_out_bias,
    targets,
):
    rows, span, width = block_input.shape
    segs = modulation.shape[1]
    seq = lax.axis_size("seq")
    place = Rows(seq, rows)
    heads = width // HEAD_DIM
    hidden = mlp_in_weight.shape[1]
    inner = proj_mid_weight.shape[1]
    goal_width = targets.shape[2]
    tokens = rows * span
    share = place.share

    x_in = jnp.concatenate(place.to_rows(block_input), axis=0)
    seg_pieces = place.to_rows(segment_ids)
    segs_own = jnp.concatenate(seg_pieces, axis=0)
    seg_query = segs_own[:, None]
    seg_keys = place.gather_parts(seg_query) if share > 1 else seg_query
    goals = jnp.concatenate(place.to_rows(targets), axis=0)
    mod_row = lax.dynamic_index_in_dim(modulation, place.row, 0, keepdims=False)

    per = qkv_weight.shape[0]
    first = gather_bundle(
        jnp.concatenate(stack_columns(qkv_weight, width) + [attn_out_weight], axis=0)
    )
    second = gather_bundle(jnp.concatenate(stack_columns(mlp_in_weight, width), axis=0))
    third = gather_bundle(mlp_out_weight)
    half = inner // 2
    fourth = gather_bundle(
        jnp.concatenate(stack_columns(proj_in_weight, half), axis=0)
    )
    fifth = gather_bundle(proj_mid_weight)
    sixth = gather_bundle(proj_out_weight)
    w_q, w_k, w_v, w_attn = split_rows(first, per)
    w_qkv = jnp.concatenate([w_q, w_k, w_v], axis=1)
    w_mlp_in = jnp.concatenate(split_rows(second, per), axis=1)
    w_mlp_out = third.reshape(hidden, width)
    w_proj_in = jnp.concatenate(split_rows(fourth, per), axis=1)
    w_proj_mid = fifth.reshape(inner, inner)
    w_proj_out = sixth.reshape(inner, goal_width)

    one_hot = (segs_own[:, None] == jnp.arange(segs, dtype=jnp.int32)[None, :]).astype(BF)
    inputs = x_in.astype(F32)
    mod_tok = dot_nn(one_hot, mod_row)
    shift1, scale1, gate1, shift2, scale2, gate2 = (
        mod_tok[:, part * width : (part + 1) * width] for part in range(6)
    )
    normed1, inv_std1 = norm_stats(inputs)
    modulated1 = (normed1 * (1.0 + scale1) + shift1).astype(BF)
    bias_float = query_value_bias.astype(F32)
    full_bias = jnp.concatenate(
        [bias_float[:width], jnp.zeros((width,), F32), bias_float[width:]]
    )
    qkv = (dot_nn(modulated1, w_qkv) + full_bias).astype(BF)
    if share > 1:
        kv_all = place.gather_parts(qkv[:, width:])
        parts = ((qkv, 0), (kv_all, 0), (kv_all, 1))
    else:
        parts = ((qkv, 0), (qkv, 1), (qkv, 2))
    attended, totals = attend_forward(parts, seg_query, seg_keys, heads)
    branch = dot_nn(attended, w_attn) + attn_out_bias.astype(F32)
    middle = inputs + gate1 * branch
    normed2, inv_std2 = norm_stats(middle)
    modulated2 = (normed2 * (1.0 + scale2) + shift2).astype(BF)
    hmid = dot_nn(modulated2, w_mlp_in) + mlp_in_bias.astype(F32)
    act_mid = jax.nn.gelu(hmid, approximate=True).astype(BF)
    mlp_branch = dot_nn(act_mid, w_mlp_out) + mlp_out_bias.astype(F32)
    out_low = (middle + gate2 * mlp_branch).astype(BF)
    hidden1 = dot_nn(out_low, w_proj_in) + proj_in_bias.astype(F32)
    act1 = jax.nn.silu(hidden1).astype(BF)
    hidden2 = dot_nn(act1, w_proj_mid) + proj_mid_bias.astype(F32)
    act2 = jax.nn.silu(hidden2).astype(BF)
    feats = dot_nn(act2, w_proj_out) + proj_out_bias.astype(F32)
    goals = goals.astype(F32)
    inv_feat = lax.rsqrt(jnp.sum(feats * feats, axis=-1, keepdims=True) + EPSILON)
    feat_unit = feats * inv_feat
    goal_unit = goals * lax.rsqrt(jnp.sum(goals * goals, axis=-1, keepdims=True) + EPSILON)
    cosine = jnp.sum(feat_unit * goal_unit, axis=-1, keepdims=True)
    loss_weight = 0.5 * goal_width
    grad_feats = (-loss_weight * inv_feat * (goal_unit - cosine * feat_unit)).astype(BF)

    def blocks(grad, cut):
        low = grad.astype(BF).reshape(seq, grad.shape[0] // seq, grad.shape[1])
        return [low[:, :, start : start + cut] for start in range(0, grad.shape[1], cut)]

    sixth_sum = reduce_bundle(
        jnp.concatenate(blocks(dot_tn(act2, grad_feats), goal_width), axis=1)
    )
    bias_out = jnp.sum(grad_feats.astype(F32), axis=0)
    grad_hidden2 = (dot_nt(grad_feats, w_proj_out) * silu_grad(hidden2)).astype(BF)
    fifth_sum = reduce_bundle(jnp.concatenate(blocks(dot_tn(act1, grad_hidden2), inner), axis=1))
    bias_mid = jnp.sum(grad_hidden2.astype(F32), axis=0)
    grad_hidden1 = (dot_nt(grad_hidden2, w_proj_mid) * silu_grad(hidden1)).astype(BF)
    fourth_sum = reduce_bundle(jnp.concatenate(blocks(dot_tn(out_low, grad_hidden1), half), axis=1))
    bias_in = jnp.sum(grad_hidden1.astype(F32), axis=0)
    grad_output = dot_nt(grad_hidden1, w_proj_in)
    grad_gate2 = grad_output * mlp_branch
    grad_mlp = (grad_output * gate2).astype(BF)
    third_sum = reduce_bundle(jnp.concatenate(blocks(dot_tn(act_mid, grad_mlp), width), axis=1))
    bias_ff_out = jnp.sum(grad_mlp.astype(F32), axis=0)
    grad_hmid = (dot_nt(grad_mlp, w_mlp_out) * gelu_grad(hmid)).astype(BF)
    second_sum = reduce_bundle(jnp.concatenate(blocks(dot_tn(modulated2, grad_hmid), width), axis=1))
    bias_ff_in = jnp.sum(grad_hmid.astype(F32), axis=0)
    grad_modulated2 = dot_nt(grad_hmid, w_mlp_in)
    grad_middle = grad_output + norm_back(grad_modulated2 * (1.0 + scale2), normed2, inv_std2)
    grad_gate1 = grad_middle * branch
    grad_branch = (grad_middle * gate1).astype(BF)
    grad_attn_w = dot_tn(attended, grad_branch)
    bias_attn = jnp.sum(grad_branch.astype(F32), axis=0)
    grad_attended = dot_nt(grad_branch, w_attn).astype(BF)
    grads = attend_backward(parts, seg_query, seg_keys, totals, attended, grad_attended, heads)
    if share > 1:
        grad_qkv = jnp.concatenate(
            [grads[0], place.sum_parts(grads[1]), place.sum_parts(grads[2])], axis=1
        )
    else:
        grad_qkv = grads[0]
    first_sum = reduce_bundle(
        jnp.concatenate(
            blocks(dot_tn(modulated1, grad_qkv), width) + blocks(grad_attn_w, width), axis=1
        )
    )
    column_sums = jnp.sum(grad_qkv.astype(F32), axis=0)
    bias_qv = jnp.concatenate([column_sums[:width], column_sums[2 * width :]])
    grad_modulated1 = dot_nt(grad_qkv, w_qkv)
    grad_input = grad_middle + norm_back(grad_modulated1 * (1.0 + scale1), normed1, inv_std1)

    def by_segment(value):
        return dot_tn(one_hot, value.astype(BF))

    grad_mod = jnp.concatenate(
        [
            by_segment(grad_modulated1),
            by_segment(grad_modulated1 * normed1),
            by_segment(grad_gate1),
            by_segment(grad_modulated2),
            by_segment(grad_modulated2 * normed2),
            by_segment(grad_gate2),
        ],
        axis=-1,
    )
    grad_mod = place.all_parts(grad_mod)
    grad_modulation = lax.all_gather(grad_mod.astype(BF), "seq", axis=0)[:: share].astype(F32)

    def back(value):
        return place.to_spans(
            [value[shift * span : (shift + 1) * span] for shift in range(rows)]
        )

    block_out = back(out_low)
    grad_input = back(grad_input.astype(BF)).astype(F32)

    biases = [bias_qv, bias_attn, bias_ff_in, bias_ff_out, bias_in, bias_mid, bias_out]
    packed = jnp.concatenate([bias.reshape(seq, -1) for bias in biases], axis=1)
    packed = lax.psum(packed, ("dp", "seq"))
    packed = lax.dynamic_index_in_dim(packed, lax.axis_index("seq"), 0, keepdims=False)
    shares = []
    start = 0
    for bias in biases:
        stop = start + bias.shape[0] // seq
        shares.append(packed[start:stop])
        start = stop

    def columns_of(total, count):
        return [total[start : start + count].astype(F32) for start in range(0, total.shape[0], count)]

    first_parts = columns_of(first_sum, per)
    return (
        block_out,
        grad_input,
        grad_modulation,
        jnp.concatenate(first_parts[:3], axis=1),
        shares[0],
        first_parts[3],
        shares[1],
        jnp.concatenate(columns_of(second_sum, per), axis=1),
        shares[2],
        third_sum.astype(F32),
        shares[3],
        jnp.concatenate(columns_of(fourth_sum, per), axis=1),
        shares[4],
        fifth_sum.astype(F32),
        shares[5],
        sixth_sum.astype(F32),
        shares[6],
    )


def solution(mesh):
    placed = (
        P("dp", "seq", None),
        P("dp", None, None),
        P("dp", "seq"),
        P("seq", None),
        P(),
        P("seq", None),
        P(),
        P("seq", None),
        P(),
        P("seq", None),
        P(),
        P("seq", None),
        P(),
        P("seq", None),
        P(),
        P("seq", None),
        P(),
        P("dp", "seq", None),
    )
    return jax.shard_map(
        local,
        mesh=mesh,
        in_specs=placed,
        out_specs=(
            P("dp", "seq", None),
            P("dp", "seq", None),
            P("dp", None, None),
        )
        + (P("seq", None), P("seq")) * 7,
        check_vma=False,
    )
```

```python
import functools
import math

import jax
import jax.numpy as jnp
from jax import lax
from jax.experimental import pallas as pl
from jax.experimental.pallas import tpu as pltpu
from jax.sharding import PartitionSpec as P

HEAD_DIM = 72
EPSILON = 1e-06
GELU_COEF = 0.044715
MASKED = -1e30
LOG2E = 1.4426950408889634
LANES = 128
BF = jnp.bfloat16
F32 = jnp.float32


def dot_nn(left, right):
    return jnp.dot(left, right, preferred_element_type=F32)


def dot_tn(left, right):
    return lax.dot_general(left, right, (((0,), (0,)), ((), ())), preferred_element_type=F32)


def dot_nt(left, right):
    return lax.dot_general(left, right, (((1,), (1,)), ((), ())), preferred_element_type=F32)


def silu_grad(value):
    sigmoid_val = jax.nn.sigmoid(value)
    return sigmoid_val * (1.0 + value * (1.0 - sigmoid_val))


def gelu_grad(value):
    factor = math.sqrt(2.0 / math.pi)
    tangent = jnp.tanh(factor * (value + GELU_COEF * value * value * value))
    return 0.5 * (1.0 + tangent) + 0.5 * value * (1.0 - tangent * tangent) * factor * (
        1.0 + 3.0 * GELU_COEF * value * value
    )


def norm_stats(values):
    centred = values - jnp.mean(values, axis=-1, keepdims=True)
    inv_std = lax.rsqrt(jnp.mean(centred * centred, axis=-1, keepdims=True) + EPSILON)
    return (centred * inv_std, inv_std)


def norm_back(grad_normed, normed, inv_std):
    return inv_std * (
        grad_normed
        - jnp.mean(grad_normed, axis=-1, keepdims=True)
        - normed * jnp.mean(grad_normed * normed, axis=-1, keepdims=True)
    )


def head_window(head, width):
    tile = jnp.minimum((head * HEAD_DIM) // LANES, width // LANES - 2)
    base = pl.multiple_of(tile * LANES, LANES)
    offset = head * HEAD_DIM - base
    lane = lax.broadcasted_iota(jnp.int32, (1, 2 * LANES), 1)
    mine = (lane >= offset) & (lane < offset + HEAD_DIM)
    spare = jnp.where(offset >= 4, 0, LANES)
    return base, mine, lane - spare, offset >= 4


def with_segments(block, mine, lane, seg, hit, miss):
    code = jnp.where(lane == seg, hit, miss)
    code = jnp.where((lane >= 0) & (lane < 4), code, 0.0)
    return jnp.where(mine, block.astype(F32), code).astype(BF)


def attend_forward_kernel(q_ref, k_ref, v_ref, segq_ref, segk_ref, out_ref, total_ref, *, block):
    head = pl.program_id(0)
    width = q_ref.shape[1]
    base, mine, lane, low = head_window(head, width)
    window = pl.ds(base, 2 * LANES)
    factor = HEAD_DIM ** (-0.5) * LOG2E
    keys = with_segments(k_ref[:, window], mine, lane, segk_ref[...], 0.0, 1.0)
    values = jnp.where(
        mine, v_ref[:, window].astype(F32), jnp.where(lane == 0, 1.0, 0.0)
    ).astype(BF)
    values_t = values.T
    for start in range(0, q_ref.shape[0], block):
        rows = pl.ds(start, block)
        query = with_segments(q_ref[rows, window], mine, lane, segq_ref[rows, :], MASKED, 0.0)
        scores = dot_nt(keys, query) * factor
        top = jnp.max(scores, axis=0, keepdims=True)
        weights = jnp.exp2(scores - top).astype(BF)
        gathered = dot_nn(values_t, weights)
        total = jnp.where(low, gathered[0:1], gathered[LANES : LANES + 1])
        result = (gathered * (1.0 / total)).T
        out_ref[rows, window] = jnp.where(
            mine, result, out_ref[rows, window].astype(F32)
        ).astype(BF)
        total_ref[pl.ds(head, 1), rows] = top + jnp.log2(total)


def whole(shape):
    return pl.BlockSpec(shape, lambda *_: (0,) * len(shape))


def attend_forward(parts, seg_query, seg_keys, heads):
    (query, qcol), (keys, kcol), (values, vcol) = parts
    count, tokens = seg_query.shape[0], seg_keys.shape[0]
    width = heads * HEAD_DIM
    return pl.pallas_call(
        functools.partial(attend_forward_kernel, block=min(256, count)),
        grid=(heads,),
        in_specs=[
            pl.BlockSpec((count, width), lambda h: (0, qcol)),
            pl.BlockSpec((tokens, width), lambda h: (0, kcol)),
            pl.BlockSpec((tokens, width), lambda h: (0, vcol)),
            whole((count, 1)),
            whole((tokens, 1)),
        ],
        out_specs=[whole((count, width)), whole((heads, count))],
        out_shape=[
            jax.ShapeDtypeStruct((count, width), BF),
            jax.ShapeDtypeStruct((heads, count), F32),
        ],
        compiler_params=pltpu.CompilerParams(vmem_limit_bytes=56 * 1024 * 1024),
        cost_estimate=pl.CostEstimate(
            flops=heads * count * tokens * 4 * 256,
            bytes_accessed=2 * width * (2 * count + 2 * tokens),
            transcendentals=heads * count * tokens,
        ),
        name="attend_forward",
    )(query, keys, values, seg_query, seg_keys)


def attend_backward_kernel(
    q_ref, k_ref, v_ref, segq_ref, segk_ref, total_ref, out_ref, grad_ref, *rest, block, columns
):
    grads, dots = rest[:-1], rest[-1]
    dq_ref, dk_ref, dv_ref = grads if len(grads) == 3 else grads * 3
    head = pl.program_id(0)
    width = q_ref.shape[1]
    count = q_ref.shape[0]
    factor = HEAD_DIM ** (-0.5) * LOG2E

    @pl.when(head == 0)
    def _():
        if len(grads) == 1:
            spare = pl.ds(3 * width, dq_ref.shape[1] - 3 * width)
            dq_ref[:, spare] = jnp.zeros((count, dq_ref.shape[1] - 3 * width), BF)
        row = lax.broadcasted_iota(jnp.int32, dots.shape[:1] + (width,), 0)
        col = lax.broadcasted_iota(jnp.int32, dots.shape[:1] + (width,), 1)
        pick = ((col >= row * HEAD_DIM) & (col < (row + 1) * HEAD_DIM)).astype(F32).astype(BF)
        for start in range(0, count, block):
            rows = pl.ds(start, block)
            product = out_ref[rows, :].astype(F32) * grad_ref[rows, :].astype(F32)
            high = product.astype(BF)
            rest_part = (product - high.astype(F32)).astype(BF)
            dots[:, rows] = dot_nt(pick, high) + dot_nt(pick, rest_part)

    base, mine, lane, _ = head_window(head, width)
    window = pl.ds(base, 2 * LANES)
    keys = with_segments(k_ref[:, window], mine, lane, segk_ref[...], 0.0, 1.0)
    keys_t = keys.T
    values = v_ref[:, window]
    grad_keys = None
    for start in range(0, count, block):
        rows = pl.ds(start, block)
        query = with_segments(q_ref[rows, window], mine, lane, segq_ref[rows, :], MASKED, 0.0)
        grad = jnp.where(mine, grad_ref[rows, window].astype(F32), 0.0).astype(BF)
        scores = dot_nt(keys, query) * factor
        probs = jnp.exp2(scores - total_ref[pl.ds(head, 1), rows])
        grad_probs = dot_nt(values, grad)
        grad_scores = (probs * (grad_probs - dots[pl.ds(head, 1), rows])).astype(BF)
        part_v = dot_nn(probs.astype(BF), grad)
        part_k = dot_nn(grad_scores, query)
        if grad_keys is None:
            grad_keys, grad_values = part_k, part_v
        else:
            grad_keys, grad_values = grad_keys + part_k, grad_values + part_v
        grad_query = (dot_nn(keys_t, grad_scores) * HEAD_DIM ** (-0.5)).T
        put(dq_ref, rows, base + columns[0], mine, grad_query)
    every = pl.ds(0, k_ref.shape[0])
    put(dk_ref, every, base + columns[1], mine, grad_keys * HEAD_DIM ** (-0.5))
    put(dv_ref, every, base + columns[2], mine, grad_values)


def put(ref, rows, base, mine, value):
    window = pl.ds(pl.multiple_of(base, LANES), 2 * LANES)
    ref[rows, window] = jnp.where(mine, value, ref[rows, window].astype(F32)).astype(BF)


def attend_backward(parts, seg_query, seg_keys, totals, out, grad, heads):
    (query, qcol), (keys, kcol), (values, vcol) = parts
    count, tokens = seg_query.shape[0], seg_keys.shape[0]
    width = heads * HEAD_DIM
    if count == tokens:
        shapes = [(count, -(-3 * width // (4 * LANES)) * 4 * LANES)]
        columns = (0, width, 2 * width)
    else:
        shapes = [(count, width), (tokens, width), (tokens, width)]
        columns = (0, 0, 0)
    return pl.pallas_call(
        functools.partial(attend_backward_kernel, block=min(256, count), columns=columns),
        grid=(heads,),
        in_specs=[
            pl.BlockSpec((count, width), lambda h: (0, qcol)),
            pl.BlockSpec((tokens, width), lambda h: (0, kcol)),
            pl.BlockSpec((tokens, width), lambda h: (0, vcol)),
            whole((count, 1)),
            whole((tokens, 1)),
            whole((heads, count)),
            whole((count, width)),
            whole((count, width)),
        ],
        out_specs=[whole(shape) for shape in shapes],
        out_shape=[jax.ShapeDtypeStruct(shape, BF) for shape in shapes],
        scratch_shapes=[pltpu.VMEM((heads, count), F32)],
        compiler_params=pltpu.CompilerParams(vmem_limit_bytes=60 * 1024 * 1024),
        cost_estimate=pl.CostEstimate(
            flops=heads * count * tokens * 10 * 256,
            bytes_accessed=2 * width * (4 * count + 4 * tokens),
            transcendentals=heads * count * tokens,
        ),
        name="attend_backward",
    )(query, keys, values, seg_query, seg_keys, totals, out, grad)


class Rows:
    def __init__(self, seq, rows):
        self.seq, self.rows = seq, rows
        self.share = seq // rows
        here = lax.axis_index("seq")
        self.row, self.part = here // self.share, here % self.share

    def device(self, row, part):
        return (row % self.rows) * self.share + part % self.share

    def shift_rows(self, shift):
        return [
            (self.device(r, p), self.device(r + shift, p))
            for r in range(self.rows)
            for p in range(self.share)
        ]

    def shift_parts(self, shift):
        return [
            (self.device(r, p), self.device(r, p + shift))
            for r in range(self.rows)
            for p in range(self.share)
        ]

    def to_rows(self, array):
        pieces = []
        for shift in range(self.rows):
            piece = lax.dynamic_index_in_dim(
                array, (self.row + shift) % self.rows, 0, keepdims=False
            )
            if shift:
                piece = lax.ppermute(piece, "seq", self.shift_rows(shift))
            pieces.append(piece)
        return pieces

    def to_spans(self, pieces):
        result = jnp.zeros((self.rows,) + pieces[0].shape, pieces[0].dtype)
        for shift, piece in enumerate(pieces):
            if shift:
                piece = lax.ppermute(piece, "seq", self.shift_rows(-shift))
            result = lax.dynamic_update_index_in_dim(
                result, piece, (self.row + shift) % self.rows, 0
            )
        return result

    def gather_parts(self, array):
        return jnp.concatenate(
            [array]
            + [
                lax.ppermute(array, "seq", self.shift_parts(shift))
                for shift in range(1, self.share)
            ],
            axis=0,
        )

    def sum_parts(self, array):
        count = array.shape[0] // self.share
        total = array[:count].astype(F32)
        for shift in range(1, self.share):
            piece = array[shift * count : (shift + 1) * count]
            total = total + lax.ppermute(piece, "seq", self.shift_parts(-shift)).astype(F32)
        return total.astype(array.dtype)

    def all_parts(self, array):
        total = array
        for shift in range(1, self.share):
            total = total + lax.ppermute(array, "seq", self.shift_parts(shift))
        return total


COPIES = ("plane", "core")
EVERY = ("seq", "plane", "core")


def own_slice(weights, cut):
    copies = lax.axis_size(COPIES)
    here = lax.axis_index(COPIES)
    blocks = [weight.shape[1] // cut for weight in weights]
    per = weights[0].shape[0]
    count = per * sum(blocks) // copies
    piece, row = here * count // per, here * count % per
    own = None
    first = 0
    for weight, number in zip(weights, blocks):
        column = jnp.clip(piece - first, 0, number - 1) * cut
        part = lax.dynamic_slice(weight, (row, column), (count, cut))
        own = part if own is None else jnp.where(piece >= first, part, own)
        first += number
    return own, (lax.axis_size("seq"), sum(blocks) * per, cut)


def gather_slices(slices, after=None):
    own, shape = slices
    if after is not None:
        own, _ = lax.optimization_barrier((own, after))
    return lax.all_gather(own, EVERY, axis=0, tiled=True).reshape(shape)


def reduce_bundle(bundle):
    seq, count, columns = bundle.shape
    planes = lax.axis_size("plane")
    core = lax.axis_index("core")
    parts = bundle.reshape(seq, planes, 2, count // planes // 2, columns)
    keep = lax.dynamic_index_in_dim(parts, core, 2, keepdims=False).swapaxes(0, 1)
    send = lax.dynamic_index_in_dim(parts, 1 - core, 2, keepdims=False).swapaxes(0, 1)
    got = lax.ppermute(send, "core", [(0, 1), (1, 0)])
    both = (keep.astype(F32) + got.astype(F32)).astype(BF)
    mine = lax.psum_scatter(both, "plane", scatter_dimension=0, tiled=True)[0]
    own = lax.psum_scatter(mine, "seq", scatter_dimension=0, tiled=True)[0]
    return lax.all_gather(own, COPIES, axis=0, tiled=True)


def split_rows(full, count):
    return [
        full[:, start : start + count].reshape(-1, full.shape[2])
        for start in range(0, full.shape[1], count)
    ]


MIB = 1024 * 1024


def spec(shape, index, once=False):
    if once:
        return pl.BlockSpec(shape, index, pipeline_mode=pl.Buffered(1))
    return pl.BlockSpec(shape, index)


def fixed(shape):
    return spec(shape, lambda *_: (0,) * len(shape), once=True)


def call(kernel, grid, inputs, outputs, args, name, flops, scratch=(), scalars=None):
    moved = sum(math.prod(arg.shape) * arg.dtype.itemsize for arg in args)
    moved += sum(math.prod(shape) * jnp.dtype(kind).itemsize for shape, kind, _ in outputs)
    grid_spec = pltpu.PrefetchScalarGridSpec(
        num_scalar_prefetch=0 if scalars is None else 1,
        grid=grid,
        in_specs=inputs,
        out_specs=[block for _, _, block in outputs],
        scratch_shapes=list(scratch),
    )
    given = args if scalars is None else [scalars] + list(args)
    return pl.pallas_call(
        kernel,
        grid_spec=grid_spec,
        out_shape=[jax.ShapeDtypeStruct(shape, kind) for shape, kind, _ in outputs],
        compiler_params=pltpu.CompilerParams(vmem_limit_bytes=60 * MIB),
        cost_estimate=pl.CostEstimate(flops=flops, bytes_accessed=moved, transcendentals=0),
        name=name,
    )(*given)


def square(block):
    return block.reshape(-1, block.shape[-1])


def chunks(count, size=256):
    return [pl.ds(start, min(size, count)) for start in range(0, count, min(size, count))]


def project_kernel(x_ref, hot_ref, shift_ref, scale_ref, w_ref, bias_ref, qkv_ref, modt_ref, low_ref):
    @pl.when(pl.program_id(0) == 0)
    def _():
        for rows in chunks(x_ref.shape[0]):
            normed, _ = norm_stats(x_ref[rows, :].astype(F32))
            hot = hot_ref[rows, :]
            low = normed * (1.0 + dot_nn(hot, scale_ref[...])) + dot_nn(hot, shift_ref[...])
            low_ref[rows, :] = low.astype(BF)
            modt_ref[:, rows] = low.astype(BF).T

    weight = square(w_ref[...])
    for rows in chunks(x_ref.shape[0]):
        qkv_ref[rows, :] = (dot_nn(low_ref[rows, :], weight) + bias_ref[...]).astype(BF)


def project(x, hot, mod, weights, bias):
    tokens, width = x.shape
    seq, _, per, _ = weights.shape
    part = lambda index: spec((mod.shape[0], width), lambda j: (0, index), once=True)
    return call(
        project_kernel,
        (3,),
        [
            fixed((tokens, width)),
            fixed(hot.shape),
            part(0),
            part(1),
            spec((seq, 1, per, width), lambda j: (0, j, 0, 0)),
            spec((1, width), lambda j: (0, j)),
        ],
        [
            ((tokens, 3 * width), BF, spec((tokens, width), lambda j: (0, j))),
            ((width, tokens), BF, fixed((width, tokens))),
        ],
        [x, hot, mod, mod, weights, bias],
        "project",
        6 * tokens * width * width,
        [pltpu.VMEM((tokens, width), BF)],
    )


def merge_kernel(
    out_ref, x_ref, hot_ref, gate_ref, shift_ref, scale_ref, w_ref, bias_ref,
    branch_ref, mid_ref, low_ref, lowt_ref, outt_ref,
):
    hot = hot_ref[...]
    branch = dot_nn(out_ref[...], square(w_ref[...])) + bias_ref[...]
    middle = x_ref[...].astype(F32) + dot_nn(hot, gate_ref[...]) * branch
    normed, _ = norm_stats(middle)
    low = normed * (1.0 + dot_nn(hot, scale_ref[...])) + dot_nn(hot, shift_ref[...])
    low = low.astype(BF)
    branch_ref[...] = branch.astype(BF)
    mid_ref[...] = middle
    low_ref[...] = low
    lowt_ref[...] = low.T
    outt_ref[...] = out_ref[...].T


def merge(attended, x, hot, mod, weights, bias):
    tokens, width = x.shape
    seq, _, per, _ = weights.shape
    size = min(256, tokens)
    part = lambda index: spec((mod.shape[0], width), lambda i: (0, index), once=True)
    rows = spec((size, width), lambda i: (i, 0))
    turned = spec((width, size), lambda i: (0, i))
    return call(
        merge_kernel,
        (tokens // size,),
        [
            rows,
            rows,
            spec((size, hot.shape[1]), lambda i: (i, 0)),
            part(2),
            part(3),
            part(4),
            spec((seq, 1, per, width), lambda i: (0, 3, 0, 0), once=True),
            fixed((1, width)),
        ],
        [
            ((tokens, width), BF, rows),
            ((tokens, width), F32, rows),
            ((tokens, width), BF, rows),
            ((width, tokens), BF, turned),
            ((width, tokens), BF, turned),
        ],
        [attended, x, hot, mod, mod, mod, weights, bias],
        "merge",
        2 * tokens * width * width,
    )


def gelu_pair(value):
    factor = math.sqrt(2.0 / math.pi)
    squared = value * value
    tangent = jnp.tanh(factor * value * (1.0 + GELU_COEF * squared))
    half = 0.5 * (1.0 + tangent)
    slope = half + (0.5 * factor) * value * (1.0 - tangent * tangent) * (
        1.0 + 3.0 * GELU_COEF * squared
    )
    return value * half, slope


def feed_kernel(
    low_ref, w_in_ref, b_in_ref, w_out_ref, b_out_ref, mid_ref, hot_ref, gate_ref,
    actt_ref, slope_ref, res_ref, rest_ref, branch_ref, total,
):
    step = pl.program_id(0)
    w_in, w_out = square(w_in_ref[...]), w_out_ref[...]
    for rows in chunks(low_ref.shape[0]):
        hmid = dot_nn(low_ref[rows, :], w_in) + b_in_ref[...]
        act, slope = gelu_pair(hmid)
        act = act.astype(BF)
        slope_ref[rows, :] = slope.astype(BF)
        actt_ref[:, rows] = act.T
        part = dot_nn(act, w_out)

        @pl.when(step == 0)
        def _():
            total[rows, :] = part

        @pl.when(step > 0)
        def _():
            total[rows, :] += part

    @pl.when(step == pl.num_programs(0) - 1)
    def _():
        for rows in chunks(low_ref.shape[0]):
            branch = total[rows, :] + b_out_ref[...]
            result = mid_ref[rows, :] + dot_nn(hot_ref[rows, :], gate_ref[...]) * branch
            result = result.astype(BF)
            res_ref[rows, :] = result
            rest_ref[:, rows] = result.T
            branch_ref[rows, :] = branch.astype(BF)


def feed(low, w_in, b_in, w_out, b_out, mid, hot, mod):
    tokens, width = low.shape
    seq, blocks, per, cut = w_in.shape
    hidden = blocks * cut
    return call(
        feed_kernel,
        (blocks,),
        [
            fixed((tokens, width)),
            spec((seq, 1, per, cut), lambda j: (0, j, 0, 0)),
            spec((1, cut), lambda j: (0, j)),
            spec((cut, width), lambda j: (j, 0)),
            fixed((1, width)),
            fixed((tokens, width)),
            fixed(hot.shape),
            spec((mod.shape[0], width), lambda j: (0, 5), once=True),
        ],
        [
            ((hidden, tokens), BF, spec((cut, tokens), lambda j: (j, 0))),
            ((tokens, hidden), BF, spec((tokens, cut), lambda j: (0, j))),
            ((tokens, width), BF, fixed((tokens, width))),
            ((width, tokens), BF, fixed((width, tokens))),
            ((tokens, width), BF, fixed((tokens, width))),
        ],
        [low, w_in, b_in, w_out, b_out, mid, hot, mod],
        "feed",
        4 * tokens * width * hidden,
        [pltpu.VMEM((tokens, width), F32)],
    )


def silu_pair(value):
    gate = jax.nn.sigmoid(value)
    return value * gate, gate * (1.0 + value * (1.0 - gate))


def align_kernel(
    res_ref, w_in_ref, b_in_ref, w_mid_ref, b_mid_ref, w_out_ref, b_out_ref, goal_ref,
    act1t_ref, act2t_ref, gfeat_ref, gh2_ref, gh1_ref, gout_ref, act1_ref, slope1_ref,
):
    blocks, cut = w_in_ref.shape[1], w_in_ref.shape[3]
    res = res_ref[...]
    for j in range(blocks):
        columns = pl.ds(j * cut, cut)
        hidden1 = dot_nn(res, square(w_in_ref[:, j])) + b_in_ref[:, columns]
        act, slope = silu_pair(hidden1)
        act1_ref[:, columns] = act.astype(BF)
        slope1_ref[:, columns] = slope
    act1 = act1_ref[...]
    act1t_ref[...] = act1.T
    hidden2 = dot_nn(act1, w_mid_ref[...]) + b_mid_ref[...]
    act2, slope2 = silu_pair(hidden2)
    act2 = act2.astype(BF)
    act2t_ref[...] = act2.T
    feats = dot_nn(act2, w_out_ref[...]) + b_out_ref[...]
    goals = goal_ref[...].astype(F32)
    inv_feat = lax.rsqrt(jnp.sum(feats * feats, axis=-1, keepdims=True) + EPSILON)
    feat_unit = feats * inv_feat
    goal_unit = goals * lax.rsqrt(jnp.sum(goals * goals, axis=-1, keepdims=True) + EPSILON)
    cosine = jnp.sum(feat_unit * goal_unit, axis=-1, keepdims=True)
    weight = -0.5 * feats.shape[1]
    gfeat = (weight * inv_feat * (goal_unit - cosine * feat_unit)).astype(BF)
    gfeat_ref[...] = gfeat
    gh2 = (dot_nt(gfeat, w_out_ref[...]) * slope2).astype(BF)
    gh2_ref[...] = gh2
    gh1 = (dot_nt(gh2, w_mid_ref[...]) * slope1_ref[...]).astype(BF)
    gh1_ref[...] = gh1
    total = None
    for j in range(blocks):
        part = dot_nt(gh1_ref[:, pl.ds(j * cut, cut)], square(w_in_ref[:, j]))
        total = part if total is None else total + part
    gout_ref[...] = total


def align(res, w_in, b_in, w_mid, b_mid, w_out, b_out, goals):
    tokens, width = res.shape
    inner, goal_width = w_out.shape
    size = min(256, tokens)
    rows = lambda n: spec((size, n), lambda i: (i, 0))
    turned = lambda n: spec((n, size), lambda i: (0, i))
    return call(
        align_kernel,
        (tokens // size,),
        [
            rows(width),
            fixed(w_in.shape),
            fixed((1, inner)),
            fixed(w_mid.shape),
            fixed((1, inner)),
            fixed(w_out.shape),
            fixed((1, goal_width)),
            rows(goal_width),
        ],
        [
            ((inner, tokens), BF, turned(inner)),
            ((inner, tokens), BF, turned(inner)),
            ((tokens, goal_width), BF, rows(goal_width)),
            ((tokens, inner), BF, rows(inner)),
            ((tokens, inner), BF, rows(inner)),
            ((tokens, width), F32, rows(width)),
        ],
        [res, w_in, b_in, w_mid, b_mid, w_out, b_out, goals],
        "align",
        4 * tokens * inner * (width + inner + goal_width),
        [pltpu.VMEM((size, inner), BF), pltpu.VMEM((size, inner), F32)],
    )


def feed_back_kernel(
    gout_ref, branch_ref, hot_ref, hott_ref, gate_ref, w_out_ref, slope_ref, w_in_ref,
    gmlp_ref, ghmid_ref, gmod_ref, ggate_ref,
):
    step = pl.program_id(0)

    @pl.when(step == 0)
    def _():
        sums = None
        for rows in chunks(gout_ref.shape[0]):
            gout = gout_ref[rows, :]
            gmlp_ref[rows, :] = (gout * dot_nn(hot_ref[rows, :], gate_ref[...])).astype(BF)
            part = dot_nn(hott_ref[:, rows], (gout * branch_ref[rows, :].astype(F32)).astype(BF))
            sums = part if sums is None else sums + part
        ggate_ref[...] = sums

    w_out, w_in = w_out_ref[...], square(w_in_ref[...])
    for rows in chunks(gout_ref.shape[0]):
        ghmid = (dot_nt(gmlp_ref[rows, :], w_out) * slope_ref[rows, :].astype(F32)).astype(BF)
        ghmid_ref[rows, :] = ghmid
        part = dot_nt(ghmid, w_in)

        @pl.when(step == 0)
        def _():
            gmod_ref[rows, :] = part

        @pl.when(step > 0)
        def _():
            gmod_ref[rows, :] += part


def feed_back(gout, branch, hot, hott, mod, w_out, slope, w_in):
    tokens, width = gout.shape
    seq, blocks, per, cut = w_in.shape
    hidden = blocks * cut
    return call(
        feed_back_kernel,
        (blocks,),
        [
            fixed((tokens, width)),
            fixed((tokens, width)),
            fixed(hot.shape),
            fixed(hott.shape),
            spec((mod.shape[0], width), lambda j: (0, 5), once=True),
            spec((cut, width), lambda j: (j, 0)),
            spec((tokens, cut), lambda j: (0, j)),
            spec((seq, 1, per, cut), lambda j: (0, j, 0, 0)),
        ],
        [
            ((tokens, width), BF, fixed((tokens, width))),
            ((tokens, hidden), BF, spec((tokens, cut), lambda j: (0, j))),
            ((tokens, width), F32, fixed((tokens, width))),
            ((hott.shape[0], width), F32, fixed((hott.shape[0], width))),
        ],
        [gout, branch, hot, hott, mod, w_out, slope, w_in],
        "feed_back",
        4 * tokens * width * hidden,
    )


def add_rows(ref, value):
    @pl.when(pl.program_id(0) == 0)
    def _():
        ref[...] = value

    @pl.when(pl.program_id(0) > 0)
    def _():
        ref[...] += value


def merge_back_kernel(
    gout_ref, gmod_ref, mid_ref, branch_ref, hot_ref, hott_ref, gate_ref, scale_ref, w_ref,
    gmid_ref, gbranch_ref, gatt_ref, gshift_ref, gscale_ref, ggate_ref,
):
    hot, hott = hot_ref[...], hott_ref[...]
    gmod = gmod_ref[...]
    normed, inv_std = norm_stats(mid_ref[...])
    gmid = gout_ref[...] + norm_back(
        gmod * (1.0 + dot_nn(hot, scale_ref[...])), normed, inv_std
    )
    gmid_ref[...] = gmid
    gbranch = (gmid * dot_nn(hot, gate_ref[...])).astype(BF)
    gbranch_ref[...] = gbranch
    gatt_ref[...] = dot_nt(gbranch, square(w_ref[...])).astype(BF)
    add_rows(gshift_ref, dot_nn(hott, gmod.astype(BF)))
    add_rows(gscale_ref, dot_nn(hott, (gmod * normed).astype(BF)))
    add_rows(ggate_ref, dot_nn(hott, (gmid * branch_ref[...].astype(F32)).astype(BF)))


def merge_back(gout, gmod, mid, branch, hot, hott, mod, weights):
    tokens, width = gout.shape
    seq, _, per, _ = weights.shape
    size = min(256, tokens)
    part = lambda index: spec((mod.shape[0], width), lambda i: (0, index), once=True)
    rows = spec((size, width), lambda i: (i, 0))
    sums = ((hott.shape[0], width), F32, fixed((hott.shape[0], width)))
    return call(
        merge_back_kernel,
        (tokens // size,),
        [
            rows,
            rows,
            rows,
            rows,
            spec((size, hot.shape[1]), lambda i: (i, 0)),
            spec((hott.shape[0], size), lambda i: (0, i)),
            part(2),
            part(4),
            spec((seq, 1, per, width), lambda i: (0, 3, 0, 0), once=True),
        ],
        [
            ((tokens, width), F32, rows),
            ((tokens, width), BF, rows),
            ((tokens, width), BF, rows),
            sums,
            sums,
            sums,
        ],
        [gout, gmod, mid, branch, hot, hott, mod, mod, weights],
        "merge_back",
        2 * tokens * width * width,
    )


def project_back_kernel(
    gqkv_ref, x_ref, gmid_ref, hot_ref, hott_ref, scale_ref, w_ref,
    gin_ref, gshift_ref, gscale_ref,
):
    width = x_ref.shape[1]
    hott = hott_ref[...]
    gmod = None
    for j in range(3):
        part = dot_nt(gqkv_ref[:, pl.ds(j * width, width)], square(w_ref[:, j]))
        gmod = part if gmod is None else gmod + part
    normed, inv_std = norm_stats(x_ref[...].astype(F32))
    gin = gmid_ref[...] + norm_back(
        gmod * (1.0 + dot_nn(hot_ref[...], scale_ref[...])), normed, inv_std
    )
    gin_ref[...] = gin.astype(BF)
    add_rows(gshift_ref, dot_nn(hott, gmod.astype(BF)))
    add_rows(gscale_ref, dot_nn(hott, (gmod * normed).astype(BF)))


def project_back(gqkv, x, gmid, hot, hott, mod, weights):
    tokens, width = x.shape
    seq, _, per, _ = weights.shape
    size = min(256, tokens)
    rows = spec((size, width), lambda i: (i, 0))
    sums = ((hott.shape[0], width), F32, fixed((hott.shape[0], width)))
    return call(
        project_back_kernel,
        (tokens // size,),
        [
            spec((size, 3 * width), lambda i: (i, 0)),
            rows,
            rows,
            spec((size, hot.shape[1]), lambda i: (i, 0)),
            spec((hott.shape[0], size), lambda i: (0, i)),
            spec((mod.shape[0], width), lambda i: (0, 1), once=True),
            spec((seq, 3, per, width), lambda i: (0, 0, 0, 0), once=True),
        ],
        [((tokens, width), BF, rows), sums, sums],
        [gqkv, x, gmid, hot, hott, mod, weights],
        "project_back",
        6 * tokens * width * width,
    )


def weight_kernel(where_ref, left_ref, right_ref, *refs, first):
    left = left_ref[...].reshape(-1, left_ref.shape[-1])
    got_ref = None if first else refs[0]
    out_ref = refs[0] if first else refs[1]
    result = dot_nn(left, right_ref[...]).reshape(out_ref.shape)
    if first:
        ones = jnp.ones((16, right_ref.shape[0]), BF)
        refs[1][...] = dot_nn(ones, right_ref[...])
    else:
        result = result + got_ref[...].astype(F32)
    out_ref[...] = result.astype(BF)


def weight_half(where, turned, right, seq, planes, by_columns, got=None):
    count, tokens = turned.shape
    columns = right.shape[1]
    first = got is None
    half = (lambda w: 1 - w[0]) if first else (lambda w: w[0])
    if by_columns:
        per, cut = count // seq // 2, columns // planes
        left = turned.reshape(seq, 2, per, tokens)
        left_spec = spec((seq, 1, per, tokens), lambda j, w: (0, half(w), 0, 0))
        right_spec = spec((tokens, cut), lambda j, w: (0, j))
        sum_spec = spec((16, cut), lambda j, w: (0, j))
    else:
        per, cut = count // seq // planes // 2, columns
        left = turned.reshape(seq, planes, 2, per, tokens)
        left_spec = spec((seq, 1, 1, per, tokens), lambda j, w: (0, j, half(w), 0, 0))
        right_spec = spec((tokens, cut), lambda j, w: (0, 0))
        sum_spec = spec((16, cut), lambda j, w: (0, 0))
    block = spec((1, seq, per, cut), lambda j, w: (j, 0, 0, 0))
    outputs = [((planes, seq, per, cut), BF, block)]
    inputs, args = [left_spec, right_spec], [left, right]
    if first:
        outputs.append(((16, columns), F32, sum_spec))
    else:
        inputs.append(block)
        args.append(got)
    return call(
        functools.partial(weight_kernel, first=first),
        (planes,),
        inputs,
        outputs,
        args,
        "weight_other" if first else "weight_own",
        count * tokens * columns,
        scalars=where,
    )


ANY = pl.BlockSpec(memory_space=pl.ANY)
SEQ, PLANES = 4, 4


class Link:
    def __init__(self):
        self.z, self.p, self.c = (lax.axis_index(name) for name in ("seq", "plane", "core"))

    def ahead(self, shift):
        return lax.rem(self.z + shift, SEQ)

    def behind(self, shift):
        return lax.rem(self.z + SEQ - shift, SEQ)

    def across(self, bit):
        low = lax.rem(self.p, 2)
        high = self.p // 2
        low = 1 - low if bit % 2 else low
        high = 1 - high if bit // 2 else high
        return high * 2 + low

    def copy(self, source, target, sems, axis, index):
        return pltpu.make_async_remote_copy(
            src_ref=source,
            dst_ref=target,
            send_sem=sems[0],
            recv_sem=sems[1],
            device_id={axis: index},
            device_id_type=pl.DeviceIdType.MESH,
        )

    def greet(self):
        barrier = pltpu.get_barrier_semaphore()
        for step in range(1, SEQ):
            signal = functools.partial(
                pl.semaphore_signal, barrier, inc=1, device_id_type=pl.DeviceIdType.MESH
            )
            signal(device_id={"seq": self.ahead(step)})
            signal(device_id={"plane": self.across(step)})
        pl.semaphore_signal(
            barrier, inc=1, device_id={"core": 1 - self.c}, device_id_type=pl.DeviceIdType.MESH
        )
        pl.semaphore_wait(barrier, 2 * SEQ - 1)


class Gather:
    def __init__(self, slices, shards, targets, sems):
        self.link = Link()
        self.slices, self.shards, self.targets = slices, shards, targets
        self.z_sems, self.p_sems, self.c_sems, self.local_sems = sems

    @staticmethod
    def scratch(count):
        dma = pltpu.SemaphoreType.DMA
        return [dma((2, count, 3)), dma((2, count, 3, 3)), dma((2, count, 3)), dma((count, 4))]

    def rows(self, target):
        half = target.shape[2] // 2
        return pl.ds(pl.multiple_of(self.link.c * half, half), half)

    def locals(self):
        for k, (shard, target) in enumerate(zip(self.shards, self.targets)):
            width = target.shape[3]
            block = 0
            for array in shard:
                for start in range(0, array.shape[1], width):
                    yield pltpu.make_async_copy(
                        array.at[:, pl.ds(start, width)],
                        target.at[self.link.z, block],
                        self.local_sems.at[k, block],
                    )
                    block += 1

    def along(self, k, shift, incoming):
        link, target = self.link, self.targets[k]
        place = link.behind(shift) if incoming else link.z
        return link.copy(
            self.slices[k],
            target.at[place, link.p, self.rows(target), :],
            (self.z_sems.at[0, k, shift - 1], self.z_sems.at[1, k, shift - 1]),
            "seq",
            link.ahead(shift),
        )

    def across(self, k, shift, bit, incoming):
        link, target = self.link, self.targets[k]
        plane = link.across(bit)
        place = (link.behind(shift), plane if incoming else link.p, self.rows(target))
        return link.copy(
            target.at[place],
            target.at[place],
            (self.p_sems.at[0, k, shift - 1, bit - 1], self.p_sems.at[1, k, shift - 1, bit - 1]),
            "plane",
            plane,
        )

    def beside(self, k, shift, incoming):
        link, target = self.link, self.targets[k]
        half = target.shape[2] // 2
        core = 1 - link.c if incoming else link.c
        rows = pl.ds(pl.multiple_of(core * half, half), half)
        place = target.at[link.behind(shift), :, rows, :]
        return link.copy(
            place,
            place,
            (self.c_sems.at[0, k, shift - 1], self.c_sems.at[1, k, shift - 1]),
            "core",
            1 - link.c,
        )

    def start(self):
        for k in range(len(self.targets)):
            for shift in (1, 3, 2):
                self.along(k, shift, False).start()

    def start_local(self):
        for copy in self.locals():
            copy.start()

    def spread(self, k, shift):
        self.along(k, shift, True).wait_recv()
        for bit in range(1, PLANES):
            self.across(k, shift, bit, False).start()

    def pair(self, k, shift):
        for bit in range(1, PLANES):
            self.across(k, shift, bit, True).wait_recv()
        self.beside(k, shift, False).start()

    def finish(self):
        for k in range(len(self.targets)):
            for shift in range(1, SEQ):
                self.beside(k, shift, True).wait_recv()
                self.along(k, shift, False).wait_send()
                self.beside(k, shift, False).wait_send()
                for bit in range(1, PLANES):
                    self.across(k, shift, bit, False).wait_send()
        for copy in self.locals():
            copy.wait()


class Rounds:
    def __init__(self, sources, targets, sems):
        self.link = Link()
        self.sources, self.targets, self.sems, self.local_sems = sources, targets, *sems

    @staticmethod
    def scratch(count):
        dma = pltpu.SemaphoreType.DMA
        return [dma((2, count, 3)), dma((count,))]

    def along(self, k, shift, incoming):
        link = self.link
        return link.copy(
            self.sources[k].at[link.ahead(shift)],
            self.targets[k].at[link.behind(shift) if incoming else link.z],
            (self.sems.at[0, k, shift - 1], self.sems.at[1, k, shift - 1]),
            "seq",
            link.ahead(shift),
        )

    def local(self, k):
        z = self.link.z
        return pltpu.make_async_copy(
            self.sources[k].at[z], self.targets[k].at[z], self.local_sems.at[k]
        )

    def start(self):
        for k in range(len(self.targets)):
            for shift in (2, 1, 3):
                self.along(k, shift, False).start()
            self.local(k).start()

    def finish(self):
        for k in range(len(self.targets)):
            for shift in range(1, SEQ):
                self.along(k, shift, True).wait_recv()
                self.along(k, shift, False).wait_send()
            self.local(k).wait()


class Finish:
    def __init__(self, sources, targets, refs):
        self.link = Link()
        self.sources, self.targets = sources, targets
        count = len(sources)
        self.bufs = refs[:count]
        self.z_sems, self.p_sems, self.c_sems, self.local_sems = refs[count:]

    @staticmethod
    def scratch(shapes):
        dma = pltpu.SemaphoreType.DMA
        count = len(shapes)
        bufs = [
            pltpu.VMEM((9 if shared else 5,) + tuple(shape), BF) for shape, shared in shapes
        ]
        return bufs + [dma((2, count, 3)), dma((2, count, 3)), dma((2, count, 4)), dma((count, 2))]

    def shared(self, k):
        return len(self.targets[k].shape) == 3

    def along(self, k, shift):
        link = self.link
        return link.copy(
            self.sources[k].at[link.ahead(shift)],
            self.bufs[k].at[shift - 1],
            (self.z_sems.at[0, k, shift - 1], self.z_sems.at[1, k, shift - 1]),
            "seq",
            link.ahead(shift),
        )

    def across(self, k, bit, incoming):
        link = self.link
        plane = link.across(bit)
        if self.shared(k):
            target = self.bufs[k].at[4 + bit]
        else:
            target = self.targets[k].at[plane if incoming else link.p, link.c]
        return link.copy(
            self.bufs[k].at[4],
            target,
            (self.p_sems.at[0, k, bit - 1], self.p_sems.at[1, k, bit - 1]),
            "plane",
            plane,
        )

    def beside(self, k, bit, incoming):
        link = self.link
        core = 1 - link.c if incoming else link.c
        if self.shared(k):
            source, target = self.bufs[k].at[8], self.targets[k].at[core]
        else:
            plane = link.across(bit)
            target = self.targets[k].at[plane, core]
            source = self.bufs[k].at[4] if bit == 0 else self.targets[k].at[plane, link.c]
        return link.copy(
            source,
            target,
            (self.c_sems.at[0, k, bit], self.c_sems.at[1, k, bit]),
            "core",
            1 - link.c,
        )

    def mine(self, k):
        return pltpu.make_async_copy(
            self.sources[k].at[self.link.z], self.bufs[k].at[3], self.local_sems.at[k, 0]
        )

    def own(self, k):
        link = self.link
        if self.shared(k):
            source, target = self.bufs[k].at[8], self.targets[k].at[link.c]
        else:
            source, target = self.bufs[k].at[4], self.targets[k].at[link.p, link.c]
        return pltpu.make_async_copy(source, target, self.local_sems.at[k, 1])

    def start(self):
        for k in range(len(self.sources)):
            for shift in (2, 1, 3):
                self.along(k, shift).start()
            self.mine(k).start()

    def add(self, k):
        for shift in range(1, SEQ):
            self.along(k, shift).wait_recv()
        self.mine(k).wait()
        buf = self.bufs[k]
        total = buf[0].astype(F32) + buf[1].astype(F32) + buf[2].astype(F32) + buf[3].astype(F32)
        buf[4] = total.astype(BF)
        for bit in range(1, PLANES):
            self.across(k, bit, False).start()
        if not self.shared(k):
            self.own(k).start()
            self.beside(k, 0, False).start()

    def pass_on(self, k):
        for bit in range(1, PLANES):
            self.across(k, bit, True).wait_recv()
            if not self.shared(k):
                self.beside(k, bit, False).start()
        if self.shared(k):
            buf = self.bufs[k]
            total = buf[4].astype(F32) + buf[5].astype(F32) + buf[6].astype(F32) + buf[7].astype(F32)
            buf[8] = total.astype(BF)
            self.own(k).start()
            self.beside(k, 0, False).start()

    def finish(self):
        for k in range(len(self.sources)):
            for bit in range(1 if self.shared(k) else PLANES):
                self.beside(k, bit, True).wait_recv()
                self.beside(k, bit, False).wait_send()
            for step in range(1, SEQ):
                self.along(k, step).wait_send()
                self.across(k, step, False).wait_send()
            self.own(k).wait()


def bring_kernel(*refs, bundles, rounds):
    refs = list(refs)
    take = lambda count: [refs.pop(0) for _ in range(count)]
    slices = take(len(bundles))
    shards = [take(count) for count in bundles]
    sources = take(rounds)
    targets = take(len(bundles))
    arrived = take(rounds)
    gather = Gather(slices, shards, targets, take(4))
    tokens = Rounds(sources, arrived, take(2))
    gather.link.greet()
    gather.start()
    tokens.start()
    gather.start_local()
    for k in range(len(bundles)):
        for shift in (1, 3, 2):
            gather.spread(k, shift)
        for shift in (1, 3, 2):
            gather.pair(k, shift)
    tokens.finish()
    gather.finish()


def bring(slices, shards, sources, collective):
    per = [shard[0].shape[0] for shard in shards]
    cut = [piece.shape[1] for piece in slices]
    blocks = [sum(a.shape[1] for a in shard) // n for shard, n in zip(shards, cut)]
    flat = [array for shard in shards for array in shard]
    shapes = [
        jax.ShapeDtypeStruct((SEQ, b, r, n), BF) for b, r, n in zip(blocks, per, cut)
    ] + [jax.ShapeDtypeStruct(array.shape, array.dtype) for array in sources]
    args = list(slices) + flat + list(sources)
    return pl.pallas_call(
        functools.partial(
            bring_kernel, bundles=[len(shard) for shard in shards], rounds=len(sources)
        ),
        in_specs=[ANY] * len(args),
        out_specs=[ANY] * len(shapes),
        out_shape=shapes,
        scratch_shapes=Gather.scratch(len(slices)) + Rounds.scratch(len(sources)),
        compiler_params=pltpu.CompilerParams(
            collective_id=collective, has_side_effects=True, vmem_limit_bytes=60 * MIB
        ),
        cost_estimate=pl.CostEstimate(flops=0, bytes_accessed=300_000_000, transcendentals=0),
        name="bring",
    )(*args)


def settle_kernel(*refs, count, rounds):
    refs = list(refs)
    take = lambda number: [refs.pop(0) for _ in range(number)]
    sums, sources = take(count), take(rounds)
    targets, arrived = take(count), take(rounds)
    work = Finish(sums, targets, take(count + 4))
    tokens = Rounds(sources, arrived, take(2)) if rounds else None
    work.link.greet()
    work.start()
    if rounds:
        tokens.start()
    for k in range(count):
        work.add(k)
    for k in range(count):
        work.pass_on(k)
    work.finish()
    if rounds:
        tokens.finish()


def settle(sums, shared, sources, collective):
    shapes = [
        jax.ShapeDtypeStruct(((2,) if one else (PLANES, 2)) + total.shape[1:], BF)
        for total, one in zip(sums, shared)
    ] + [jax.ShapeDtypeStruct(array.shape, array.dtype) for array in sources]
    args = list(sums) + list(sources)
    scratch = Finish.scratch([(total.shape[1:], one) for total, one in zip(sums, shared)])
    if sources:
        scratch = scratch + Rounds.scratch(len(sources))
    return pl.pallas_call(
        functools.partial(settle_kernel, count=len(sums), rounds=len(sources)),
        in_specs=[ANY] * len(args),
        out_specs=[ANY] * len(shapes),
        out_shape=shapes,
        scratch_shapes=scratch,
        compiler_params=pltpu.CompilerParams(
            collective_id=collective, has_side_effects=True, vmem_limit_bytes=60 * MIB
        ),
        cost_estimate=pl.CostEstimate(flops=0, bytes_accessed=200_000_000, transcendentals=0),
        name="settle",
    )(*args)


def local(
    block_input,
    modulation,
    segment_ids,
    qkv_weight,
    query_value_bias,
    attn_out_weight,
    attn_out_bias,
    mlp_in_weight,
    mlp_in_bias,
    mlp_out_weight,
    mlp_out_bias,
    proj_in_weight,
    proj_in_bias,
    proj_mid_weight,
    proj_mid_bias,
    proj_out_weight,
    proj_out_bias,
    targets,
):
    rows, span, width = block_input.shape
    segs = modulation.shape[1]
    seq = lax.axis_size("seq")
    place = Rows(seq, rows)
    heads = width // HEAD_DIM
    hidden = mlp_in_weight.shape[1]
    inner = proj_mid_weight.shape[1]
    goal_width = targets.shape[2]
    tokens = rows * span
    share = place.share

    x_in = jnp.concatenate(place.to_rows(block_input), axis=0)
    seg_pieces = place.to_rows(segment_ids)
    segs_own = jnp.concatenate(seg_pieces, axis=0)
    seg_query = segs_own[:, None]
    seg_keys = place.gather_parts(seg_query) if share > 1 else seg_query
    goals = jnp.concatenate(place.to_rows(targets), axis=0)
    mod_row = lax.dynamic_index_in_dim(modulation, place.row, 0, keepdims=False)

    per = qkv_weight.shape[0]
    half = inner // 2
    first = gather_slices(own_slice([qkv_weight, attn_out_weight], width))
    second = gather_slices(own_slice([mlp_in_weight], width), first)
    third = gather_slices(own_slice([mlp_out_weight], width), second)
    fourth = gather_slices(own_slice([proj_in_weight], half), third)
    fifth = gather_slices(own_slice([proj_mid_weight], inner), fourth)
    sixth = gather_slices(own_slice([proj_out_weight], goal_width), fifth)
    w_q, w_k, w_v, w_attn = split_rows(first, per)
    w_qkv = jnp.concatenate([w_q, w_k, w_v], axis=1)
    w_mlp_in = jnp.concatenate(split_rows(second, per), axis=1)
    w_mlp_out = third.reshape(hidden, width)
    w_proj_in = jnp.concatenate(split_rows(fourth, per), axis=1)
    w_proj_mid = fifth.reshape(inner, inner)
    w_proj_out = sixth.reshape(inner, goal_width)

    one_hot = (segs_own[:, None] == jnp.arange(segs, dtype=jnp.int32)[None, :]).astype(BF)
    inputs = x_in.astype(F32)
    mod_tok = dot_nn(one_hot, mod_row)
    shift1, scale1, gate1, shift2, scale2, gate2 = (
        mod_tok[:, part * width : (part + 1) * width] for part in range(6)
    )
    normed1, inv_std1 = norm_stats(inputs)
    modulated1 = (normed1 * (1.0 + scale1) + shift1).astype(BF)
    bias_float = query_value_bias.astype(F32)
    full_bias = jnp.concatenate(
        [bias_float[:width], jnp.zeros((width,), F32), bias_float[width:]]
    )
    qkv = (dot_nn(modulated1, w_qkv) + full_bias).astype(BF)
    if share > 1:
        kv_all = place.gather_parts(qkv[:, width:])
        parts = ((qkv, 0), (kv_all, 0), (kv_all, 1))
    else:
        parts = ((qkv, 0), (qkv, 1), (qkv, 2))
    attended, totals = attend_forward(parts, seg_query, seg_keys, heads)
    branch = dot_nn(attended, w_attn) + attn_out_bias.astype(F32)
    middle = inputs + gate1 * branch
    normed2, inv_std2 = norm_stats(middle)
    modulated2 = (normed2 * (1.0 + scale2) + shift2).astype(BF)
    hmid = dot_nn(modulated2, w_mlp_in) + mlp_in_bias.astype(F32)
    act_mid = jax.nn.gelu(hmid, approximate=True).astype(BF)
    mlp_branch = dot_nn(act_mid, w_mlp_out) + mlp_out_bias.astype(F32)
    out_low = (middle + gate2 * mlp_branch).astype(BF)
    hidden1 = dot_nn(out_low, w_proj_in) + proj_in_bias.astype(F32)
    act1 = jax.nn.silu(hidden1).astype(BF)
    hidden2 = dot_nn(act1, w_proj_mid) + proj_mid_bias.astype(F32)
    act2 = jax.nn.silu(hidden2).astype(BF)
    feats = dot_nn(act2, w_proj_out) + proj_out_bias.astype(F32)
    goals = goals.astype(F32)
    inv_feat = lax.rsqrt(jnp.sum(feats * feats, axis=-1, keepdims=True) + EPSILON)
    feat_unit = feats * inv_feat
    goal_unit = goals * lax.rsqrt(jnp.sum(goals * goals, axis=-1, keepdims=True) + EPSILON)
    cosine = jnp.sum(feat_unit * goal_unit, axis=-1, keepdims=True)
    loss_weight = 0.5 * goal_width
    grad_feats = (-loss_weight * inv_feat * (goal_unit - cosine * feat_unit)).astype(BF)

    def blocks(grad, cut):
        low = grad.astype(BF).reshape(seq, grad.shape[0] // seq, grad.shape[1])
        return [low[:, :, start : start + cut] for start in range(0, grad.shape[1], cut)]

    sixth_sum = reduce_bundle(
        jnp.concatenate(blocks(dot_tn(act2, grad_feats), goal_width), axis=1)
    )
    bias_out = jnp.sum(grad_feats.astype(F32), axis=0)
    grad_hidden2 = (dot_nt(grad_feats, w_proj_out) * silu_grad(hidden2)).astype(BF)
    fifth_sum = reduce_bundle(jnp.concatenate(blocks(dot_tn(act1, grad_hidden2), inner), axis=1))
    bias_mid = jnp.sum(grad_hidden2.astype(F32), axis=0)
    grad_hidden1 = (dot_nt(grad_hidden2, w_proj_mid) * silu_grad(hidden1)).astype(BF)
    fourth_sum = reduce_bundle(jnp.concatenate(blocks(dot_tn(out_low, grad_hidden1), half), axis=1))
    bias_in = jnp.sum(grad_hidden1.astype(F32), axis=0)
    grad_output = dot_nt(grad_hidden1, w_proj_in)
    grad_gate2 = grad_output * mlp_branch
    grad_mlp = (grad_output * gate2).astype(BF)
    third_sum = reduce_bundle(jnp.concatenate(blocks(dot_tn(act_mid, grad_mlp), width), axis=1))
    bias_ff_out = jnp.sum(grad_mlp.astype(F32), axis=0)
    grad_hmid = (dot_nt(grad_mlp, w_mlp_out) * gelu_grad(hmid)).astype(BF)
    second_sum = reduce_bundle(jnp.concatenate(blocks(dot_tn(modulated2, grad_hmid), width), axis=1))
    bias_ff_in = jnp.sum(grad_hmid.astype(F32), axis=0)
    grad_modulated2 = dot_nt(grad_hmid, w_mlp_in)
    grad_middle = grad_output + norm_back(grad_modulated2 * (1.0 + scale2), normed2, inv_std2)
    grad_gate1 = grad_middle * branch
    grad_branch = (grad_middle * gate1).astype(BF)
    grad_attn_w = dot_tn(attended, grad_branch)
    bias_attn = jnp.sum(grad_branch.astype(F32), axis=0)
    grad_attended = dot_nt(grad_branch, w_attn).astype(BF)
    grads = attend_backward(parts, seg_query, seg_keys, totals, attended, grad_attended, heads)
    if share > 1:
        grad_qkv = jnp.concatenate(
            [grads[0], place.sum_parts(grads[1]), place.sum_parts(grads[2])], axis=1
        )
    else:
        grad_qkv = grads[0][:, : 3 * width]
    first_sum = reduce_bundle(
        jnp.concatenate(
            blocks(dot_tn(modulated1, grad_qkv), width) + blocks(grad_attn_w, width), axis=1
        )
    )
    column_sums = jnp.sum(grad_qkv.astype(F32), axis=0)
    bias_qv = jnp.concatenate([column_sums[:width], column_sums[2 * width :]])
    grad_modulated1 = dot_nt(grad_qkv, w_qkv)
    grad_input = grad_middle + norm_back(grad_modulated1 * (1.0 + scale1), normed1, inv_std1)

    def by_segment(value):
        return dot_tn(one_hot, value.astype(BF))

    grad_mod = jnp.concatenate(
        [
            by_segment(grad_modulated1),
            by_segment(grad_modulated1 * normed1),
            by_segment(grad_gate1),
            by_segment(grad_modulated2),
            by_segment(grad_modulated2 * normed2),
            by_segment(grad_gate2),
        ],
        axis=-1,
    )
    grad_mod = place.all_parts(grad_mod)
    grad_modulation = lax.all_gather(grad_mod.astype(BF), "seq", axis=0)[:: share].astype(F32)

    def back(value):
        return place.to_spans(
            [value[shift * span : (shift + 1) * span] for shift in range(rows)]
        )

    block_out = back(out_low)
    grad_input = back(grad_input.astype(BF)).astype(F32)

    biases = [bias_qv, bias_attn, bias_ff_in, bias_ff_out, bias_in, bias_mid, bias_out]
    packed = jnp.concatenate([bias.reshape(seq, -1) for bias in biases], axis=1)
    packed = lax.psum(packed, EVERY)
    packed = lax.dynamic_index_in_dim(packed, lax.axis_index("seq"), 0, keepdims=False)
    shares = []
    start = 0
    for bias in biases:
        stop = start + bias.shape[0] // seq
        shares.append(packed[start:stop])
        start = stop

    def columns_of(total, count):
        return [total[start : start + count].astype(F32) for start in range(0, total.shape[0], count)]

    first_parts = columns_of(first_sum, per)
    return (
        block_out,
        grad_input,
        grad_modulation,
        jnp.concatenate(first_parts[:3], axis=1),
        shares[0],
        first_parts[3],
        shares[1],
        jnp.concatenate(columns_of(second_sum, per), axis=1),
        shares[2],
        third_sum.astype(F32),
        shares[3],
        jnp.concatenate(columns_of(fourth_sum, per), axis=1),
        shares[4],
        fifth_sum.astype(F32),
        shares[5],
        sixth_sum.astype(F32),
        shares[6],
    )


def tie(value, *others):
    return lax.optimization_barrier((value,) + others)[0]


def swap_cores(value):
    return lax.ppermute(value, "core", [(0, 1), (1, 0)])


def swap_planes(value, bit):
    return lax.ppermute(value, "plane", [(p, p ^ bit) for p in range(lax.axis_size("plane"))])


def scatter_planes(both, after=None):
    planes, seq, count, columns = both.shape
    flat = both.reshape(planes * seq * count, columns)
    if after is not None:
        flat = tie(flat, after)
    own = lax.psum_scatter(flat, "plane", scatter_dimension=0, tiled=True)
    return own.reshape(seq, count, columns)


def scatter_seq(both):
    seq, count, columns = both.shape
    return lax.psum_scatter(
        both.reshape(seq * count, columns), "seq", scatter_dimension=0, tiled=True
    )


def gather_copies(own):
    full = lax.all_gather(own, COPIES, axis=0, tiled=True)
    return full.reshape(lax.axis_size("plane"), 2, own.shape[0], own.shape[1])


def sum_vectors(packed):
    bit = 1
    total = packed + swap_cores(packed)
    while bit < lax.axis_size("plane"):
        total = total + swap_planes(total, bit)
        bit *= 2
    seq = lax.axis_size("seq")
    here = lax.axis_index("seq")
    own = lax.dynamic_index_in_dim(total, here, 0, keepdims=False)
    for shift in range(1, seq):
        piece = lax.dynamic_index_in_dim(total, (here + shift) % seq, 0, keepdims=False)
        own = own + lax.ppermute(piece, "seq", [(z, (z + shift) % seq) for z in range(seq)])
    return own


def exchange(array):
    seq = lax.axis_size("seq")
    here = lax.axis_index("seq")
    result = array
    for shift in range(1, seq):
        piece = lax.dynamic_index_in_dim(array, (here + shift) % seq, 0, keepdims=False)
        piece = lax.ppermute(piece, "seq", [(z, (z + shift) % seq) for z in range(seq)])
        result = lax.dynamic_update_index_in_dim(result, piece, (here + seq - shift) % seq, 0)
    return result


def unpack_kernel(full_ref, out_ref):
    out_ref[...] = full_ref[0, 0].astype(F32)


def unpack(full, columns=None):
    planes, _, count, cut = full.shape
    if columns is None:
        shape, place = (planes * 2 * count, cut), (lambda p, c: (2 * p + c, 0))
    else:
        shape, place = (2 * count, columns), (lambda p, c: (c, p))
    return call(
        unpack_kernel,
        (planes, 2),
        [spec((1, 1, count, cut), lambda p, c: (p, c, 0, 0))],
        [(shape, F32, spec((count, cut), place))],
        [full],
        "unpack",
        0,
    )[0]


def local_row(
    block_input, modulation, segment_ids,
    qkv_weight, query_value_bias,
    attn_out_weight, attn_out_bias,
    mlp_in_weight, mlp_in_bias,
    mlp_out_weight, mlp_out_bias,
    proj_in_weight, proj_in_bias,
    proj_mid_weight, proj_mid_bias,
    proj_out_weight, proj_out_bias,
    targets,
):
    rows, span, width = block_input.shape
    seq, planes = lax.axis_size("seq"), lax.axis_size("plane")
    heads = width // HEAD_DIM
    hidden = mlp_in_weight.shape[1]
    inner = proj_mid_weight.shape[1]
    goal_width = targets.shape[2]
    tokens = rows * span
    where = lax.axis_index("core").reshape(1).astype(jnp.int32)

    slice1, _ = own_slice([qkv_weight, attn_out_weight], width)
    slice2, _ = own_slice([mlp_in_weight], width)
    third = gather_slices(own_slice([mlp_out_weight], width))
    w1, w2, x, seg_own = bring(
        [slice1, slice2],
        [[qkv_weight, attn_out_weight], [mlp_in_weight]],
        [block_input, segment_ids.reshape(rows, -1, LANES)],
        0,
    )
    x = x.reshape(tokens, width)
    seg_own = seg_own.reshape(tokens)
    goals = exchange(tie(targets, x)).reshape(tokens, goal_width)
    mod_row = lax.dynamic_index_in_dim(modulation, lax.axis_index("seq"), 0, keepdims=False)
    mod = jnp.pad(mod_row, ((0, 16 - mod_row.shape[0]), (0, 0)))
    hot = (seg_own[:, None] == jnp.arange(16, dtype=jnp.int32)[None, :]).astype(BF)
    hott = (seg_own[None, :] == jnp.arange(16, dtype=jnp.int32)[:, None]).astype(BF)
    seg_column = seg_own[:, None]
    vector = lambda bias: bias.astype(F32)[None, :]

    per = qkv_weight.shape[0]
    bias_float = query_value_bias.astype(F32)
    full_bias = jnp.concatenate(
        [bias_float[:width], jnp.zeros((width,), F32), bias_float[width:]]
    )
    qkv, mod1t = project(x, hot, mod, w1, full_bias[None, :])
    fourth = gather_slices(own_slice([tie(proj_in_weight, x)], inner // planes))
    fifth = gather_slices(own_slice([tie(proj_mid_weight, x)], inner))
    sixth = gather_slices(own_slice([tie(proj_out_weight, x)], goal_width))
    parts = ((qkv, 0), (qkv, 1), (qkv, 2))
    attended, totals = attend_forward(parts, seg_column, seg_column, heads)
    branch, mid, low2, mod2t, attt = merge(attended, x, hot, mod, w1, vector(attn_out_bias))
    w3 = third.reshape(hidden, width)
    actt, slope, out_low, outt, mlp_branch = feed(
        low2, w2, vector(mlp_in_bias), w3, vector(mlp_out_bias), mid, hot, mod
    )
    w4 = fourth.reshape(seq, planes, per, inner // planes)
    w5, w6 = fifth.reshape(inner, inner), sixth.reshape(inner, goal_width)
    act1t, act2t, gfeat, gh2, gh1, gout = align(
        out_low, w4, vector(proj_in_bias), w5, vector(proj_mid_bias), w6, vector(proj_out_bias), goals
    )
    block_out = exchange(tie(out_low, gout).reshape(block_input.shape))

    half = functools.partial(weight_half, where, seq=seq, planes=planes)
    other6, sum6 = half(act2t, tie(gfeat, gout), by_columns=False)
    got6 = swap_cores(other6)
    other5, sum5 = half(act1t, tie(gh2, other6), by_columns=True)
    got5 = swap_cores(other5)
    other4, sum4 = half(outt, tie(gh1, other5), by_columns=True)
    got4 = swap_cores(other4)
    (own6,) = half(act2t, tie(gfeat, other4), by_columns=False, got=got6)
    (own5,) = half(act1t, tie(gh2, own6), by_columns=True, got=got5)
    (own4,) = half(outt, tie(gh1, own5), by_columns=True, got=got4)
    plane6 = scatter_planes(own6)
    plane5 = scatter_planes(own5)
    plane4 = scatter_planes(own4)
    gmlp, ghmid, gmod2, ggate2 = feed_back(
        tie(gout, own4), mlp_branch, hot, hott, mod, w3, slope, w2
    )
    other3, sum3 = half(actt, tie(gmlp, gmod2), by_columns=False)
    got3 = swap_cores(other3)
    other2, sum2 = half(mod2t, tie(ghmid, other3), by_columns=True)
    got2 = swap_cores(other2)
    (own3,) = half(actt, tie(gmlp, other2), by_columns=False, got=got3)
    plane3 = scatter_planes(own3)
    (own2,) = half(mod2t, tie(ghmid, own3), by_columns=True, got=got2)
    plane2 = scatter_planes(own2)
    gmid, gbranch, gatt, gshift2, gscale2, ggate1 = merge_back(
        gout, tie(gmod2, own2), mid, branch, hot, hott, mod, w1
    )
    half1 = functools.partial(weight_half, where, seq=seq, planes=1)
    other0, sum0 = half1(attt, tie(gbranch, gatt), by_columns=True)
    got0 = swap_cores(other0)
    (gqkv,) = attend_backward(parts, seg_column, seg_column, totals, attended, tie(gatt, other0), heads)
    (own0,) = half1(attt, tie(gbranch, gqkv), by_columns=True, got=got0)
    other1, sum1 = half(mod1t, tie(gqkv, own0), by_columns=True)
    got1 = swap_cores(other1)
    gin, gshift1, gscale1 = project_back(
        tie(gqkv, other1), x, gmid, hot, hott, mod, w1
    )
    (own1,) = half(mod1t, tie(gqkv, gin), by_columns=True, got=got1)
    plane1 = scatter_planes(own1)
    grad_input = exchange(gin.reshape(block_input.shape)).astype(F32)

    segs = modulation.shape[1]
    grad_mod = jnp.concatenate(
        [gshift1, gscale1, ggate1, gshift2, gscale2, ggate2], axis=1
    )[:segs].astype(BF)
    grad_mod = jnp.pad(grad_mod.reshape(-1, LANES), ((0, 8), (0, 0)))
    grad_mod = jnp.broadcast_to(grad_mod[None], (rows,) + grad_mod.shape)
    full6, full5, full4, full3, full2, full0 = settle(
        [plane6, plane5, plane4, plane3, plane2, tie(own0[0], own1)],
        [False] * 5 + [True],
        [],
        1,
    )
    full1, all_mod = settle([plane1], [False], [tie(grad_mod, full0)], 2)
    grad_modulation = all_mod[:, :-8].reshape(rows, segs, 6 * width).astype(F32)

    columns1 = sum1[0]
    biases = [
        jnp.concatenate([columns1[:width], columns1[2 * width : 3 * width]]),
        sum0[0], sum2[0], sum3[0], sum4[0], sum5[0], sum6[0],
    ]
    packed = sum_vectors(jnp.concatenate([bias.reshape(seq, -1) for bias in biases], axis=1))
    shares = []
    start = 0
    for bias in biases:
        stop = start + bias.shape[0] // seq
        shares.append(packed[start:stop])
        start = stop

    return (
        block_out,
        grad_input,
        grad_modulation,
        unpack(full1, 3 * width),
        shares[0],
        full0.reshape(per, width).astype(F32),
        shares[1],
        unpack(full2, hidden),
        shares[2],
        unpack(full3),
        shares[3],
        unpack(full4, inner),
        shares[4],
        unpack(full5, inner),
        shares[5],
        unpack(full6),
        shares[6],
    )


def solution(mesh):
    copies, seq = mesh.shape["dp"], mesh.shape["seq"]
    grid = jax.sharding.Mesh(
        mesh.devices.reshape(copies // 2, 2, seq), ("plane", "core", "seq")
    )
    rows, weight = P(COPIES, "seq", None), P("seq", None)
    placed = (rows, P(COPIES, None, None), P(COPIES, "seq")) + (weight, P()) * 7 + (rows,)

    def step(*args):
        per_device = args[0].shape[0] // copies
        one_row = per_device == seq and copies // 2 == seq and args[0].shape[1] == 1024
        return jax.shard_map(
            local_row if one_row else local,
            mesh=grid,
            in_specs=placed,
            out_specs=(rows, rows, P(COPIES, None, None)) + (weight, P("seq")) * 7,
            check_vma=False,
        )(*args)

    return step
```

```python
import functools
import math

import jax
import jax.numpy as jnp
from jax import lax
from jax.experimental import pallas as pl
from jax.experimental.pallas import tpu as pltpu
from jax.sharding import PartitionSpec as P

HEAD_DIM = 72
EPSILON = 1e-06
GELU_COEF = 0.044715
MASKED = -1e30
LOG2E = 1.4426950408889634
LANES = 128
BF = jnp.bfloat16
F32 = jnp.float32


def dot_nn(left, right):
    return jnp.dot(left, right, preferred_element_type=F32)


def dot_tn(left, right):
    return lax.dot_general(left, right, (((0,), (0,)), ((), ())), preferred_element_type=F32)


def dot_nt(left, right):
    return lax.dot_general(left, right, (((1,), (1,)), ((), ())), preferred_element_type=F32)


def silu_grad(value):
    sigmoid_val = jax.nn.sigmoid(value)
    return sigmoid_val * (1.0 + value * (1.0 - sigmoid_val))


def gelu_grad(value):
    factor = math.sqrt(2.0 / math.pi)
    tangent = jnp.tanh(factor * (value + GELU_COEF * value * value * value))
    return 0.5 * (1.0 + tangent) + 0.5 * value * (1.0 - tangent * tangent) * factor * (
        1.0 + 3.0 * GELU_COEF * value * value
    )


def norm_stats(values):
    centred = values - jnp.mean(values, axis=-1, keepdims=True)
    inv_std = lax.rsqrt(jnp.mean(centred * centred, axis=-1, keepdims=True) + EPSILON)
    return (centred * inv_std, inv_std)


def norm_back(grad_normed, normed, inv_std):
    return inv_std * (
        grad_normed
        - jnp.mean(grad_normed, axis=-1, keepdims=True)
        - normed * jnp.mean(grad_normed * normed, axis=-1, keepdims=True)
    )


GATHER_AT = (1, 1, 2, 3, 3, 4, 5, 6, 7, 8, 9, 10, 11, 12, 13, 14, 15, 15, 15)
FEED_AT = (1, 1, 1, 1, 2, 2, 2, 3, 3, 3, 4, 4, 4, 5, 5, 5, 6, 6, 6, 7, 7, 7, 7, 7, 7, 7, 7, 7)
SETTLE_AT = (4, 7, 12, 15)


def head_window(head, width):
    tile = jnp.minimum((head * HEAD_DIM) // LANES, width // LANES - 2)
    base = pl.multiple_of(tile * LANES, LANES)
    offset = head * HEAD_DIM - base
    lane = lax.broadcasted_iota(jnp.int32, (1, 2 * LANES), 1)
    mine = (lane >= offset) & (lane < offset + HEAD_DIM)
    spare = jnp.where(offset >= 4, 0, LANES)
    return base, mine, lane - spare, offset >= 4


def with_segments(block, mine, lane, seg, hit, miss):
    code = jnp.where(lane == seg, hit, miss)
    code = jnp.where((lane >= 0) & (lane < 4), code, 0.0)
    return jnp.where(mine, block.astype(F32), code).astype(BF)


def attend_head(head, refs, seg_refs, out_ref, total_ref, block):
    (q_ref, qcol), (k_ref, kcol), (v_ref, vcol) = refs
    segq_ref, segk_ref = seg_refs
    base, mine, lane, low = head_window(head, out_ref.shape[1])
    window = lambda column: pl.ds(pl.multiple_of(base + column, LANES), 2 * LANES)
    factor = HEAD_DIM ** (-0.5) * LOG2E
    keys = with_segments(k_ref[:, window(kcol)], mine, lane, segk_ref[...], 0.0, 1.0)
    values = jnp.where(
        mine, v_ref[:, window(vcol)].astype(F32), jnp.where(lane == 0, 1.0, 0.0)
    ).astype(BF)
    values_t = values.T
    for start in range(0, out_ref.shape[0], block):
        rows = pl.ds(start, block)
        query = with_segments(
            q_ref[rows, window(qcol)], mine, lane, segq_ref[rows, :], MASKED, 0.0
        )
        scores = dot_nt(keys, query) * factor
        top = jnp.max(scores, axis=0, keepdims=True)
        weights = jnp.exp2(scores - top).astype(BF)
        gathered = dot_nn(values_t, weights)
        total = jnp.where(low, gathered[0:1], gathered[LANES : LANES + 1])
        result = (gathered * (1.0 / total)).T
        out_ref[rows, window(0)] = jnp.where(
            mine, result, out_ref[rows, window(0)].astype(F32)
        ).astype(BF)
        total_ref[pl.ds(head, 1), rows] = top + jnp.log2(total)


def attend_forward_kernel(q_ref, k_ref, v_ref, segq_ref, segk_ref, out_ref, total_ref, *, block):
    parts = ((q_ref, 0), (k_ref, 0), (v_ref, 0))
    attend_head(pl.program_id(0), parts, (segq_ref, segk_ref), out_ref, total_ref, block)


def whole(shape):
    return pl.BlockSpec(shape, lambda *_: (0,) * len(shape))


def attend_forward(parts, seg_query, seg_keys, heads):
    (query, qcol), (keys, kcol), (values, vcol) = parts
    count, tokens = seg_query.shape[0], seg_keys.shape[0]
    width = heads * HEAD_DIM
    return pl.pallas_call(
        functools.partial(attend_forward_kernel, block=min(256, count)),
        grid=(heads,),
        in_specs=[
            pl.BlockSpec((count, width), lambda h: (0, qcol)),
            pl.BlockSpec((tokens, width), lambda h: (0, kcol)),
            pl.BlockSpec((tokens, width), lambda h: (0, vcol)),
            whole((count, 1)),
            whole((tokens, 1)),
        ],
        out_specs=[whole((count, width)), whole((heads, count))],
        out_shape=[
            jax.ShapeDtypeStruct((count, width), BF),
            jax.ShapeDtypeStruct((heads, count), F32),
        ],
        compiler_params=pltpu.CompilerParams(vmem_limit_bytes=56 * 1024 * 1024),
        cost_estimate=pl.CostEstimate(
            flops=heads * count * tokens * 4 * 256,
            bytes_accessed=2 * width * (2 * count + 2 * tokens),
            transcendentals=heads * count * tokens,
        ),
        name="attend_forward",
    )(query, keys, values, seg_query, seg_keys)


def attend_backward_kernel(
    q_ref, k_ref, v_ref, segq_ref, segk_ref, total_ref, out_ref, grad_ref, *rest, block, columns,
    carried=0
):
    work = None
    if carried:
        rest = list(rest)
        take = lambda number: [rest.pop(0) for _ in range(number)]
        sums = take(carried)
        grads = take(1)
        targets = take(carried)
        dots = rest.pop(0)
        work = Sum(sums, targets, rest)
        head = pl.program_id(0)

        @pl.when(head == 0)
        def _():
            work.link.greet()
            work.start()

        for k in range(carried):
            pl.when(head == SETTLE_AT[k])(functools.partial(work.add, k))
    else:
        grads, dots = rest[:-1], rest[-1]
    dq_ref, dk_ref, dv_ref = grads if len(grads) == 3 else grads * 3
    head = pl.program_id(0)
    width = q_ref.shape[1]
    count = q_ref.shape[0]
    factor = HEAD_DIM ** (-0.5) * LOG2E

    @pl.when(head == 0)
    def _():
        if len(grads) == 1:
            spare = pl.ds(3 * width, dq_ref.shape[1] - 3 * width)
            dq_ref[:, spare] = jnp.zeros((count, dq_ref.shape[1] - 3 * width), BF)
        row = lax.broadcasted_iota(jnp.int32, dots.shape[:1] + (width,), 0)
        col = lax.broadcasted_iota(jnp.int32, dots.shape[:1] + (width,), 1)
        pick = ((col >= row * HEAD_DIM) & (col < (row + 1) * HEAD_DIM)).astype(F32).astype(BF)
        for start in range(0, count, block):
            rows = pl.ds(start, block)
            product = out_ref[rows, :].astype(F32) * grad_ref[rows, :].astype(F32)
            high = product.astype(BF)
            rest_part = (product - high.astype(F32)).astype(BF)
            dots[:, rows] = dot_nt(pick, high) + dot_nt(pick, rest_part)

    base, mine, lane, _ = head_window(head, width)
    window = pl.ds(base, 2 * LANES)
    keys = with_segments(k_ref[:, window], mine, lane, segk_ref[...], 0.0, 1.0)
    keys_t = keys.T
    values = v_ref[:, window]
    grad_keys = None
    for start in range(0, count, block):
        rows = pl.ds(start, block)
        query = with_segments(q_ref[rows, window], mine, lane, segq_ref[rows, :], MASKED, 0.0)
        grad = jnp.where(mine, grad_ref[rows, window].astype(F32), 0.0).astype(BF)
        scores = dot_nt(keys, query) * factor
        probs = jnp.exp2(scores - total_ref[pl.ds(head, 1), rows])
        grad_probs = dot_nt(values, grad)
        grad_scores = (probs * (grad_probs - dots[pl.ds(head, 1), rows])).astype(BF)
        part_v = dot_nn(probs.astype(BF), grad)
        part_k = dot_nn(grad_scores, query)
        if grad_keys is None:
            grad_keys, grad_values = part_k, part_v
        else:
            grad_keys, grad_values = grad_keys + part_k, grad_values + part_v
        grad_query = (dot_nn(keys_t, grad_scores) * HEAD_DIM ** (-0.5)).T
        put(dq_ref, rows, base + columns[0], mine, grad_query)
    every = pl.ds(0, k_ref.shape[0])
    put(dk_ref, every, base + columns[1], mine, grad_keys * HEAD_DIM ** (-0.5))
    put(dv_ref, every, base + columns[2], mine, grad_values)
    if work is not None:
        pl.when(head == pl.num_programs(0) - 1)(work.finish)


def put(ref, rows, base, mine, value):
    window = pl.ds(pl.multiple_of(base, LANES), 2 * LANES)
    ref[rows, window] = jnp.where(mine, value, ref[rows, window].astype(F32)).astype(BF)


def attend_backward(
    parts, seg_query, seg_keys, totals, out, grad, heads, sums=(), collective=None
):
    (query, qcol), (keys, kcol), (values, vcol) = parts
    count, tokens = seg_query.shape[0], seg_keys.shape[0]
    width = heads * HEAD_DIM
    if count == tokens:
        shapes = [(count, -(-3 * width // (4 * LANES)) * 4 * LANES)]
        columns = (0, width, 2 * width)
    else:
        shapes = [(count, width), (tokens, width), (tokens, width)]
        columns = (0, 0, 0)
    return pl.pallas_call(
        functools.partial(
            attend_backward_kernel, block=min(256, count), columns=columns, carried=len(sums)
        ),
        grid=(heads,),
        in_specs=[
            pl.BlockSpec((count, width), lambda h: (0, qcol)),
            pl.BlockSpec((tokens, width), lambda h: (0, kcol)),
            pl.BlockSpec((tokens, width), lambda h: (0, vcol)),
            whole((count, 1)),
            whole((tokens, 1)),
            whole((heads, count)),
            whole((count, width)),
            whole((count, width)),
        ]
        + [ANY] * len(sums),
        out_specs=[whole(shape) for shape in shapes] + [ANY] * len(sums),
        out_shape=[jax.ShapeDtypeStruct(shape, BF) for shape in shapes]
        + [summed(total) for total in sums],
        scratch_shapes=[pltpu.VMEM((heads, count), F32)]
        + (Sum.scratch(sums) if sums else []),
        compiler_params=pltpu.CompilerParams(
            vmem_limit_bytes=60 * 1024 * 1024,
            collective_id=collective,
            has_side_effects=bool(sums),
        ),
        cost_estimate=pl.CostEstimate(
            flops=heads * count * tokens * 10 * 256,
            bytes_accessed=2 * width * (4 * count + 4 * tokens),
            transcendentals=heads * count * tokens,
        ),
        name="attend_backward",
    )(query, keys, values, seg_query, seg_keys, totals, out, grad, *sums)


class Rows:
    def __init__(self, seq, rows):
        self.seq, self.rows = seq, rows
        self.share = seq // rows
        here = lax.axis_index("seq")
        self.row, self.part = here // self.share, here % self.share

    def device(self, row, part):
        return (row % self.rows) * self.share + part % self.share

    def shift_rows(self, shift):
        return [
            (self.device(r, p), self.device(r + shift, p))
            for r in range(self.rows)
            for p in range(self.share)
        ]

    def shift_parts(self, shift):
        return [
            (self.device(r, p), self.device(r, p + shift))
            for r in range(self.rows)
            for p in range(self.share)
        ]

    def to_rows(self, array):
        pieces = []
        for shift in range(self.rows):
            piece = lax.dynamic_index_in_dim(
                array, (self.row + shift) % self.rows, 0, keepdims=False
            )
            if shift:
                piece = lax.ppermute(piece, "seq", self.shift_rows(shift))
            pieces.append(piece)
        return pieces

    def to_spans(self, pieces):
        result = jnp.zeros((self.rows,) + pieces[0].shape, pieces[0].dtype)
        for shift, piece in enumerate(pieces):
            if shift:
                piece = lax.ppermute(piece, "seq", self.shift_rows(-shift))
            result = lax.dynamic_update_index_in_dim(
                result, piece, (self.row + shift) % self.rows, 0
            )
        return result

    def gather_parts(self, array):
        return jnp.concatenate(
            [array]
            + [
                lax.ppermute(array, "seq", self.shift_parts(shift))
                for shift in range(1, self.share)
            ],
            axis=0,
        )

    def sum_parts(self, array):
        count = array.shape[0] // self.share
        total = array[:count].astype(F32)
        for shift in range(1, self.share):
            piece = array[shift * count : (shift + 1) * count]
            total = total + lax.ppermute(piece, "seq", self.shift_parts(-shift)).astype(F32)
        return total.astype(array.dtype)

    def all_parts(self, array):
        total = array
        for shift in range(1, self.share):
            total = total + lax.ppermute(array, "seq", self.shift_parts(shift))
        return total


COPIES = ("plane", "core")
EVERY = ("seq", "plane", "core")


def own_slice(weights, cut):
    copies = lax.axis_size(COPIES)
    here = lax.axis_index(COPIES)
    blocks = [weight.shape[1] // cut for weight in weights]
    per = weights[0].shape[0]
    count = per * sum(blocks) // copies
    piece, row = here * count // per, here * count % per
    own = None
    first = 0
    for weight, number in zip(weights, blocks):
        column = jnp.clip(piece - first, 0, number - 1) * cut
        part = lax.dynamic_slice(weight, (row, column), (count, cut))
        own = part if own is None else jnp.where(piece >= first, part, own)
        first += number
    return own, (lax.axis_size("seq"), sum(blocks) * per, cut)


def gather_slices(slices, after=None):
    own, shape = slices
    if after is not None:
        own, _ = lax.optimization_barrier((own, after))
    return lax.all_gather(own, EVERY, axis=0, tiled=True).reshape(shape)


def reduce_bundle(bundle):
    seq, count, columns = bundle.shape
    planes = lax.axis_size("plane")
    core = lax.axis_index("core")
    parts = bundle.reshape(seq, planes, 2, count // planes // 2, columns)
    keep = lax.dynamic_index_in_dim(parts, core, 2, keepdims=False).swapaxes(0, 1)
    send = lax.dynamic_index_in_dim(parts, 1 - core, 2, keepdims=False).swapaxes(0, 1)
    got = lax.ppermute(send, "core", [(0, 1), (1, 0)])
    both = (keep.astype(F32) + got.astype(F32)).astype(BF)
    mine = lax.psum_scatter(both, "plane", scatter_dimension=0, tiled=True)[0]
    own = lax.psum_scatter(mine, "seq", scatter_dimension=0, tiled=True)[0]
    return lax.all_gather(own, COPIES, axis=0, tiled=True)


def split_rows(full, count):
    return [
        full[:, start : start + count].reshape(-1, full.shape[2])
        for start in range(0, full.shape[1], count)
    ]


MIB = 1024 * 1024


def spec(shape, index, once=False):
    if once:
        return pl.BlockSpec(shape, index, pipeline_mode=pl.Buffered(1))
    return pl.BlockSpec(shape, index)


def fixed(shape):
    return spec(shape, lambda *_: (0,) * len(shape), once=True)


def call(
    kernel, grid, inputs, outputs, args, name, flops, scratch=(), scalars=None, collective=None
):
    moved = sum(math.prod(arg.shape) * arg.dtype.itemsize for arg in args)
    moved += sum(math.prod(shape) * jnp.dtype(kind).itemsize for shape, kind, _ in outputs)
    grid_spec = pltpu.PrefetchScalarGridSpec(
        num_scalar_prefetch=0 if scalars is None else 1,
        grid=grid,
        in_specs=inputs,
        out_specs=[block for _, _, block in outputs],
        scratch_shapes=list(scratch),
    )
    given = args if scalars is None else [scalars] + list(args)
    return pl.pallas_call(
        kernel,
        grid_spec=grid_spec,
        out_shape=[jax.ShapeDtypeStruct(shape, kind) for shape, kind, _ in outputs],
        compiler_params=pltpu.CompilerParams(
            vmem_limit_bytes=60 * MIB,
            collective_id=collective,
            has_side_effects=collective is not None,
        ),
        cost_estimate=pl.CostEstimate(flops=flops, bytes_accessed=moved, transcendentals=0),
        name=name,
    )(*given)


def square(block):
    return block.reshape(-1, block.shape[-1])


def chunks(count, size=256):
    return [pl.ds(start, min(size, count)) for start in range(0, count, min(size, count))]


def carry(refs, bundles):
    refs = list(refs)
    take = lambda count: [refs.pop(0) for _ in range(count)]
    return take, (take(len(bundles)), [take(count) for count in bundles])


def project_kernel(
    x_ref, hot_ref, shift_ref, scale_ref, w_ref, bias_ref, seg_ref, *refs, block, bundles
):
    take, given = carry(refs, bundles)
    (goal_in,) = take(1)
    qkv_ref, modt_ref, out_ref, total_ref = take(4)
    targets = take(len(bundles))
    (goal_out,) = take(1)
    (low_ref,) = take(1)
    gather = Gather(*given, targets, take(Gather.room(len(bundles))))
    tokens = Rounds([goal_in], [goal_out], take(2))
    head = pl.program_id(0)
    width = x_ref.shape[1]

    @pl.when(head == 0)
    def _():
        gather.link.greet()
        gather.start()
        gather.start_local()
        tokens.start()
        for rows in chunks(x_ref.shape[0]):
            normed, _ = norm_stats(x_ref[rows, :].astype(F32))
            hot = hot_ref[rows, :]
            low = normed * (1.0 + dot_nn(hot, scale_ref[...])) + dot_nn(hot, shift_ref[...])
            low_ref[rows, :] = low.astype(BF)
            modt_ref[:, rows] = low.astype(BF).T
        for j in range(3):
            columns = pl.ds(j * width, width)
            weight = square(w_ref[:, j])
            for rows in chunks(x_ref.shape[0]):
                qkv_ref[rows, columns] = (
                    dot_nn(low_ref[rows, :], weight) + bias_ref[:, columns]
                ).astype(BF)

    for index, step in enumerate(gather.steps()):
        pl.when(head == GATHER_AT[index])(step)
    parts = ((qkv_ref, 0), (qkv_ref, width), (qkv_ref, 2 * width))
    attend_head(head, parts, (seg_ref, seg_ref), out_ref, total_ref, block)

    @pl.when(head == pl.num_programs(0) - 1)
    def _():
        gather.finish()
        tokens.finish()


def project(x, hot, mod, weights, bias, seg, heads, slices, shards, goals, collective):
    tokens, width = x.shape
    seq, _, per, _ = weights.shape
    part = lambda index: spec((mod.shape[0], width), lambda h: (0, index), once=True)
    flat = list(slices) + [array for shard in shards for array in shard]
    return call(
        functools.partial(
            project_kernel, block=min(256, tokens), bundles=[len(shard) for shard in shards]
        ),
        (heads,),
        [
            fixed((tokens, width)),
            fixed(hot.shape),
            part(0),
            part(1),
            spec((seq, 3, per, width), lambda h: (0, 0, 0, 0), once=True),
            fixed((1, 3 * width)),
            fixed(seg.shape),
        ]
        + [ANY] * (len(flat) + 1),
        [
            ((tokens, 3 * width), BF, fixed((tokens, 3 * width))),
            ((width, tokens), BF, fixed((width, tokens))),
            ((tokens, width), BF, fixed((tokens, width))),
            ((heads, tokens), F32, fixed((heads, tokens))),
        ]
        + [(shape.shape, BF, ANY) for shape in gathered(slices, shards)]
        + [(goals.shape, BF, ANY)],
        [x, hot, mod, mod, weights, bias, seg] + flat + [goals],
        "project",
        6 * tokens * width * width + heads * tokens * tokens * 4 * 256,
        [pltpu.VMEM((tokens, width), BF)]
        + Gather.scratch(gathered(slices, shards))
        + Rounds.scratch(1),
        collective=collective,
    )


def merge_kernel(
    out_ref, x_ref, hot_ref, gate_ref, shift_ref, scale_ref, w_ref, bias_ref,
    branch_ref, mid_ref, low_ref, lowt_ref, outt_ref,
):
    hot = hot_ref[...]
    branch = dot_nn(out_ref[...], square(w_ref[...])) + bias_ref[...]
    middle = x_ref[...].astype(F32) + dot_nn(hot, gate_ref[...]) * branch
    normed, _ = norm_stats(middle)
    low = normed * (1.0 + dot_nn(hot, scale_ref[...])) + dot_nn(hot, shift_ref[...])
    low = low.astype(BF)
    branch_ref[...] = branch.astype(BF)
    mid_ref[...] = middle
    low_ref[...] = low
    lowt_ref[...] = low.T
    outt_ref[...] = out_ref[...].T


def merge(attended, x, hot, mod, weights, bias):
    tokens, width = x.shape
    seq, _, per, _ = weights.shape
    size = min(256, tokens)
    part = lambda index: spec((mod.shape[0], width), lambda i: (0, index), once=True)
    rows = spec((size, width), lambda i: (i, 0))
    turned = spec((width, size), lambda i: (0, i))
    return call(
        merge_kernel,
        (tokens // size,),
        [
            rows,
            rows,
            spec((size, hot.shape[1]), lambda i: (i, 0)),
            part(2),
            part(3),
            part(4),
            spec((seq, 1, per, width), lambda i: (0, 3, 0, 0), once=True),
            fixed((1, width)),
        ],
        [
            ((tokens, width), BF, rows),
            ((tokens, width), F32, rows),
            ((tokens, width), BF, rows),
            ((width, tokens), BF, turned),
            ((width, tokens), BF, turned),
        ],
        [attended, x, hot, mod, mod, mod, weights, bias],
        "merge",
        2 * tokens * width * width,
    )


def gelu_pair(value):
    factor = math.sqrt(2.0 / math.pi)
    squared = value * value
    tangent = jnp.tanh(factor * value * (1.0 + GELU_COEF * squared))
    half = 0.5 * (1.0 + tangent)
    slope = half + (0.5 * factor) * value * (1.0 - tangent * tangent) * (
        1.0 + 3.0 * GELU_COEF * squared
    )
    return value * half, slope


def feed_kernel(
    low_ref, w_in_ref, b_in_ref, w_out_ref, b_out_ref, mid_ref, hot_ref, gate_ref, *refs, bundles
):
    take, given = carry(refs, bundles)
    actt_ref, slope_ref, res_ref, rest_ref, branch_ref = take(5)
    targets = take(len(bundles))
    (total,) = take(1)
    gather = Gather(*given, targets, take(Gather.room(len(bundles))))
    steps = gather.steps()
    step = pl.program_id(0)

    @pl.when(step == 0)
    def _():
        gather.link.greet()
        gather.start()
        gather.start_local()
        total[...] = jnp.zeros_like(total)

    w_in, w_out = square(w_in_ref[...]), w_out_ref[...]
    pieces = chunks(low_ref.shape[0])
    for number, rows in enumerate(pieces):
        if number % 2 == 0:
            for index, action in enumerate(steps):
                if FEED_AT[index] % 2 == number // 2:
                    pl.when(step == FEED_AT[index] // 2)(action)
        hmid = dot_nn(low_ref[rows, :], w_in) + b_in_ref[...]
        act, slope = gelu_pair(hmid)
        act = act.astype(BF)
        slope_ref[rows, :] = slope.astype(BF)
        actt_ref[:, rows] = act.T
        total[rows, :] += dot_nn(act, w_out)

    @pl.when(step == pl.num_programs(0) - 1)
    def _():
        for rows in pieces:
            branch = total[rows, :] + b_out_ref[...]
            result = mid_ref[rows, :] + dot_nn(hot_ref[rows, :], gate_ref[...]) * branch
            result = result.astype(BF)
            res_ref[rows, :] = result
            rest_ref[:, rows] = result.T
            branch_ref[rows, :] = branch.astype(BF)
        gather.finish()


def feed(low, w_in, b_in, w_out, b_out, mid, hot, mod, slices, shards, collective):
    tokens, width = low.shape
    seq, blocks, per, cut = w_in.shape
    hidden = blocks * cut
    flat = list(slices) + [array for shard in shards for array in shard]
    return call(
        functools.partial(feed_kernel, bundles=[len(shard) for shard in shards]),
        (blocks,),
        [
            fixed((tokens, width)),
            spec((seq, 1, per, cut), lambda j: (0, j, 0, 0)),
            spec((1, cut), lambda j: (0, j)),
            spec((cut, width), lambda j: (j, 0)),
            fixed((1, width)),
            fixed((tokens, width)),
            fixed(hot.shape),
            spec((mod.shape[0], width), lambda j: (0, 5), once=True),
        ]
        + [ANY] * len(flat),
        [
            ((hidden, tokens), BF, spec((cut, tokens), lambda j: (j, 0))),
            ((tokens, hidden), BF, spec((tokens, cut), lambda j: (0, j))),
            ((tokens, width), BF, fixed((tokens, width))),
            ((width, tokens), BF, fixed((width, tokens))),
            ((tokens, width), BF, fixed((tokens, width))),
        ]
        + [(shape.shape, BF, ANY) for shape in gathered(slices, shards)],
        [low, w_in, b_in, w_out, b_out, mid, hot, mod] + flat,
        "feed",
        4 * tokens * width * hidden,
        [pltpu.VMEM((tokens, width), F32)] + Gather.scratch(gathered(slices, shards)),
        collective=collective,
    )


def silu_pair(value):
    gate = jax.nn.sigmoid(value)
    return value * gate, gate * (1.0 + value * (1.0 - gate))


def align_kernel(
    res_ref, w_in_ref, b_in_ref, w_mid_ref, b_mid_ref, w_out_ref, b_out_ref, goal_ref, rows_ref,
    act1t_ref, act2t_ref, gfeat_ref, gh2_ref, gh1_ref, gout_ref, back_ref, act1_ref, slope1_ref,
    *sems,
):
    tokens = Rounds([rows_ref], [back_ref], sems)

    @pl.when(pl.program_id(0) == 0)
    def _():
        tokens.link.greet()
        tokens.start()

    blocks, cut = w_in_ref.shape[1], w_in_ref.shape[3]
    res = res_ref[...]
    for j in range(blocks):
        columns = pl.ds(j * cut, cut)
        hidden1 = dot_nn(res, square(w_in_ref[:, j])) + b_in_ref[:, columns]
        act, slope = silu_pair(hidden1)
        act1_ref[:, columns] = act.astype(BF)
        slope1_ref[:, columns] = slope
    act1 = act1_ref[...]
    act1t_ref[...] = act1.T
    hidden2 = dot_nn(act1, w_mid_ref[...]) + b_mid_ref[...]
    act2, slope2 = silu_pair(hidden2)
    act2 = act2.astype(BF)
    act2t_ref[...] = act2.T
    feats = dot_nn(act2, w_out_ref[...]) + b_out_ref[...]
    goals = goal_ref[...].astype(F32)
    inv_feat = lax.rsqrt(jnp.sum(feats * feats, axis=-1, keepdims=True) + EPSILON)
    feat_unit = feats * inv_feat
    goal_unit = goals * lax.rsqrt(jnp.sum(goals * goals, axis=-1, keepdims=True) + EPSILON)
    cosine = jnp.sum(feat_unit * goal_unit, axis=-1, keepdims=True)
    weight = -0.5 * feats.shape[1]
    gfeat = (weight * inv_feat * (goal_unit - cosine * feat_unit)).astype(BF)
    gfeat_ref[...] = gfeat
    gh2 = (dot_nt(gfeat, w_out_ref[...]) * slope2).astype(BF)
    gh2_ref[...] = gh2
    gh1 = (dot_nt(gh2, w_mid_ref[...]) * slope1_ref[...]).astype(BF)
    gh1_ref[...] = gh1
    total = None
    for j in range(blocks):
        part = dot_nt(gh1_ref[:, pl.ds(j * cut, cut)], square(w_in_ref[:, j]))
        total = part if total is None else total + part
    gout_ref[...] = total
    pl.when(pl.program_id(0) == pl.num_programs(0) - 1)(tokens.finish)


def align(res, w_in, b_in, w_mid, b_mid, w_out, b_out, goals, collective):
    tokens, width = res.shape
    inner, goal_width = w_out.shape
    size = min(256, tokens)
    rows = lambda n: spec((size, n), lambda i: (i, 0))
    turned = lambda n: spec((n, size), lambda i: (0, i))
    return call(
        align_kernel,
        (tokens // size,),
        [
            rows(width),
            fixed(w_in.shape),
            fixed((1, inner)),
            fixed(w_mid.shape),
            fixed((1, inner)),
            fixed(w_out.shape),
            fixed((1, goal_width)),
            rows(goal_width),
            ANY,
        ],
        [
            ((inner, tokens), BF, turned(inner)),
            ((inner, tokens), BF, turned(inner)),
            ((tokens, goal_width), BF, rows(goal_width)),
            ((tokens, inner), BF, rows(inner)),
            ((tokens, inner), BF, rows(inner)),
            ((tokens, width), F32, rows(width)),
            ((SEQ, tokens // SEQ, width), BF, ANY),
        ],
        [res, w_in, b_in, w_mid, b_mid, w_out, b_out, goals, res.reshape(SEQ, -1, width)],
        "align",
        4 * tokens * inner * (width + inner + goal_width),
        [pltpu.VMEM((size, inner), BF), pltpu.VMEM((size, inner), F32)] + Rounds.scratch(1),
        collective=collective,
    )


def feed_back_kernel(
    gout_ref, branch_ref, hot_ref, hott_ref, gate_ref, w_out_ref, slope_ref, w_in_ref,
    gmlp_ref, ghmid_ref, gmod_ref, ggate_ref,
):
    step = pl.program_id(0)

    @pl.when(step == 0)
    def _():
        sums = None
        for rows in chunks(gout_ref.shape[0]):
            gout = gout_ref[rows, :]
            gmlp_ref[rows, :] = (gout * dot_nn(hot_ref[rows, :], gate_ref[...])).astype(BF)
            part = dot_nn(hott_ref[:, rows], (gout * branch_ref[rows, :].astype(F32)).astype(BF))
            sums = part if sums is None else sums + part
        ggate_ref[...] = sums
        gmod_ref[...] = jnp.zeros_like(gmod_ref)

    w_out, w_in = w_out_ref[...], square(w_in_ref[...])
    for rows in chunks(gout_ref.shape[0]):
        ghmid = (dot_nt(gmlp_ref[rows, :], w_out) * slope_ref[rows, :].astype(F32)).astype(BF)
        ghmid_ref[rows, :] = ghmid
        gmod_ref[rows, :] += dot_nt(ghmid, w_in)


def feed_back(gout, branch, hot, hott, mod, w_out, slope, w_in):
    tokens, width = gout.shape
    seq, blocks, per, cut = w_in.shape
    hidden = blocks * cut
    return call(
        feed_back_kernel,
        (blocks,),
        [
            fixed((tokens, width)),
            fixed((tokens, width)),
            fixed(hot.shape),
            fixed(hott.shape),
            spec((mod.shape[0], width), lambda j: (0, 5), once=True),
            spec((cut, width), lambda j: (j, 0)),
            spec((tokens, cut), lambda j: (0, j)),
            spec((seq, 1, per, cut), lambda j: (0, j, 0, 0)),
        ],
        [
            ((tokens, width), BF, fixed((tokens, width))),
            ((tokens, hidden), BF, spec((tokens, cut), lambda j: (0, j))),
            ((tokens, width), F32, fixed((tokens, width))),
            ((hott.shape[0], width), F32, fixed((hott.shape[0], width))),
        ],
        [gout, branch, hot, hott, mod, w_out, slope, w_in],
        "feed_back",
        4 * tokens * width * hidden,
    )


def add_rows(ref, value):
    @pl.when(pl.program_id(0) == 0)
    def _():
        ref[...] = value

    @pl.when(pl.program_id(0) > 0)
    def _():
        ref[...] += value


def merge_back_kernel(
    gout_ref, gmod_ref, mid_ref, branch_ref, hot_ref, hott_ref, gate_ref, scale_ref, w_ref,
    gmid_ref, gbranch_ref, gatt_ref, gshift_ref, gscale_ref, ggate_ref,
):
    hot, hott = hot_ref[...], hott_ref[...]
    gmod = gmod_ref[...]
    normed, inv_std = norm_stats(mid_ref[...])
    gmid = gout_ref[...] + norm_back(
        gmod * (1.0 + dot_nn(hot, scale_ref[...])), normed, inv_std
    )
    gmid_ref[...] = gmid
    gbranch = (gmid * dot_nn(hot, gate_ref[...])).astype(BF)
    gbranch_ref[...] = gbranch
    gatt_ref[...] = dot_nt(gbranch, square(w_ref[...])).astype(BF)
    add_rows(gshift_ref, dot_nn(hott, gmod.astype(BF)))
    add_rows(gscale_ref, dot_nn(hott, (gmod * normed).astype(BF)))
    add_rows(ggate_ref, dot_nn(hott, (gmid * branch_ref[...].astype(F32)).astype(BF)))


def merge_back(gout, gmod, mid, branch, hot, hott, mod, weights):
    tokens, width = gout.shape
    seq, _, per, _ = weights.shape
    size = min(256, tokens)
    part = lambda index: spec((mod.shape[0], width), lambda i: (0, index), once=True)
    rows = spec((size, width), lambda i: (i, 0))
    sums = ((hott.shape[0], width), F32, fixed((hott.shape[0], width)))
    return call(
        merge_back_kernel,
        (tokens // size,),
        [
            rows,
            rows,
            rows,
            rows,
            spec((size, hot.shape[1]), lambda i: (i, 0)),
            spec((hott.shape[0], size), lambda i: (0, i)),
            part(2),
            part(4),
            spec((seq, 1, per, width), lambda i: (0, 3, 0, 0), once=True),
        ],
        [
            ((tokens, width), F32, rows),
            ((tokens, width), BF, rows),
            ((tokens, width), BF, rows),
            sums,
            sums,
            sums,
        ],
        [gout, gmod, mid, branch, hot, hott, mod, mod, weights],
        "merge_back",
        2 * tokens * width * width,
    )


def project_back_kernel(
    gqkv_ref, x_ref, gmid_ref, hot_ref, hott_ref, scale_ref, w_ref, *refs, carried
):
    refs = list(refs)
    take = lambda number: [refs.pop(0) for _ in range(number)]
    sums = take(carried)
    gin_ref, gshift_ref, gscale_ref = take(3)
    work = Sum(sums, take(carried), refs)

    @pl.when(pl.program_id(0) == 0)
    def _():
        work.link.greet()
        work.start()

    width = x_ref.shape[1]
    hott = hott_ref[...]
    gmod = None
    for j in range(3):
        part = dot_nt(gqkv_ref[:, pl.ds(j * width, width)], square(w_ref[:, j]))
        gmod = part if gmod is None else gmod + part
    normed, inv_std = norm_stats(x_ref[...].astype(F32))
    gin = gmid_ref[...] + norm_back(
        gmod * (1.0 + dot_nn(hot_ref[...], scale_ref[...])), normed, inv_std
    )
    gin_ref[...] = gin.astype(BF)
    add_rows(gshift_ref, dot_nn(hott, gmod.astype(BF)))
    add_rows(gscale_ref, dot_nn(hott, (gmod * normed).astype(BF)))

    @pl.when(pl.program_id(0) == pl.num_programs(0) - 1)
    def _():
        for k in range(carried):
            work.add(k)
        work.finish()


def project_back(gqkv, x, gmid, hot, hott, mod, weights, carried, collective):
    tokens, width = x.shape
    seq, _, per, _ = weights.shape
    size = min(256, tokens)
    rows = spec((size, width), lambda i: (i, 0))
    sums = ((hott.shape[0], width), F32, fixed((hott.shape[0], width)))
    return call(
        functools.partial(project_back_kernel, carried=len(carried)),
        (tokens // size,),
        [
            spec((size, 3 * width), lambda i: (i, 0)),
            rows,
            rows,
            spec((size, hot.shape[1]), lambda i: (i, 0)),
            spec((hott.shape[0], size), lambda i: (0, i)),
            spec((mod.shape[0], width), lambda i: (0, 1), once=True),
            spec((seq, 3, per, width), lambda i: (0, 0, 0, 0), once=True),
        ]
        + [ANY] * len(carried),
        [((tokens, width), BF, rows), sums, sums]
        + [(total.shape[1:], total.dtype, ANY) for total in carried],
        [gqkv, x, gmid, hot, hott, mod, weights] + list(carried),
        "project_back",
        6 * tokens * width * width,
        Sum.scratch(carried),
        collective=collective,
    )


def weight_kernel(where_ref, left_ref, right_ref, *refs, first):
    left = left_ref[...].reshape(-1, left_ref.shape[-1])
    got_ref = None if first else refs[0]
    out_ref = refs[0] if first else refs[1]
    result = dot_nn(left, right_ref[...]).reshape(out_ref.shape)
    if first:
        ones = jnp.ones((16, right_ref.shape[0]), BF)
        refs[1][...] = dot_nn(ones, right_ref[...])
    else:
        result = result + got_ref[...].astype(F32)
    out_ref[...] = result.astype(BF)


def weight_half(where, turned, right, seq, planes, by_columns, got=None):
    count, tokens = turned.shape
    columns = right.shape[1]
    first = got is None
    half = (lambda w: 1 - w[0]) if first else (lambda w: w[0])
    if by_columns:
        per, cut = count // seq // 2, columns // planes
        left = turned.reshape(seq, 2, per, tokens)
        left_spec = spec((seq, 1, per, tokens), lambda j, w: (0, half(w), 0, 0))
        right_spec = spec((tokens, cut), lambda j, w: (0, j))
        sum_spec = spec((16, cut), lambda j, w: (0, j))
    else:
        per, cut = count // seq // planes // 2, columns
        left = turned.reshape(seq, planes, 2, per, tokens)
        left_spec = spec((seq, 1, 1, per, tokens), lambda j, w: (0, j, half(w), 0, 0))
        right_spec = spec((tokens, cut), lambda j, w: (0, 0))
        sum_spec = spec((16, cut), lambda j, w: (0, 0))
    block = spec((1, seq, per, cut), lambda j, w: (j, 0, 0, 0))
    outputs = [((planes, seq, per, cut), BF, block)]
    inputs, args = [left_spec, right_spec], [left, right]
    if first:
        outputs.append(((16, columns), F32, sum_spec))
    else:
        inputs.append(block)
        args.append(got)
    return call(
        functools.partial(weight_kernel, first=first),
        (planes,),
        inputs,
        outputs,
        args,
        "weight_other" if first else "weight_own",
        count * tokens * columns,
        scalars=where,
    )


ANY = pl.BlockSpec(memory_space=pl.ANY)
SEQ, PLANES = 4, 4


class Link:
    def __init__(self):
        self.z, self.p, self.c = (lax.axis_index(name) for name in ("seq", "plane", "core"))

    def ahead(self, shift):
        return lax.rem(self.z + shift, SEQ)

    def behind(self, shift):
        return lax.rem(self.z + SEQ - shift, SEQ)

    def across(self, bit):
        low = lax.rem(self.p, 2)
        high = self.p // 2
        low = 1 - low if bit % 2 else low
        high = 1 - high if bit // 2 else high
        return high * 2 + low

    def copy(self, source, target, sems, axis, index):
        return pltpu.make_async_remote_copy(
            src_ref=source,
            dst_ref=target,
            send_sem=sems[0],
            recv_sem=sems[1],
            device_id={axis: index},
            device_id_type=pl.DeviceIdType.MESH,
        )

    def greet(self):
        barrier = pltpu.get_barrier_semaphore()
        for step in range(1, SEQ):
            signal = functools.partial(
                pl.semaphore_signal, barrier, inc=1, device_id_type=pl.DeviceIdType.MESH
            )
            signal(device_id={"seq": self.ahead(step)})
            signal(device_id={"plane": self.across(step)})
        pl.semaphore_signal(
            barrier, inc=1, device_id={"core": 1 - self.c}, device_id_type=pl.DeviceIdType.MESH
        )
        pl.semaphore_wait(barrier, 2 * SEQ - 1)


class Gather:
    def __init__(self, slices, shards, targets, sems):
        self.link = Link()
        self.slices, self.shards, self.targets = slices, shards, targets
        self.z_sems, self.p_sems, self.c_sems, self.local_sems, self.out_sems = sems[:5]
        self.bufs = sems[5:]

    @staticmethod
    def scratch(targets):
        dma = pltpu.SemaphoreType.DMA
        count = len(targets)
        return [
            dma((2, count, 3)),
            dma((2, count, 3, 6)),
            dma((2, count, 3)),
            dma((count, 4)),
            dma((count,)),
        ] + [pltpu.VMEM(target.shape[1:], BF) for target in targets]

    @staticmethod
    def room(count):
        return 5 + count

    def rows(self, target):
        half = target.shape[2] // 2
        return pl.ds(pl.multiple_of(self.link.c * half, half), half)

    def locals(self):
        for k, (shard, target) in enumerate(zip(self.shards, self.targets)):
            width = target.shape[3]
            block = 0
            for array in shard:
                if len(array.shape) == 3:
                    parts = [array.at[index] for index in range(array.shape[0])]
                else:
                    parts = [
                        array.at[:, pl.ds(start, width)]
                        for start in range(0, array.shape[1], width)
                    ]
                for part in parts:
                    yield pltpu.make_async_copy(
                        part, self.bufs[k].at[block], self.local_sems.at[k, block]
                    )
                    block += 1

    def stored(self, k):
        return pltpu.make_async_copy(
            self.bufs[k], self.targets[k].at[self.link.z], self.out_sems.at[k]
        )

    def store(self):
        for copy in self.locals():
            copy.wait()
        for k in range(len(self.targets)):
            self.stored(k).start()

    def along(self, k, shift, incoming):
        link, target = self.link, self.targets[k]
        place = link.behind(shift) if incoming else link.z
        return link.copy(
            self.slices[k],
            target.at[place, link.p, self.rows(target), :],
            (self.z_sems.at[0, k, shift - 1], self.z_sems.at[1, k, shift - 1]),
            "seq",
            link.ahead(shift),
        )

    def across(self, k, shift, index, incoming):
        link, target = self.link, self.targets[k]
        half = target.shape[2] // 2
        first = -(-half // 32) * 16
        start, size = ((0, first), (first, half - first))[index % 2]
        peer = (1, 1, 2, 2, 2, 1)[index]
        plane = link.p
        if incoming:
            plane = link.across(3 if index >= 4 else peer)
        elif index >= 4:
            plane = link.across(3 - peer)
        rows = pl.ds(pl.multiple_of(link.c * half + start, 16), size)
        place = target.at[link.behind(shift), plane, rows, :]
        return link.copy(
            place,
            place,
            (self.p_sems.at[0, k, shift - 1, index], self.p_sems.at[1, k, shift - 1, index]),
            "plane",
            link.across(peer),
        )

    def beside(self, k, shift, incoming):
        link, target = self.link, self.targets[k]
        half = target.shape[2] // 2
        core = 1 - link.c if incoming else link.c
        rows = pl.ds(pl.multiple_of(core * half, half), half)
        place = target.at[link.behind(shift), :, rows, :]
        return link.copy(
            place,
            place,
            (self.c_sems.at[0, k, shift - 1], self.c_sems.at[1, k, shift - 1]),
            "core",
            1 - link.c,
        )

    def start(self):
        for k in range(len(self.targets)):
            for shift in (1, 3, 2):
                self.along(k, shift, False).start()

    def start_local(self):
        for copy in self.locals():
            copy.start()

    def steps(self):
        return [self.store] + [
            functools.partial(stage, k, shift)
            for k in range(len(self.targets))
            for stage in (self.spread, self.relay, self.pair)
            for shift in (1, 3, 2)
        ]

    def spread(self, k, shift):
        self.along(k, shift, True).wait_recv()
        for index in (0, 3, 1, 2):
            self.across(k, shift, index, False).start()

    def relay(self, k, shift):
        self.across(k, shift, 0, True).wait_recv()
        self.across(k, shift, 4, False).start()
        self.across(k, shift, 3, True).wait_recv()
        self.across(k, shift, 5, False).start()

    def pair(self, k, shift):
        for index in (1, 2, 4, 5):
            self.across(k, shift, index, True).wait_recv()
        self.beside(k, shift, False).start()

    def finish(self):
        for k in range(len(self.targets)):
            for shift in range(1, SEQ):
                self.beside(k, shift, True).wait_recv()
                self.along(k, shift, False).wait_send()
                self.beside(k, shift, False).wait_send()
                for index in range(6):
                    self.across(k, shift, index, False).wait_send()
            self.stored(k).wait()


class Rounds:
    def __init__(self, sources, targets, sems):
        self.link = Link()
        self.sources, self.targets, self.sems, self.local_sems = sources, targets, *sems

    @staticmethod
    def scratch(count):
        dma = pltpu.SemaphoreType.DMA
        return [dma((2, count, 3)), dma((count,))]

    def along(self, k, shift, incoming):
        link = self.link
        return link.copy(
            self.sources[k].at[link.ahead(shift)],
            self.targets[k].at[link.behind(shift) if incoming else link.z],
            (self.sems.at[0, k, shift - 1], self.sems.at[1, k, shift - 1]),
            "seq",
            link.ahead(shift),
        )

    def local(self, k):
        z = self.link.z
        return pltpu.make_async_copy(
            self.sources[k].at[z], self.targets[k].at[z], self.local_sems.at[k]
        )

    def start(self):
        for k in range(len(self.targets)):
            for shift in (2, 1, 3):
                self.along(k, shift, False).start()
            self.local(k).start()

    def finish(self):
        for k in range(len(self.targets)):
            for shift in range(1, SEQ):
                self.along(k, shift, True).wait_recv()
                self.along(k, shift, False).wait_send()
            self.local(k).wait()


class Sum:
    def __init__(self, sources, results, refs):
        self.link = Link()
        self.sources, self.results = sources, results
        self.bufs = refs[: len(sources)]
        self.sems, self.local_sems = refs[len(sources) :]

    @staticmethod
    def scratch(sources):
        dma = pltpu.SemaphoreType.DMA
        bufs = [pltpu.VMEM((5,) + source.shape[1:], source.dtype) for source in sources]
        return bufs + [dma((2, len(sources), 3)), dma((len(sources), 2))]

    def along(self, k, shift):
        link = self.link
        return link.copy(
            self.sources[k].at[link.ahead(shift)],
            self.bufs[k].at[shift - 1],
            (self.sems.at[0, k, shift - 1], self.sems.at[1, k, shift - 1]),
            "seq",
            link.ahead(shift),
        )

    def mine(self, k):
        return pltpu.make_async_copy(
            self.sources[k].at[self.link.z], self.bufs[k].at[3], self.local_sems.at[k, 0]
        )

    def stored(self, k):
        return pltpu.make_async_copy(
            self.bufs[k].at[4], self.results[k], self.local_sems.at[k, 1]
        )

    def start(self):
        for k in range(len(self.sources)):
            for shift in (2, 1, 3):
                self.along(k, shift).start()
            self.mine(k).start()

    def add(self, k):
        for shift in range(1, SEQ):
            self.along(k, shift).wait_recv()
        self.mine(k).wait()
        buf = self.bufs[k]
        total = buf[0].astype(F32) + buf[1].astype(F32) + buf[2].astype(F32) + buf[3].astype(F32)
        buf[4] = total.astype(buf.dtype)
        self.stored(k).start()

    def finish(self):
        for k in range(len(self.sources)):
            for shift in range(1, SEQ):
                self.along(k, shift).wait_send()
            self.stored(k).wait()


class Share:
    def __init__(self, sources, targets, refs):
        self.link = Link()
        self.sources, self.targets = sources, targets
        self.bufs = refs[: len(sources)]
        self.p_sems, self.c_sems, self.local_sems = refs[len(sources) :]

    @staticmethod
    def scratch(sources, shared):
        dma = pltpu.SemaphoreType.DMA
        count = len(sources)
        bufs = [
            pltpu.VMEM((5 if one else 1,) + source.shape[-2:], source.dtype)
            for source, one in zip(sources, shared)
        ]
        return bufs + [dma((2, count, 3)), dma((2, count, 4)), dma((count, 2))]

    def shared(self, k):
        return len(self.targets[k].shape) == 3

    def loaded(self, k):
        return pltpu.make_async_copy(self.sources[k], self.bufs[k].at[0], self.local_sems.at[k, 0])

    def across(self, k, bit, incoming):
        link = self.link
        plane = link.across(bit)
        if self.shared(k):
            target = self.bufs[k].at[bit]
        else:
            target = self.targets[k].at[plane if incoming else link.p, link.c]
        return link.copy(
            self.bufs[k].at[0],
            target,
            (self.p_sems.at[0, k, bit - 1], self.p_sems.at[1, k, bit - 1]),
            "plane",
            plane,
        )

    def beside(self, k, bit, incoming):
        link = self.link
        core = 1 - link.c if incoming else link.c
        if self.shared(k):
            source, target = self.bufs[k].at[4], self.targets[k].at[core]
        else:
            plane = link.across(bit)
            target = self.targets[k].at[plane, core]
            source = self.bufs[k].at[0] if bit == 0 else self.targets[k].at[plane, link.c]
        return link.copy(
            source,
            target,
            (self.c_sems.at[0, k, bit], self.c_sems.at[1, k, bit]),
            "core",
            1 - link.c,
        )

    def own(self, k):
        link = self.link
        if self.shared(k):
            source, target = self.bufs[k].at[4], self.targets[k].at[link.c]
        else:
            source, target = self.bufs[k].at[0], self.targets[k].at[link.p, link.c]
        return pltpu.make_async_copy(source, target, self.local_sems.at[k, 1])

    def send(self, k):
        for bit in range(1, PLANES):
            self.across(k, bit, False).start()
        if not self.shared(k):
            self.own(k).start()
            self.beside(k, 0, False).start()

    def pass_on(self, k):
        for bit in range(1, PLANES):
            self.across(k, bit, True).wait_recv()
            if not self.shared(k):
                self.beside(k, bit, False).start()
        if self.shared(k):
            buf = self.bufs[k]
            total = buf[0].astype(F32) + buf[1].astype(F32) + buf[2].astype(F32) + buf[3].astype(F32)
            buf[4] = total.astype(buf.dtype)
            self.own(k).start()
            self.beside(k, 0, False).start()

    def finish(self):
        for k in range(len(self.targets)):
            for bit in range(1 if self.shared(k) else PLANES):
                self.beside(k, bit, True).wait_recv()
                self.beside(k, bit, False).wait_send()
            for bit in range(1, PLANES):
                self.across(k, bit, False).wait_send()
            self.own(k).wait()


def bring_kernel(*refs, bundles, rounds):
    refs = list(refs)
    take = lambda count: [refs.pop(0) for _ in range(count)]
    slices = take(len(bundles))
    shards = [take(count) for count in bundles]
    sources = take(rounds)
    targets = take(len(bundles))
    arrived = take(rounds)
    gather = Gather(slices, shards, targets, take(Gather.room(len(bundles))))
    tokens = Rounds(sources, arrived, take(2))
    gather.link.greet()
    gather.start()
    tokens.start()
    gather.start_local()
    for step in gather.steps():
        step()
    tokens.finish()
    gather.finish()


def gathered(slices, shards):
    shapes = []
    for piece, shard in zip(slices, shards):
        cut = piece.shape[1]
        if shard[0].ndim == 3:
            blocks, per = shard[0].shape[:2]
        else:
            blocks, per = sum(array.shape[1] for array in shard) // cut, shard[0].shape[0]
        shapes.append(jax.ShapeDtypeStruct((SEQ, blocks, per, cut), BF))
    return shapes


def bring(slices, shards, sources, collective):
    flat = [array for shard in shards for array in shard]
    shapes = gathered(slices, shards) + [jax.ShapeDtypeStruct(array.shape, array.dtype) for array in sources]
    args = list(slices) + flat + list(sources)
    return pl.pallas_call(
        functools.partial(
            bring_kernel, bundles=[len(shard) for shard in shards], rounds=len(sources)
        ),
        in_specs=[ANY] * len(args),
        out_specs=[ANY] * len(shapes),
        out_shape=shapes,
        scratch_shapes=Gather.scratch(gathered(slices, shards)) + Rounds.scratch(len(sources)),
        compiler_params=pltpu.CompilerParams(
            collective_id=collective, has_side_effects=True, vmem_limit_bytes=60 * MIB
        ),
        cost_estimate=pl.CostEstimate(flops=0, bytes_accessed=300_000_000, transcendentals=0),
        name="bring",
    )(*args)


def settle_kernel(*refs, sums, shares, rounds, through):
    refs = list(refs)
    take = lambda number: [refs.pop(0) for _ in range(number)]
    sum_in, share_in, round_in = take(sums), take(shares), take(rounds)
    sum_out, share_out, round_out = take(sums), take(shares + sums * through), take(rounds)
    add = Sum(sum_in, sum_out, take(sums + 2))
    share = Share(share_in + sum_in * through, share_out, take(len(share_out) + 3))
    tokens = Rounds(round_in, round_out, take(2)) if rounds else None
    add.link.greet()
    add.start()
    if rounds:
        tokens.start()
    for k in range(shares):
        share.loaded(k).start()
    for k in range(shares):
        share.loaded(k).wait()
        share.send(k)
    for k in range(shares):
        share.pass_on(k)
    for k in range(sums):
        add.add(k)
        if through:
            share.bufs[shares + k][0] = add.bufs[k][4]
            share.send(shares + k)
    if through:
        for k in range(sums):
            share.pass_on(shares + k)
    add.finish()
    share.finish()
    if rounds:
        tokens.finish()


def summed(array):
    return jax.ShapeDtypeStruct(array.shape[1:], array.dtype)


def shared_out(array, shared):
    return jax.ShapeDtypeStruct(
        ((2,) if shared else (PLANES, 2)) + array.shape[-2:], array.dtype
    )


def settle(sums, shares, rounds, shared, collective, through=False):
    args = list(sums) + list(shares) + list(rounds)
    given = list(shares) + (list(sums) if through else [])
    shapes = (
        [summed(array) for array in sums]
        + [shared_out(array, one) for array, one in zip(given, shared)]
        + [jax.ShapeDtypeStruct(array.shape, array.dtype) for array in rounds]
    )
    return pl.pallas_call(
        functools.partial(
            settle_kernel,
            sums=len(sums),
            shares=len(shares),
            rounds=len(rounds),
            through=int(through),
        ),
        in_specs=[ANY] * len(args),
        out_specs=[ANY] * len(shapes),
        out_shape=shapes,
        scratch_shapes=Sum.scratch(sums)
        + Share.scratch(given, shared)
        + (Rounds.scratch(len(rounds)) if rounds else []),
        compiler_params=pltpu.CompilerParams(
            collective_id=collective, has_side_effects=True, vmem_limit_bytes=60 * MIB
        ),
        cost_estimate=pl.CostEstimate(flops=0, bytes_accessed=200_000_000, transcendentals=0),
        name="settle",
    )(*args)


def local(
    block_input,
    modulation,
    segment_ids,
    qkv_weight,
    query_value_bias,
    attn_out_weight,
    attn_out_bias,
    mlp_in_weight,
    mlp_in_bias,
    mlp_out_weight,
    mlp_out_bias,
    proj_in_weight,
    proj_in_bias,
    proj_mid_weight,
    proj_mid_bias,
    proj_out_weight,
    proj_out_bias,
    targets,
):
    rows, span, width = block_input.shape
    segs = modulation.shape[1]
    seq = lax.axis_size("seq")
    place = Rows(seq, rows)
    heads = width // HEAD_DIM
    hidden = mlp_in_weight.shape[1]
    inner = proj_mid_weight.shape[1]
    goal_width = targets.shape[2]
    tokens = rows * span
    share = place.share

    x_in = jnp.concatenate(place.to_rows(block_input), axis=0)
    seg_pieces = place.to_rows(segment_ids)
    segs_own = jnp.concatenate(seg_pieces, axis=0)
    seg_query = segs_own[:, None]
    seg_keys = place.gather_parts(seg_query) if share > 1 else seg_query
    goals = jnp.concatenate(place.to_rows(targets), axis=0)
    mod_row = lax.dynamic_index_in_dim(modulation, place.row, 0, keepdims=False)

    per = qkv_weight.shape[0]
    half = inner // 2
    first = gather_slices(own_slice([qkv_weight, attn_out_weight], width))
    second = gather_slices(own_slice([mlp_in_weight], width), first)
    third = gather_slices(own_slice([mlp_out_weight], width), second)
    fourth = gather_slices(own_slice([proj_in_weight], half), third)
    fifth = gather_slices(own_slice([proj_mid_weight], inner), fourth)
    sixth = gather_slices(own_slice([proj_out_weight], goal_width), fifth)
    w_q, w_k, w_v, w_attn = split_rows(first, per)
    w_qkv = jnp.concatenate([w_q, w_k, w_v], axis=1)
    w_mlp_in = jnp.concatenate(split_rows(second, per), axis=1)
    w_mlp_out = third.reshape(hidden, width)
    w_proj_in = jnp.concatenate(split_rows(fourth, per), axis=1)
    w_proj_mid = fifth.reshape(inner, inner)
    w_proj_out = sixth.reshape(inner, goal_width)

    one_hot = (segs_own[:, None] == jnp.arange(segs, dtype=jnp.int32)[None, :]).astype(BF)
    inputs = x_in.astype(F32)
    mod_tok = dot_nn(one_hot, mod_row)
    shift1, scale1, gate1, shift2, scale2, gate2 = (
        mod_tok[:, part * width : (part + 1) * width] for part in range(6)
    )
    normed1, inv_std1 = norm_stats(inputs)
    modulated1 = (normed1 * (1.0 + scale1) + shift1).astype(BF)
    bias_float = query_value_bias.astype(F32)
    full_bias = jnp.concatenate(
        [bias_float[:width], jnp.zeros((width,), F32), bias_float[width:]]
    )
    qkv = (dot_nn(modulated1, w_qkv) + full_bias).astype(BF)
    if share > 1:
        kv_all = place.gather_parts(qkv[:, width:])
        parts = ((qkv, 0), (kv_all, 0), (kv_all, 1))
    else:
        parts = ((qkv, 0), (qkv, 1), (qkv, 2))
    attended, totals = attend_forward(parts, seg_query, seg_keys, heads)
    branch = dot_nn(attended, w_attn) + attn_out_bias.astype(F32)
    middle = inputs + gate1 * branch
    normed2, inv_std2 = norm_stats(middle)
    modulated2 = (normed2 * (1.0 + scale2) + shift2).astype(BF)
    hmid = dot_nn(modulated2, w_mlp_in) + mlp_in_bias.astype(F32)
    act_mid = jax.nn.gelu(hmid, approximate=True).astype(BF)
    mlp_branch = dot_nn(act_mid, w_mlp_out) + mlp_out_bias.astype(F32)
    out_low = (middle + gate2 * mlp_branch).astype(BF)
    hidden1 = dot_nn(out_low, w_proj_in) + proj_in_bias.astype(F32)
    act1 = jax.nn.silu(hidden1).astype(BF)
    hidden2 = dot_nn(act1, w_proj_mid) + proj_mid_bias.astype(F32)
    act2 = jax.nn.silu(hidden2).astype(BF)
    feats = dot_nn(act2, w_proj_out) + proj_out_bias.astype(F32)
    goals = goals.astype(F32)
    inv_feat = lax.rsqrt(jnp.sum(feats * feats, axis=-1, keepdims=True) + EPSILON)
    feat_unit = feats * inv_feat
    goal_unit = goals * lax.rsqrt(jnp.sum(goals * goals, axis=-1, keepdims=True) + EPSILON)
    cosine = jnp.sum(feat_unit * goal_unit, axis=-1, keepdims=True)
    loss_weight = 0.5 * goal_width
    grad_feats = (-loss_weight * inv_feat * (goal_unit - cosine * feat_unit)).astype(BF)

    def blocks(grad, cut):
        low = grad.astype(BF).reshape(seq, grad.shape[0] // seq, grad.shape[1])
        return [low[:, :, start : start + cut] for start in range(0, grad.shape[1], cut)]

    sixth_sum = reduce_bundle(
        jnp.concatenate(blocks(dot_tn(act2, grad_feats), goal_width), axis=1)
    )
    bias_out = jnp.sum(grad_feats.astype(F32), axis=0)
    grad_hidden2 = (dot_nt(grad_feats, w_proj_out) * silu_grad(hidden2)).astype(BF)
    fifth_sum = reduce_bundle(jnp.concatenate(blocks(dot_tn(act1, grad_hidden2), inner), axis=1))
    bias_mid = jnp.sum(grad_hidden2.astype(F32), axis=0)
    grad_hidden1 = (dot_nt(grad_hidden2, w_proj_mid) * silu_grad(hidden1)).astype(BF)
    fourth_sum = reduce_bundle(jnp.concatenate(blocks(dot_tn(out_low, grad_hidden1), half), axis=1))
    bias_in = jnp.sum(grad_hidden1.astype(F32), axis=0)
    grad_output = dot_nt(grad_hidden1, w_proj_in)
    grad_gate2 = grad_output * mlp_branch
    grad_mlp = (grad_output * gate2).astype(BF)
    third_sum = reduce_bundle(jnp.concatenate(blocks(dot_tn(act_mid, grad_mlp), width), axis=1))
    bias_ff_out = jnp.sum(grad_mlp.astype(F32), axis=0)
    grad_hmid = (dot_nt(grad_mlp, w_mlp_out) * gelu_grad(hmid)).astype(BF)
    second_sum = reduce_bundle(jnp.concatenate(blocks(dot_tn(modulated2, grad_hmid), width), axis=1))
    bias_ff_in = jnp.sum(grad_hmid.astype(F32), axis=0)
    grad_modulated2 = dot_nt(grad_hmid, w_mlp_in)
    grad_middle = grad_output + norm_back(grad_modulated2 * (1.0 + scale2), normed2, inv_std2)
    grad_gate1 = grad_middle * branch
    grad_branch = (grad_middle * gate1).astype(BF)
    grad_attn_w = dot_tn(attended, grad_branch)
    bias_attn = jnp.sum(grad_branch.astype(F32), axis=0)
    grad_attended = dot_nt(grad_branch, w_attn).astype(BF)
    grads = attend_backward(parts, seg_query, seg_keys, totals, attended, grad_attended, heads)
    if share > 1:
        grad_qkv = jnp.concatenate(
            [grads[0], place.sum_parts(grads[1]), place.sum_parts(grads[2])], axis=1
        )
    else:
        grad_qkv = grads[0][:, : 3 * width]
    first_sum = reduce_bundle(
        jnp.concatenate(
            blocks(dot_tn(modulated1, grad_qkv), width) + blocks(grad_attn_w, width), axis=1
        )
    )
    column_sums = jnp.sum(grad_qkv.astype(F32), axis=0)
    bias_qv = jnp.concatenate([column_sums[:width], column_sums[2 * width :]])
    grad_modulated1 = dot_nt(grad_qkv, w_qkv)
    grad_input = grad_middle + norm_back(grad_modulated1 * (1.0 + scale1), normed1, inv_std1)

    def by_segment(value):
        return dot_tn(one_hot, value.astype(BF))

    grad_mod = jnp.concatenate(
        [
            by_segment(grad_modulated1),
            by_segment(grad_modulated1 * normed1),
            by_segment(grad_gate1),
            by_segment(grad_modulated2),
            by_segment(grad_modulated2 * normed2),
            by_segment(grad_gate2),
        ],
        axis=-1,
    )
    grad_mod = place.all_parts(grad_mod)
    grad_modulation = lax.all_gather(grad_mod.astype(BF), "seq", axis=0)[:: share].astype(F32)

    def back(value):
        return place.to_spans(
            [value[shift * span : (shift + 1) * span] for shift in range(rows)]
        )

    block_out = back(out_low)
    grad_input = back(grad_input.astype(BF)).astype(F32)

    biases = [bias_qv, bias_attn, bias_ff_in, bias_ff_out, bias_in, bias_mid, bias_out]
    packed = jnp.concatenate([bias.reshape(seq, -1) for bias in biases], axis=1)
    packed = lax.psum(packed, EVERY)
    packed = lax.dynamic_index_in_dim(packed, lax.axis_index("seq"), 0, keepdims=False)
    shares = []
    start = 0
    for bias in biases:
        stop = start + bias.shape[0] // seq
        shares.append(packed[start:stop])
        start = stop

    def columns_of(total, count):
        return [total[start : start + count].astype(F32) for start in range(0, total.shape[0], count)]

    first_parts = columns_of(first_sum, per)
    return (
        block_out,
        grad_input,
        grad_modulation,
        jnp.concatenate(first_parts[:3], axis=1),
        shares[0],
        first_parts[3],
        shares[1],
        jnp.concatenate(columns_of(second_sum, per), axis=1),
        shares[2],
        third_sum.astype(F32),
        shares[3],
        jnp.concatenate(columns_of(fourth_sum, per), axis=1),
        shares[4],
        fifth_sum.astype(F32),
        shares[5],
        sixth_sum.astype(F32),
        shares[6],
    )


def tie(value, *others):
    return lax.optimization_barrier((value,) + others)[0]


def swap_cores(value):
    return lax.ppermute(value, "core", [(0, 1), (1, 0)])


def swap_planes(value, bit):
    return lax.ppermute(value, "plane", [(p, p ^ bit) for p in range(lax.axis_size("plane"))])


def scatter_planes(both, after=None):
    planes, seq, count, columns = both.shape
    flat = both.reshape(planes * seq * count, columns)
    if after is not None:
        flat = tie(flat, after)
    own = lax.psum_scatter(flat, "plane", scatter_dimension=0, tiled=True)
    return own.reshape(seq, count, columns)


def scatter_seq(both):
    seq, count, columns = both.shape
    return lax.psum_scatter(
        both.reshape(seq * count, columns), "seq", scatter_dimension=0, tiled=True
    )


def gather_copies(own):
    full = lax.all_gather(own, COPIES, axis=0, tiled=True)
    return full.reshape(lax.axis_size("plane"), 2, own.shape[0], own.shape[1])


def unpack_kernel(*refs):
    count = len(refs) // 2
    for full_ref, out_ref in zip(refs[:count], refs[count:]):
        out_ref[...] = square(full_ref[...]).astype(F32)


def unpack(*fulls):
    planes = fulls[0][0].shape[0]
    inputs, outputs = [], []
    for full, columns in fulls:
        _, _, count, cut = full.shape
        inputs.append(spec((1, 2, count, cut), lambda p: (p, 0, 0, 0)))
        if columns is None:
            outputs.append(
                ((planes * 2 * count, cut), F32, spec((2 * count, cut), lambda p: (p, 0)))
            )
        else:
            outputs.append(((2 * count, columns), F32, spec((2 * count, cut), lambda p: (0, p))))
    return call(
        unpack_kernel, (planes,), inputs, outputs, [full for full, _ in fulls], "unpack", 0
    )


def local_row(
    block_input, modulation, segment_ids,
    qkv_weight, query_value_bias,
    attn_out_weight, attn_out_bias,
    mlp_in_weight, mlp_in_bias,
    mlp_out_weight, mlp_out_bias,
    proj_in_weight, proj_in_bias,
    proj_mid_weight, proj_mid_bias,
    proj_out_weight, proj_out_bias,
    targets,
):
    rows, span, width = block_input.shape
    seq, planes = lax.axis_size("seq"), lax.axis_size("plane")
    heads = width // HEAD_DIM
    hidden = mlp_in_weight.shape[1]
    inner = proj_mid_weight.shape[1]
    goal_width = targets.shape[2]
    tokens = rows * span
    where = lax.axis_index("core").reshape(1).astype(jnp.int32)

    slice1, _ = own_slice([qkv_weight, attn_out_weight], width)
    slice2, _ = own_slice([mlp_in_weight], width)
    slice3, _ = own_slice([mlp_out_weight], width)
    slice4, _ = own_slice([proj_in_weight], inner // planes)
    slice5, _ = own_slice([proj_mid_weight], inner)
    slice6, _ = own_slice([proj_out_weight], goal_width)
    w1, x, seg_own = bring(
        [slice1],
        [[qkv_weight, attn_out_weight]],
        [block_input, segment_ids.reshape(rows, -1, LANES)],
        0,
    )
    x = x.reshape(tokens, width)
    seg_own = seg_own.reshape(tokens)
    mod_row = lax.dynamic_index_in_dim(modulation, lax.axis_index("seq"), 0, keepdims=False)
    mod = jnp.pad(mod_row, ((0, 16 - mod_row.shape[0]), (0, 0)))
    hot = (seg_own[:, None] == jnp.arange(16, dtype=jnp.int32)[None, :]).astype(BF)
    hott = (seg_own[None, :] == jnp.arange(16, dtype=jnp.int32)[:, None]).astype(BF)
    seg_column = seg_own[:, None]
    vector = lambda bias: bias.astype(F32)[None, :]

    per = qkv_weight.shape[0]
    bias_float = query_value_bias.astype(F32)
    full_bias = jnp.concatenate(
        [bias_float[:width], jnp.zeros((width,), F32), bias_float[width:]]
    )
    by_rows = lambda weight: weight.reshape(planes, -1, weight.shape[1])
    qkv, mod1t, attended, totals, w2, w3, goals = project(
        x, hot, mod, w1, full_bias[None, :], seg_column, heads,
        [slice2, slice3], [[mlp_in_weight], [by_rows(mlp_out_weight)]], targets, 3,
    )
    goals = goals.reshape(tokens, goal_width)
    parts = ((qkv, 0), (qkv, 1), (qkv, 2))
    branch, mid, low2, mod2t, attt = merge(attended, x, hot, mod, w1, vector(attn_out_bias))
    w3 = w3.reshape(hidden, width)
    actt, slope, out_low, outt, mlp_branch, w4, w5, w6 = feed(
        low2, w2, vector(mlp_in_bias), w3, vector(mlp_out_bias), mid, hot, mod,
        [slice4, slice5, slice6],
        [[proj_in_weight], [by_rows(proj_mid_weight)], [by_rows(proj_out_weight)]],
        5,
    )
    w5, w6 = w5.reshape(inner, inner), w6.reshape(inner, goal_width)
    act1t, act2t, gfeat, gh2, gh1, gout, block_out = align(
        out_low, w4, vector(proj_in_bias), w5, vector(proj_mid_bias), w6, vector(proj_out_bias),
        goals, 7,
    )
    half = functools.partial(weight_half, where, seq=seq, planes=planes)
    other6, column6 = half(act2t, tie(gfeat, gout), by_columns=False)
    got6 = swap_cores(other6)
    other5, column5 = half(act1t, tie(gh2, other6), by_columns=True)
    got5 = swap_cores(other5)
    other4, column4 = half(outt, tie(gh1, other5), by_columns=True)
    got4 = swap_cores(other4)
    (own6,) = half(act2t, tie(gfeat, other4), by_columns=False, got=got6)
    (own5,) = half(act1t, tie(gh2, own6), by_columns=True, got=got5)
    (own4,) = half(outt, tie(gh1, own5), by_columns=True, got=got4)
    plane6 = scatter_planes(own6)
    plane5 = scatter_planes(own5)
    plane4 = scatter_planes(own4)
    gmlp, ghmid, gmod2, ggate2 = feed_back(
        tie(gout, own4), mlp_branch, hot, hott, mod, w3, slope, w2
    )
    other3, column3 = half(actt, tie(gmlp, gmod2), by_columns=False)
    got3 = swap_cores(other3)
    other2, column2 = half(mod2t, tie(ghmid, other3), by_columns=True)
    got2 = swap_cores(other2)
    (own3,) = half(actt, tie(gmlp, other2), by_columns=False, got=got3)
    plane3 = scatter_planes(own3)
    gmid, gbranch, gatt, gshift2, gscale2, ggate1 = merge_back(
        gout, tie(gmod2, own3), mid, branch, hot, hott, mod, w1
    )
    half1 = functools.partial(weight_half, where, seq=seq, planes=1)
    other0, column0 = half1(attt, tie(gbranch, gatt), by_columns=True)
    got0 = swap_cores(other0)
    (own2,) = half(mod2t, tie(ghmid, other0), by_columns=True, got=got2)
    plane2 = scatter_planes(own2)
    (own0,) = half1(attt, tie(gbranch, own2), by_columns=True, got=got0)
    gqkv, sum6, sum4, sum5, own_attn = attend_backward(
        parts, seg_column, seg_column, totals, attended, tie(gatt, own0), heads,
        [plane6, plane4, plane5, own0[0]], 4,
    )
    other1, column1 = half(mod1t, tie(gqkv, other0), by_columns=True)
    got1 = swap_cores(other1)
    gin, gshift1, gscale1, sum3 = project_back(
        tie(gqkv, other1), x, gmid, hot, hott, mod, w1, [plane3], 6
    )
    (own1,) = half(mod1t, tie(gqkv, gin), by_columns=True, got=got1)
    plane1 = scatter_planes(own1)

    segs = modulation.shape[1]
    grad_mod = jnp.concatenate(
        [gshift1, gscale1, ggate1, gshift2, gscale2, ggate2], axis=1
    )[:segs].astype(BF)
    grad_mod = jnp.pad(grad_mod.reshape(-1, LANES), ((0, 8), (0, 0)))
    grad_mod = jnp.broadcast_to(grad_mod[None], (rows,) + grad_mod.shape)
    columns1 = column1[0]
    biases = [
        jnp.concatenate([columns1[:width], columns1[2 * width : 3 * width]]),
        column0[0], column2[0], column3[0], column4[0], column5[0], column6[0],
    ]
    packed = jnp.concatenate([bias.reshape(seq, -1) for bias in biases], axis=1)
    count = -(-packed.shape[1] // (8 * LANES)) * 8 * LANES
    packed = jnp.pad(packed, ((0, 0), (0, count - packed.shape[1]))).reshape(seq, -1, LANES)
    sum2, full6, full5, full4, full3, full0, grad_input = settle(
        [plane2],
        [sum6, sum5, sum4, sum3, tie(own_attn, own1)],
        [gin.reshape(block_input.shape)],
        [False] * 4 + [True],
        1,
    )
    _, _, full2, full1, all_bias, all_mod = settle(
        [tie(plane1, sum2), packed], [sum2], [grad_mod], [False, False, True], 2, True
    )
    grad_input = grad_input.astype(F32)
    grad3, grad4, grad5, grad6 = unpack(
        (full3, None), (full4, inner), (full5, inner), (full6, None)
    )
    grad2, grad1 = unpack((full2, hidden), (full1, 3 * width))
    grad_modulation = all_mod[:, :-8].reshape(rows, segs, 6 * width).astype(F32)

    packed = (all_bias[0] + all_bias[1]).reshape(-1)
    shares = []
    start = 0
    for bias in biases:
        stop = start + bias.shape[0] // seq
        shares.append(packed[start:stop])
        start = stop

    return (
        block_out,
        grad_input,
        grad_modulation,
        grad1,
        shares[0],
        full0.reshape(per, width).astype(F32),
        shares[1],
        grad2,
        shares[2],
        grad3,
        shares[3],
        grad4,
        shares[4],
        grad5,
        shares[5],
        grad6,
        shares[6],
    )


def solution(mesh):
    copies, seq = mesh.shape["dp"], mesh.shape["seq"]
    grid = jax.sharding.Mesh(
        mesh.devices.reshape(copies // 2, 2, seq), ("plane", "core", "seq")
    )
    rows, weight = P(COPIES, "seq", None), P("seq", None)
    placed = (rows, P(COPIES, None, None), P(COPIES, "seq")) + (weight, P()) * 7 + (rows,)

    def step(*args):
        per_device = args[0].shape[0] // copies
        one_row = per_device == seq and copies // 2 == seq and args[0].shape[1] == 1024
        return jax.shard_map(
            local_row if one_row else local,
            mesh=grid,
            in_specs=placed,
            out_specs=(rows, rows, P(COPIES, None, None)) + (weight, P("seq")) * 7,
            check_vma=False,
        )(*args)

    return step
```

```python
import functools
import math

import jax
import jax.numpy as jnp
from jax import lax
from jax.experimental import pallas as pl
from jax.experimental.pallas import tpu as pltpu
from jax.sharding import PartitionSpec as P

HEAD_DIM = 72
EPSILON = 1e-06
GELU_COEF = 0.044715
MASKED = -1e30
LOG2E = 1.4426950408889634
LANES = 128
BF = jnp.bfloat16
F32 = jnp.float32


def dot_nn(left, right):
    return jnp.dot(left, right, preferred_element_type=F32)


def dot_tn(left, right):
    return lax.dot_general(left, right, (((0,), (0,)), ((), ())), preferred_element_type=F32)


def dot_nt(left, right):
    return lax.dot_general(left, right, (((1,), (1,)), ((), ())), preferred_element_type=F32)


def silu_grad(value):
    sigmoid_val = jax.nn.sigmoid(value)
    return sigmoid_val * (1.0 + value * (1.0 - sigmoid_val))


def gelu_grad(value):
    factor = math.sqrt(2.0 / math.pi)
    tangent = jnp.tanh(factor * (value + GELU_COEF * value * value * value))
    return 0.5 * (1.0 + tangent) + 0.5 * value * (1.0 - tangent * tangent) * factor * (
        1.0 + 3.0 * GELU_COEF * value * value
    )


def norm_stats(values):
    centred = values - jnp.mean(values, axis=-1, keepdims=True)
    inv_std = lax.rsqrt(jnp.mean(centred * centred, axis=-1, keepdims=True) + EPSILON)
    return (centred * inv_std, inv_std)


def norm_back(grad_normed, normed, inv_std):
    return inv_std * (
        grad_normed
        - jnp.mean(grad_normed, axis=-1, keepdims=True)
        - normed * jnp.mean(grad_normed * normed, axis=-1, keepdims=True)
    )


GATHER_AT = (7, 7, 7, 16, 17, 17, 11, 11, 11, 18, 18, 18, 14, 14, 14, 18, 18, 18)
SECOND_AT, THIRD_AT = 6, 15
FEED_AT = (1, 1, 4, 5, 5, 8, 7, 7, 8, 3, 3, 6, 7, 7, 8, 8, 8, 8, 5, 5, 7, 8, 8, 8, 8, 8, 8)
SETTLE_AT = (4, 7, 12, 15)


def head_window(head, width):
    tile = jnp.minimum((head * HEAD_DIM) // LANES, width // LANES - 2)
    base = pl.multiple_of(tile * LANES, LANES)
    offset = head * HEAD_DIM - base
    lane = lax.broadcasted_iota(jnp.int32, (1, 2 * LANES), 1)
    mine = (lane >= offset) & (lane < offset + HEAD_DIM)
    spare = jnp.where(offset >= 4, 0, LANES)
    return base, mine, lane - spare, offset >= 4


def with_segments(block, mine, lane, seg, hit, miss):
    code = jnp.where(lane == seg, hit, miss)
    code = jnp.where((lane >= 0) & (lane < 4), code, 0.0)
    return jnp.where(mine, block.astype(F32), code).astype(BF)


def attend_head(head, refs, seg_refs, out_ref, total_ref, block):
    (q_ref, qcol), (k_ref, kcol), (v_ref, vcol) = refs
    segq_ref, segk_ref = seg_refs
    base, mine, lane, low = head_window(head, out_ref.shape[1])
    window = lambda column: pl.ds(pl.multiple_of(base + column, LANES), 2 * LANES)
    factor = HEAD_DIM ** (-0.5) * LOG2E
    keys = with_segments(k_ref[:, window(kcol)], mine, lane, segk_ref[...], 0.0, 1.0)
    values = jnp.where(
        mine, v_ref[:, window(vcol)].astype(F32), jnp.where(lane == 0, 1.0, 0.0)
    ).astype(BF)
    values_t = values.T
    for start in range(0, out_ref.shape[0], block):
        rows = pl.ds(start, block)
        query = with_segments(
            q_ref[rows, window(qcol)], mine, lane, segq_ref[rows, :], MASKED, 0.0
        )
        scores = dot_nt(keys, query) * factor
        top = jnp.max(scores, axis=0, keepdims=True)
        weights = jnp.exp2(scores - top).astype(BF)
        gathered = dot_nn(values_t, weights)
        total = jnp.where(low, gathered[0:1], gathered[LANES : LANES + 1])
        result = (gathered * (1.0 / total)).T
        out_ref[rows, window(0)] = jnp.where(
            mine, result, out_ref[rows, window(0)].astype(F32)
        ).astype(BF)
        total_ref[pl.ds(head, 1), rows] = top + jnp.log2(total)


def attend_forward_kernel(q_ref, k_ref, v_ref, segq_ref, segk_ref, out_ref, total_ref, *, block):
    parts = ((q_ref, 0), (k_ref, 0), (v_ref, 0))
    attend_head(pl.program_id(0), parts, (segq_ref, segk_ref), out_ref, total_ref, block)


def whole(shape):
    return pl.BlockSpec(shape, lambda *_: (0,) * len(shape))


def attend_forward(parts, seg_query, seg_keys, heads):
    (query, qcol), (keys, kcol), (values, vcol) = parts
    count, tokens = seg_query.shape[0], seg_keys.shape[0]
    width = heads * HEAD_DIM
    return pl.pallas_call(
        functools.partial(attend_forward_kernel, block=min(256, count)),
        grid=(heads,),
        in_specs=[
            pl.BlockSpec((count, width), lambda h: (0, qcol)),
            pl.BlockSpec((tokens, width), lambda h: (0, kcol)),
            pl.BlockSpec((tokens, width), lambda h: (0, vcol)),
            whole((count, 1)),
            whole((tokens, 1)),
        ],
        out_specs=[whole((count, width)), whole((heads, count))],
        out_shape=[
            jax.ShapeDtypeStruct((count, width), BF),
            jax.ShapeDtypeStruct((heads, count), F32),
        ],
        compiler_params=pltpu.CompilerParams(vmem_limit_bytes=56 * 1024 * 1024),
        cost_estimate=pl.CostEstimate(
            flops=heads * count * tokens * 4 * 256,
            bytes_accessed=2 * width * (2 * count + 2 * tokens),
            transcendentals=heads * count * tokens,
        ),
        name="attend_forward",
    )(query, keys, values, seg_query, seg_keys)


def attend_backward_kernel(
    q_ref, k_ref, v_ref, segq_ref, segk_ref, total_ref, out_ref, grad_ref, *rest, block, columns,
    carried=0
):
    work = None
    if carried:
        rest = list(rest)
        take = lambda number: [rest.pop(0) for _ in range(number)]
        sums = take(carried)
        grads = take(1)
        targets = take(carried)
        dots = rest.pop(0)
        work = Sum(sums, targets, rest)
        head = pl.program_id(0)

        @pl.when(head == 0)
        def _():
            work.link.greet()
            work.start()

        for k in range(carried):
            pl.when(head == SETTLE_AT[k])(functools.partial(work.add, k))
    else:
        grads, dots = rest[:-1], rest[-1]
    dq_ref, dk_ref, dv_ref = grads if len(grads) == 3 else grads * 3
    head = pl.program_id(0)
    width = q_ref.shape[1]
    count = q_ref.shape[0]
    factor = HEAD_DIM ** (-0.5) * LOG2E

    @pl.when(head == 0)
    def _():
        if len(grads) == 1:
            spare = pl.ds(3 * width, dq_ref.shape[1] - 3 * width)
            dq_ref[:, spare] = jnp.zeros((count, dq_ref.shape[1] - 3 * width), BF)
        row = lax.broadcasted_iota(jnp.int32, dots.shape[:1] + (width,), 0)
        col = lax.broadcasted_iota(jnp.int32, dots.shape[:1] + (width,), 1)
        pick = ((col >= row * HEAD_DIM) & (col < (row + 1) * HEAD_DIM)).astype(F32).astype(BF)
        for start in range(0, count, block):
            rows = pl.ds(start, block)
            product = out_ref[rows, :].astype(F32) * grad_ref[rows, :].astype(F32)
            high = product.astype(BF)
            rest_part = (product - high.astype(F32)).astype(BF)
            dots[:, rows] = dot_nt(pick, high) + dot_nt(pick, rest_part)

    base, mine, lane, _ = head_window(head, width)
    window = pl.ds(base, 2 * LANES)
    keys = with_segments(k_ref[:, window], mine, lane, segk_ref[...], 0.0, 1.0)
    keys_t = keys.T
    values = v_ref[:, window]
    grad_keys = None
    for start in range(0, count, block):
        rows = pl.ds(start, block)
        query = with_segments(q_ref[rows, window], mine, lane, segq_ref[rows, :], MASKED, 0.0)
        grad = jnp.where(mine, grad_ref[rows, window].astype(F32), 0.0).astype(BF)
        scores = dot_nt(keys, query) * factor
        probs = jnp.exp2(scores - total_ref[pl.ds(head, 1), rows])
        grad_probs = dot_nt(values, grad)
        grad_scores = (probs * (grad_probs - dots[pl.ds(head, 1), rows])).astype(BF)
        part_v = dot_nn(probs.astype(BF), grad)
        part_k = dot_nn(grad_scores, query)
        if grad_keys is None:
            grad_keys, grad_values = part_k, part_v
        else:
            grad_keys, grad_values = grad_keys + part_k, grad_values + part_v
        grad_query = (dot_nn(keys_t, grad_scores) * HEAD_DIM ** (-0.5)).T
        put(dq_ref, rows, base + columns[0], mine, grad_query)
    every = pl.ds(0, k_ref.shape[0])
    put(dk_ref, every, base + columns[1], mine, grad_keys * HEAD_DIM ** (-0.5))
    put(dv_ref, every, base + columns[2], mine, grad_values)
    if work is not None:
        pl.when(head == pl.num_programs(0) - 1)(work.finish)


def put(ref, rows, base, mine, value):
    window = pl.ds(pl.multiple_of(base, LANES), 2 * LANES)
    ref[rows, window] = jnp.where(mine, value, ref[rows, window].astype(F32)).astype(BF)


def attend_backward(
    parts, seg_query, seg_keys, totals, out, grad, heads, sums=(), collective=None
):
    (query, qcol), (keys, kcol), (values, vcol) = parts
    count, tokens = seg_query.shape[0], seg_keys.shape[0]
    width = heads * HEAD_DIM
    if count == tokens:
        shapes = [(count, -(-3 * width // (4 * LANES)) * 4 * LANES)]
        columns = (0, width, 2 * width)
    else:
        shapes = [(count, width), (tokens, width), (tokens, width)]
        columns = (0, 0, 0)
    return pl.pallas_call(
        functools.partial(
            attend_backward_kernel, block=min(256, count), columns=columns, carried=len(sums)
        ),
        grid=(heads,),
        in_specs=[
            pl.BlockSpec((count, width), lambda h: (0, qcol)),
            pl.BlockSpec((tokens, width), lambda h: (0, kcol)),
            pl.BlockSpec((tokens, width), lambda h: (0, vcol)),
            whole((count, 1)),
            whole((tokens, 1)),
            whole((heads, count)),
            whole((count, width)),
            whole((count, width)),
        ]
        + [ANY] * len(sums),
        out_specs=[whole(shape) for shape in shapes] + [ANY] * len(sums),
        out_shape=[jax.ShapeDtypeStruct(shape, BF) for shape in shapes]
        + [summed(total) for total in sums],
        scratch_shapes=[pltpu.VMEM((heads, count), F32)]
        + (Sum.scratch(sums) if sums else []),
        compiler_params=pltpu.CompilerParams(
            vmem_limit_bytes=60 * 1024 * 1024,
            collective_id=collective,
            has_side_effects=bool(sums),
        ),
        cost_estimate=pl.CostEstimate(
            flops=heads * count * tokens * 10 * 256,
            bytes_accessed=2 * width * (4 * count + 4 * tokens),
            transcendentals=heads * count * tokens,
        ),
        name="attend_backward",
    )(query, keys, values, seg_query, seg_keys, totals, out, grad, *sums)


class Rows:
    def __init__(self, seq, rows):
        self.seq, self.rows = seq, rows
        self.share = seq // rows
        here = lax.axis_index("seq")
        self.row, self.part = here // self.share, here % self.share

    def device(self, row, part):
        return (row % self.rows) * self.share + part % self.share

    def shift_rows(self, shift):
        return [
            (self.device(r, p), self.device(r + shift, p))
            for r in range(self.rows)
            for p in range(self.share)
        ]

    def shift_parts(self, shift):
        return [
            (self.device(r, p), self.device(r, p + shift))
            for r in range(self.rows)
            for p in range(self.share)
        ]

    def to_rows(self, array):
        pieces = []
        for shift in range(self.rows):
            piece = lax.dynamic_index_in_dim(
                array, (self.row + shift) % self.rows, 0, keepdims=False
            )
            if shift:
                piece = lax.ppermute(piece, "seq", self.shift_rows(shift))
            pieces.append(piece)
        return pieces

    def to_spans(self, pieces):
        result = jnp.zeros((self.rows,) + pieces[0].shape, pieces[0].dtype)
        for shift, piece in enumerate(pieces):
            if shift:
                piece = lax.ppermute(piece, "seq", self.shift_rows(-shift))
            result = lax.dynamic_update_index_in_dim(
                result, piece, (self.row + shift) % self.rows, 0
            )
        return result

    def gather_parts(self, array):
        return jnp.concatenate(
            [array]
            + [
                lax.ppermute(array, "seq", self.shift_parts(shift))
                for shift in range(1, self.share)
            ],
            axis=0,
        )

    def sum_parts(self, array):
        count = array.shape[0] // self.share
        total = array[:count].astype(F32)
        for shift in range(1, self.share):
            piece = array[shift * count : (shift + 1) * count]
            total = total + lax.ppermute(piece, "seq", self.shift_parts(-shift)).astype(F32)
        return total.astype(array.dtype)

    def all_parts(self, array):
        total = array
        for shift in range(1, self.share):
            total = total + lax.ppermute(array, "seq", self.shift_parts(shift))
        return total


COPIES = ("plane", "core")
EVERY = ("seq", "plane", "core")


def own_slice(weights, cut):
    copies = lax.axis_size(COPIES)
    here = lax.axis_index(COPIES)
    blocks = [weight.shape[1] // cut for weight in weights]
    per = weights[0].shape[0]
    count = per * sum(blocks) // copies
    piece, row = here * count // per, here * count % per
    own = None
    first = 0
    for weight, number in zip(weights, blocks):
        column = jnp.clip(piece - first, 0, number - 1) * cut
        part = lax.dynamic_slice(weight, (row, column), (count, cut))
        own = part if own is None else jnp.where(piece >= first, part, own)
        first += number
    return own, (lax.axis_size("seq"), sum(blocks) * per, cut)


def gather_slices(slices, after=None):
    own, shape = slices
    if after is not None:
        own, _ = lax.optimization_barrier((own, after))
    return lax.all_gather(own, EVERY, axis=0, tiled=True).reshape(shape)


def reduce_bundle(bundle):
    seq, count, columns = bundle.shape
    planes = lax.axis_size("plane")
    core = lax.axis_index("core")
    parts = bundle.reshape(seq, planes, 2, count // planes // 2, columns)
    keep = lax.dynamic_index_in_dim(parts, core, 2, keepdims=False).swapaxes(0, 1)
    send = lax.dynamic_index_in_dim(parts, 1 - core, 2, keepdims=False).swapaxes(0, 1)
    got = lax.ppermute(send, "core", [(0, 1), (1, 0)])
    both = (keep.astype(F32) + got.astype(F32)).astype(BF)
    mine = lax.psum_scatter(both, "plane", scatter_dimension=0, tiled=True)[0]
    own = lax.psum_scatter(mine, "seq", scatter_dimension=0, tiled=True)[0]
    return lax.all_gather(own, COPIES, axis=0, tiled=True)


def split_rows(full, count):
    return [
        full[:, start : start + count].reshape(-1, full.shape[2])
        for start in range(0, full.shape[1], count)
    ]


MIB = 1024 * 1024


def spec(shape, index, once=False):
    if once:
        return pl.BlockSpec(shape, index, pipeline_mode=pl.Buffered(1))
    return pl.BlockSpec(shape, index)


def fixed(shape):
    return spec(shape, lambda *_: (0,) * len(shape), once=True)


def call(
    kernel, grid, inputs, outputs, args, name, flops, scratch=(), scalars=None, collective=None
):
    moved = sum(math.prod(arg.shape) * arg.dtype.itemsize for arg in args)
    moved += sum(math.prod(shape) * jnp.dtype(kind).itemsize for shape, kind, _ in outputs)
    grid_spec = pltpu.PrefetchScalarGridSpec(
        num_scalar_prefetch=0 if scalars is None else 1,
        grid=grid,
        in_specs=inputs,
        out_specs=[block for _, _, block in outputs],
        scratch_shapes=list(scratch),
    )
    given = args if scalars is None else [scalars] + list(args)
    return pl.pallas_call(
        kernel,
        grid_spec=grid_spec,
        out_shape=[jax.ShapeDtypeStruct(shape, kind) for shape, kind, _ in outputs],
        compiler_params=pltpu.CompilerParams(
            vmem_limit_bytes=60 * MIB,
            collective_id=collective,
            has_side_effects=collective is not None,
        ),
        cost_estimate=pl.CostEstimate(flops=flops, bytes_accessed=moved, transcendentals=0),
        name=name,
    )(*given)


def square(block):
    return block.reshape(-1, block.shape[-1])


def chunks(count, size=256):
    return [pl.ds(start, min(size, count)) for start in range(0, count, min(size, count))]


def carry(refs, bundles):
    refs = list(refs)
    take = lambda count: [refs.pop(0) for _ in range(count)]
    return take, [take(count) for count in bundles]


def project_kernel(
    x_ref, hot_ref, shift_ref, scale_ref, w_ref, bias_ref, seg_ref, *refs, block, bundles
):
    take, given = carry(refs, bundles)
    (goal_in,) = take(1)
    qkv_ref, modt_ref, out_ref, total_ref = take(4)
    targets = take(len(bundles))
    (goal_out,) = take(1)
    (low_ref,) = take(1)
    gather = Gather(given, targets, take(Gather.room(len(bundles))))
    tokens = Rounds([goal_in], [goal_out], take(2))
    head = pl.program_id(0)
    width = x_ref.shape[1]
    steps = gather.steps()

    def point(number):
        if number == SECOND_AT:
            gather.issue(1)
        if number == THIRD_AT:
            tokens.start()
        for step, when in zip(steps, GATHER_AT):
            if when == number:
                step()

    @pl.when(head == 0)
    def _():
        gather.link.greet()
        gather.start()
        for rows in chunks(x_ref.shape[0]):
            normed, _ = norm_stats(x_ref[rows, :].astype(F32))
            hot = hot_ref[rows, :]
            low = normed * (1.0 + dot_nn(hot, scale_ref[...])) + dot_nn(hot, shift_ref[...])
            low_ref[rows, :] = low.astype(BF)
            modt_ref[:, rows] = low.astype(BF).T
        point(0)
        for j in range(3):
            columns = pl.ds(j * width, width)
            weight = square(w_ref[:, j])
            for rows in chunks(x_ref.shape[0]):
                qkv_ref[rows, columns] = (
                    dot_nn(low_ref[rows, :], weight) + bias_ref[:, columns]
                ).astype(BF)
            point(j + 1)

    for number in range(4, max(GATHER_AT) + 1):
        if number in GATHER_AT + (SECOND_AT, THIRD_AT):
            pl.when(head == number - 3)(functools.partial(point, number))
    parts = ((qkv_ref, 0), (qkv_ref, width), (qkv_ref, 2 * width))
    attend_head(head, parts, (seg_ref, seg_ref), out_ref, total_ref, block)

    @pl.when(head == pl.num_programs(0) - 1)
    def _():
        gather.finish()
        tokens.finish()


def project(x, hot, mod, weights, bias, seg, heads, cuts, shards, goals, collective):
    tokens, width = x.shape
    seq, _, per, _ = weights.shape
    part = lambda index: spec((mod.shape[0], width), lambda h: (0, index), once=True)
    flat = [array for shard in shards for array in shard]
    return call(
        functools.partial(
            project_kernel, block=min(256, tokens), bundles=[len(shard) for shard in shards]
        ),
        (heads,),
        [
            fixed((tokens, width)),
            fixed(hot.shape),
            part(0),
            part(1),
            spec((seq, 3, per, width), lambda h: (0, 0, 0, 0), once=True),
            fixed((1, 3 * width)),
            fixed(seg.shape),
        ]
        + [ANY] * (len(flat) + 1),
        [
            ((tokens, 3 * width), BF, fixed((tokens, 3 * width))),
            ((width, tokens), BF, fixed((width, tokens))),
            ((tokens, width), BF, fixed((tokens, width))),
            ((heads, tokens), F32, fixed((heads, tokens))),
        ]
        + [(shape.shape, BF, ANY) for shape in gathered(cuts, shards)]
        + [(goals.shape, BF, ANY)],
        [x, hot, mod, mod, weights, bias, seg] + flat + [goals],
        "project",
        6 * tokens * width * width + heads * tokens * tokens * 4 * 256,
        [pltpu.VMEM((tokens, width), BF)]
        + Gather.scratch(gathered(cuts, shards))
        + Rounds.scratch(1),
        collective=collective,
    )


def merge_kernel(
    out_ref, x_ref, hot_ref, gate_ref, shift_ref, scale_ref, w_ref, bias_ref,
    branch_ref, mid_ref, low_ref, lowt_ref, outt_ref,
):
    hot = hot_ref[...]
    branch = dot_nn(out_ref[...], square(w_ref[...])) + bias_ref[...]
    middle = x_ref[...].astype(F32) + dot_nn(hot, gate_ref[...]) * branch
    normed, _ = norm_stats(middle)
    low = normed * (1.0 + dot_nn(hot, scale_ref[...])) + dot_nn(hot, shift_ref[...])
    low = low.astype(BF)
    branch_ref[...] = branch.astype(BF)
    mid_ref[...] = middle
    low_ref[...] = low
    lowt_ref[...] = low.T
    outt_ref[...] = out_ref[...].T


def merge(attended, x, hot, mod, weights, bias):
    tokens, width = x.shape
    seq, _, per, _ = weights.shape
    size = min(256, tokens)
    part = lambda index: spec((mod.shape[0], width), lambda i: (0, index), once=True)
    rows = spec((size, width), lambda i: (i, 0))
    turned = spec((width, size), lambda i: (0, i))
    return call(
        merge_kernel,
        (tokens // size,),
        [
            rows,
            rows,
            spec((size, hot.shape[1]), lambda i: (i, 0)),
            part(2),
            part(3),
            part(4),
            spec((seq, 1, per, width), lambda i: (0, 3, 0, 0), once=True),
            fixed((1, width)),
        ],
        [
            ((tokens, width), BF, rows),
            ((tokens, width), F32, rows),
            ((tokens, width), BF, rows),
            ((width, tokens), BF, turned),
            ((width, tokens), BF, turned),
        ],
        [attended, x, hot, mod, mod, mod, weights, bias],
        "merge",
        2 * tokens * width * width,
    )


def gelu_pair(value):
    factor = math.sqrt(2.0 / math.pi)
    squared = value * value
    tangent = jnp.tanh(factor * value * (1.0 + GELU_COEF * squared))
    half = 0.5 * (1.0 + tangent)
    slope = half + (0.5 * factor) * value * (1.0 - tangent * tangent) * (
        1.0 + 3.0 * GELU_COEF * squared
    )
    return value * half, slope


def feed_kernel(
    low_ref, w_in_ref, b_in_ref, w_out_ref, b_out_ref, mid_ref, hot_ref, gate_ref, *refs, bundles
):
    take, given = carry(refs, bundles)
    actt_ref, slope_ref, res_ref, rest_ref, branch_ref = take(5)
    targets = take(len(bundles))
    (total,) = take(1)
    gather = Gather(given, targets, take(Gather.room(len(bundles))), eager=True)
    steps = gather.steps()
    blocks = targets[0].shape[1]
    step = pl.program_id(0)

    @pl.when(step == 0)
    def _():
        gather.link.greet()
        gather.start()
        total[...] = jnp.zeros_like(total)

    w_in, w_out = square(w_in_ref[...]), w_out_ref[...]
    pieces = chunks(low_ref.shape[0])
    for number, rows in enumerate(pieces):
        if number % 2 == 0:
            for index, action in enumerate(steps):
                if FEED_AT[index] % 2 == number // 2:
                    pl.when(step == FEED_AT[index] // 2)(action)
        hmid = dot_nn(low_ref[rows, :], w_in) + b_in_ref[...]
        act, slope = gelu_pair(hmid)
        act = act.astype(BF)
        slope_ref[rows, :] = slope.astype(BF)
        actt_ref[:, rows] = act.T
        total[rows, :] += dot_nn(act, w_out)

    @pl.when(step == pl.num_programs(0) - 1)
    def _():
        for rows in pieces:
            branch = total[rows, :] + b_out_ref[...]
            result = mid_ref[rows, :] + dot_nn(hot_ref[rows, :], gate_ref[...]) * branch
            result = result.astype(BF)
            res_ref[rows, :] = result
            rest_ref[:, rows] = result.T
            branch_ref[rows, :] = branch.astype(BF)
        for index, action in enumerate(steps):
            if FEED_AT[index] == 2 * blocks:
                action()
        gather.finish()


def feed(low, w_in, b_in, w_out, b_out, mid, hot, mod, cuts, shards, collective):
    tokens, width = low.shape
    seq, blocks, per, cut = w_in.shape
    hidden = blocks * cut
    flat = [array for shard in shards for array in shard]
    return call(
        functools.partial(feed_kernel, bundles=[len(shard) for shard in shards]),
        (blocks,),
        [
            fixed((tokens, width)),
            spec((seq, 1, per, cut), lambda j: (0, j, 0, 0)),
            spec((1, cut), lambda j: (0, j)),
            spec((cut, width), lambda j: (j, 0)),
            fixed((1, width)),
            fixed((tokens, width)),
            fixed(hot.shape),
            spec((mod.shape[0], width), lambda j: (0, 5), once=True),
        ]
        + [ANY] * len(flat),
        [
            ((hidden, tokens), BF, spec((cut, tokens), lambda j: (j, 0))),
            ((tokens, hidden), BF, spec((tokens, cut), lambda j: (0, j))),
            ((tokens, width), BF, fixed((tokens, width))),
            ((width, tokens), BF, fixed((width, tokens))),
            ((tokens, width), BF, fixed((tokens, width))),
        ]
        + [(shape.shape, BF, ANY) for shape in gathered(cuts, shards)],
        [low, w_in, b_in, w_out, b_out, mid, hot, mod] + flat,
        "feed",
        4 * tokens * width * hidden,
        [pltpu.VMEM((tokens, width), F32)] + Gather.scratch(gathered(cuts, shards)),
        collective=collective,
    )


def silu_pair(value):
    gate = jax.nn.sigmoid(value)
    return value * gate, gate * (1.0 + value * (1.0 - gate))


def align_kernel(
    res_ref, w_in_ref, b_in_ref, w_mid_ref, b_mid_ref, w_out_ref, b_out_ref, goal_ref, rows_ref,
    act1t_ref, act2t_ref, gfeat_ref, gh2_ref, gh1_ref, gout_ref, back_ref, act1_ref, slope1_ref,
    *sems,
):
    tokens = Rounds([rows_ref], [back_ref], sems)

    @pl.when(pl.program_id(0) == 0)
    def _():
        tokens.link.greet()
        tokens.start()

    blocks, cut = w_in_ref.shape[1], w_in_ref.shape[3]
    res = res_ref[...]
    for j in range(blocks):
        columns = pl.ds(j * cut, cut)
        hidden1 = dot_nn(res, square(w_in_ref[:, j])) + b_in_ref[:, columns]
        act, slope = silu_pair(hidden1)
        act1_ref[:, columns] = act.astype(BF)
        slope1_ref[:, columns] = slope
    act1 = act1_ref[...]
    act1t_ref[...] = act1.T
    hidden2 = dot_nn(act1, w_mid_ref[...]) + b_mid_ref[...]
    act2, slope2 = silu_pair(hidden2)
    act2 = act2.astype(BF)
    act2t_ref[...] = act2.T
    feats = dot_nn(act2, w_out_ref[...]) + b_out_ref[...]
    goals = goal_ref[...].astype(F32)
    inv_feat = lax.rsqrt(jnp.sum(feats * feats, axis=-1, keepdims=True) + EPSILON)
    feat_unit = feats * inv_feat
    goal_unit = goals * lax.rsqrt(jnp.sum(goals * goals, axis=-1, keepdims=True) + EPSILON)
    cosine = jnp.sum(feat_unit * goal_unit, axis=-1, keepdims=True)
    weight = -0.5 * feats.shape[1]
    gfeat = (weight * inv_feat * (goal_unit - cosine * feat_unit)).astype(BF)
    gfeat_ref[...] = gfeat
    gh2 = (dot_nt(gfeat, w_out_ref[...]) * slope2).astype(BF)
    gh2_ref[...] = gh2
    gh1 = (dot_nt(gh2, w_mid_ref[...]) * slope1_ref[...]).astype(BF)
    gh1_ref[...] = gh1
    total = None
    for j in range(blocks):
        part = dot_nt(gh1_ref[:, pl.ds(j * cut, cut)], square(w_in_ref[:, j]))
        total = part if total is None else total + part
    gout_ref[...] = total
    pl.when(pl.program_id(0) == pl.num_programs(0) - 1)(tokens.finish)


def align(res, w_in, b_in, w_mid, b_mid, w_out, b_out, goals, collective):
    tokens, width = res.shape
    inner, goal_width = w_out.shape
    size = min(256, tokens)
    rows = lambda n: spec((size, n), lambda i: (i, 0))
    turned = lambda n: spec((n, size), lambda i: (0, i))
    return call(
        align_kernel,
        (tokens // size,),
        [
            rows(width),
            fixed(w_in.shape),
            fixed((1, inner)),
            fixed(w_mid.shape),
            fixed((1, inner)),
            fixed(w_out.shape),
            fixed((1, goal_width)),
            rows(goal_width),
            ANY,
        ],
        [
            ((inner, tokens), BF, turned(inner)),
            ((inner, tokens), BF, turned(inner)),
            ((tokens, goal_width), BF, rows(goal_width)),
            ((tokens, inner), BF, rows(inner)),
            ((tokens, inner), BF, rows(inner)),
            ((tokens, width), F32, rows(width)),
            ((SEQ, tokens // SEQ, width), BF, ANY),
        ],
        [res, w_in, b_in, w_mid, b_mid, w_out, b_out, goals, res.reshape(SEQ, -1, width)],
        "align",
        4 * tokens * inner * (width + inner + goal_width),
        [pltpu.VMEM((size, inner), BF), pltpu.VMEM((size, inner), F32)] + Rounds.scratch(1),
        collective=collective,
    )


def feed_back_kernel(
    gout_ref, branch_ref, hot_ref, hott_ref, gate_ref, w_out_ref, slope_ref, w_in_ref,
    gmlp_ref, ghmid_ref, gmod_ref, ggate_ref,
):
    step = pl.program_id(0)

    @pl.when(step == 0)
    def _():
        sums = None
        for rows in chunks(gout_ref.shape[0]):
            gout = gout_ref[rows, :]
            gmlp_ref[rows, :] = (gout * dot_nn(hot_ref[rows, :], gate_ref[...])).astype(BF)
            part = dot_nn(hott_ref[:, rows], (gout * branch_ref[rows, :].astype(F32)).astype(BF))
            sums = part if sums is None else sums + part
        ggate_ref[...] = sums
        gmod_ref[...] = jnp.zeros_like(gmod_ref)

    w_out, w_in = w_out_ref[...], square(w_in_ref[...])
    for rows in chunks(gout_ref.shape[0]):
        ghmid = (dot_nt(gmlp_ref[rows, :], w_out) * slope_ref[rows, :].astype(F32)).astype(BF)
        ghmid_ref[rows, :] = ghmid
        gmod_ref[rows, :] += dot_nt(ghmid, w_in)


def feed_back(gout, branch, hot, hott, mod, w_out, slope, w_in):
    tokens, width = gout.shape
    seq, blocks, per, cut = w_in.shape
    hidden = blocks * cut
    return call(
        feed_back_kernel,
        (blocks,),
        [
            fixed((tokens, width)),
            fixed((tokens, width)),
            fixed(hot.shape),
            fixed(hott.shape),
            spec((mod.shape[0], width), lambda j: (0, 5), once=True),
            spec((cut, width), lambda j: (j, 0)),
            spec((tokens, cut), lambda j: (0, j)),
            spec((seq, 1, per, cut), lambda j: (0, j, 0, 0)),
        ],
        [
            ((tokens, width), BF, fixed((tokens, width))),
            ((tokens, hidden), BF, spec((tokens, cut), lambda j: (0, j))),
            ((tokens, width), F32, fixed((tokens, width))),
            ((hott.shape[0], width), F32, fixed((hott.shape[0], width))),
        ],
        [gout, branch, hot, hott, mod, w_out, slope, w_in],
        "feed_back",
        4 * tokens * width * hidden,
    )


def add_rows(ref, value):
    @pl.when(pl.program_id(0) == 0)
    def _():
        ref[...] = value

    @pl.when(pl.program_id(0) > 0)
    def _():
        ref[...] += value


def merge_back_kernel(
    gout_ref, gmod_ref, mid_ref, branch_ref, hot_ref, hott_ref, gate_ref, scale_ref, w_ref,
    gmid_ref, gbranch_ref, gatt_ref, gshift_ref, gscale_ref, ggate_ref,
):
    hot, hott = hot_ref[...], hott_ref[...]
    gmod = gmod_ref[...]
    normed, inv_std = norm_stats(mid_ref[...])
    gmid = gout_ref[...] + norm_back(
        gmod * (1.0 + dot_nn(hot, scale_ref[...])), normed, inv_std
    )
    gmid_ref[...] = gmid
    gbranch = (gmid * dot_nn(hot, gate_ref[...])).astype(BF)
    gbranch_ref[...] = gbranch
    gatt_ref[...] = dot_nt(gbranch, square(w_ref[...])).astype(BF)
    add_rows(gshift_ref, dot_nn(hott, gmod.astype(BF)))
    add_rows(gscale_ref, dot_nn(hott, (gmod * normed).astype(BF)))
    add_rows(ggate_ref, dot_nn(hott, (gmid * branch_ref[...].astype(F32)).astype(BF)))


def merge_back(gout, gmod, mid, branch, hot, hott, mod, weights):
    tokens, width = gout.shape
    seq, _, per, _ = weights.shape
    size = min(256, tokens)
    part = lambda index: spec((mod.shape[0], width), lambda i: (0, index), once=True)
    rows = spec((size, width), lambda i: (i, 0))
    sums = ((hott.shape[0], width), F32, fixed((hott.shape[0], width)))
    return call(
        merge_back_kernel,
        (tokens // size,),
        [
            rows,
            rows,
            rows,
            rows,
            spec((size, hot.shape[1]), lambda i: (i, 0)),
            spec((hott.shape[0], size), lambda i: (0, i)),
            part(2),
            part(4),
            spec((seq, 1, per, width), lambda i: (0, 3, 0, 0), once=True),
        ],
        [
            ((tokens, width), F32, rows),
            ((tokens, width), BF, rows),
            ((tokens, width), BF, rows),
            sums,
            sums,
            sums,
        ],
        [gout, gmod, mid, branch, hot, hott, mod, mod, weights],
        "merge_back",
        2 * tokens * width * width,
    )


def project_back_kernel(
    gqkv_ref, x_ref, gmid_ref, hot_ref, hott_ref, scale_ref, w_ref, *refs, carried
):
    refs = list(refs)
    take = lambda number: [refs.pop(0) for _ in range(number)]
    sums = take(carried)
    gin_ref, gshift_ref, gscale_ref = take(3)
    work = Sum(sums, take(carried), refs)

    @pl.when(pl.program_id(0) == 0)
    def _():
        work.link.greet()
        work.start()

    width = x_ref.shape[1]
    hott = hott_ref[...]
    gmod = None
    for j in range(3):
        part = dot_nt(gqkv_ref[:, pl.ds(j * width, width)], square(w_ref[:, j]))
        gmod = part if gmod is None else gmod + part
    normed, inv_std = norm_stats(x_ref[...].astype(F32))
    gin = gmid_ref[...] + norm_back(
        gmod * (1.0 + dot_nn(hot_ref[...], scale_ref[...])), normed, inv_std
    )
    gin_ref[...] = gin.astype(BF)
    add_rows(gshift_ref, dot_nn(hott, gmod.astype(BF)))
    add_rows(gscale_ref, dot_nn(hott, (gmod * normed).astype(BF)))

    @pl.when(pl.program_id(0) == pl.num_programs(0) - 1)
    def _():
        for k in range(carried):
            work.add(k)
        work.finish()


def project_back(gqkv, x, gmid, hot, hott, mod, weights, carried, collective):
    tokens, width = x.shape
    seq, _, per, _ = weights.shape
    size = min(256, tokens)
    rows = spec((size, width), lambda i: (i, 0))
    sums = ((hott.shape[0], width), F32, fixed((hott.shape[0], width)))
    return call(
        functools.partial(project_back_kernel, carried=len(carried)),
        (tokens // size,),
        [
            spec((size, 3 * width), lambda i: (i, 0)),
            rows,
            rows,
            spec((size, hot.shape[1]), lambda i: (i, 0)),
            spec((hott.shape[0], size), lambda i: (0, i)),
            spec((mod.shape[0], width), lambda i: (0, 1), once=True),
            spec((seq, 3, per, width), lambda i: (0, 0, 0, 0), once=True),
        ]
        + [ANY] * len(carried),
        [((tokens, width), BF, rows), sums, sums]
        + [(total.shape[1:], total.dtype, ANY) for total in carried],
        [gqkv, x, gmid, hot, hott, mod, weights] + list(carried),
        "project_back",
        6 * tokens * width * width,
        Sum.scratch(carried),
        collective=collective,
    )


def weight_kernel(where_ref, left_ref, right_ref, *refs, first):
    left = left_ref[...].reshape(-1, left_ref.shape[-1])
    got_ref = None if first else refs[0]
    out_ref = refs[0] if first else refs[1]
    result = dot_nn(left, right_ref[...]).reshape(out_ref.shape)
    if first:
        ones = jnp.ones((16, right_ref.shape[0]), BF)
        refs[1][...] = dot_nn(ones, right_ref[...])
    else:
        result = result + got_ref[...].astype(F32)
    out_ref[...] = result.astype(BF)


def weight_half(where, turned, right, seq, planes, by_columns, got=None):
    count, tokens = turned.shape
    columns = right.shape[1]
    first = got is None
    half = (lambda w: 1 - w[0]) if first else (lambda w: w[0])
    if by_columns:
        per, cut = count // seq // 2, columns // planes
        left = turned.reshape(seq, 2, per, tokens)
        left_spec = spec((seq, 1, per, tokens), lambda j, w: (0, half(w), 0, 0))
        right_spec = spec((tokens, cut), lambda j, w: (0, j))
        sum_spec = spec((16, cut), lambda j, w: (0, j))
    else:
        per, cut = count // seq // planes // 2, columns
        left = turned.reshape(seq, planes, 2, per, tokens)
        left_spec = spec((seq, 1, 1, per, tokens), lambda j, w: (0, j, half(w), 0, 0))
        right_spec = spec((tokens, cut), lambda j, w: (0, 0))
        sum_spec = spec((16, cut), lambda j, w: (0, 0))
    block = spec((1, seq, per, cut), lambda j, w: (j, 0, 0, 0))
    outputs = [((planes, seq, per, cut), BF, block)]
    inputs, args = [left_spec, right_spec], [left, right]
    if first:
        outputs.append(((16, columns), F32, sum_spec))
    else:
        inputs.append(block)
        args.append(got)
    return call(
        functools.partial(weight_kernel, first=first),
        (planes,),
        inputs,
        outputs,
        args,
        "weight_other" if first else "weight_own",
        count * tokens * columns,
        scalars=where,
    )


ANY = pl.BlockSpec(memory_space=pl.ANY)
SEQ, PLANES = 4, 4


class Link:
    def __init__(self):
        self.z, self.p, self.c = (lax.axis_index(name) for name in ("seq", "plane", "core"))

    def ahead(self, shift):
        return lax.rem(self.z + shift, SEQ)

    def behind(self, shift):
        return lax.rem(self.z + SEQ - shift, SEQ)

    def across(self, bit):
        low = lax.rem(self.p, 2)
        high = self.p // 2
        low = 1 - low if bit % 2 else low
        high = 1 - high if bit // 2 else high
        return high * 2 + low

    def copy(self, source, target, sems, axis, index):
        return pltpu.make_async_remote_copy(
            src_ref=source,
            dst_ref=target,
            send_sem=sems[0],
            recv_sem=sems[1],
            device_id={axis: index},
            device_id_type=pl.DeviceIdType.MESH,
        )

    def greet(self):
        barrier = pltpu.get_barrier_semaphore()
        for step in range(1, SEQ):
            signal = functools.partial(
                pl.semaphore_signal, barrier, inc=1, device_id_type=pl.DeviceIdType.MESH
            )
            signal(device_id={"seq": self.ahead(step)})
            signal(device_id={"plane": self.across(step)})
        pl.semaphore_signal(
            barrier, inc=1, device_id={"core": 1 - self.c}, device_id_type=pl.DeviceIdType.MESH
        )
        pl.semaphore_wait(barrier, 2 * SEQ - 1)


class Gather:
    def __init__(self, shards, targets, sems, eager=False, after=None):
        self.link = Link()
        self.shards, self.targets = shards, targets
        self.eager, self.after = eager, after
        self.z_sems, self.p_sems, self.c_sems, self.local_sems, self.out_sems = sems[:5]
        self.bufs = sems[5:]

    @staticmethod
    def scratch(targets):
        dma = pltpu.SemaphoreType.DMA
        count = len(targets)
        return [
            dma((2, count, 3)),
            dma((2, count, 3, 6)),
            dma((2, count, 3)),
            dma((count, 4)),
            dma((count,)),
        ] + [pltpu.VMEM(target.shape[1:], BF) for target in targets]

    @staticmethod
    def room(count):
        return 5 + count

    def rows(self, target):
        half = target.shape[2] // 2
        return pl.ds(pl.multiple_of(self.link.c * half, half), half)

    def locals(self, k):
        target = self.targets[k]
        width = target.shape[3]
        block = 0
        for array in self.shards[k]:
            if len(array.shape) == 3:
                parts = [array.at[index] for index in range(array.shape[0])]
            else:
                parts = [
                    array.at[:, pl.ds(start, width)] for start in range(0, array.shape[1], width)
                ]
            for part in parts:
                yield pltpu.make_async_copy(
                    part, self.bufs[k].at[block], self.local_sems.at[k, block]
                )
                block += 1

    def stored(self, k):
        return pltpu.make_async_copy(
            self.bufs[k], self.targets[k].at[self.link.z], self.out_sems.at[k]
        )

    def along(self, k, shift, incoming):
        link, target = self.link, self.targets[k]
        place = link.behind(shift) if incoming else link.z
        return link.copy(
            self.bufs[k].at[link.p, self.rows(target), :],
            target.at[place, link.p, self.rows(target), :],
            (self.z_sems.at[0, k, shift - 1], self.z_sems.at[1, k, shift - 1]),
            "seq",
            link.ahead(shift),
        )

    def across(self, k, shift, index, incoming):
        link, target = self.link, self.targets[k]
        half = target.shape[2] // 2
        first = -(-half // 32) * 16
        start, size = ((0, first), (first, half - first))[index % 2]
        peer = (1, 1, 2, 2, 2, 1)[index]
        plane = link.p
        if incoming:
            plane = link.across(3 if index >= 4 else peer)
        elif index >= 4:
            plane = link.across(3 - peer)
        rows = pl.ds(pl.multiple_of(link.c * half + start, 16), size)
        place = target.at[link.behind(shift), plane, rows, :]
        return link.copy(
            place,
            place,
            (self.p_sems.at[0, k, shift - 1, index], self.p_sems.at[1, k, shift - 1, index]),
            "plane",
            link.across(peer),
        )

    def beside(self, k, shift, incoming):
        link, target = self.link, self.targets[k]
        half = target.shape[2] // 2
        core = 1 - link.c if incoming else link.c
        rows = pl.ds(pl.multiple_of(core * half, half), half)
        place = target.at[link.behind(shift), :, rows, :]
        return link.copy(
            place,
            place,
            (self.c_sems.at[0, k, shift - 1], self.c_sems.at[1, k, shift - 1]),
            "core",
            1 - link.c,
        )

    def start(self):
        count = range(len(self.targets))
        for k in count:
            for copy in self.locals(k):
                copy.start()
        for k in count:
            for copy in self.locals(k):
                copy.wait()
            if k == 0:
                self.issue(0)
            self.stored(k).start()

    def issue(self, k):
        if k < len(self.targets):
            for shift in (1, 3) if self.eager else (1, 3, 2):
                self.along(k, shift, False).start()

    def steps(self):
        return [
            functools.partial(stage, k, shift)
            for stage in (self.spread, self.relay, self.pair)
            for k in range(len(self.targets))
            for shift in (1, 3, 2)
        ]

    def spread(self, k, shift):
        self.along(k, shift, True).wait_recv()
        if self.eager and shift == 1:
            self.along(k, 2, False).start()
        if self.eager and shift == 3:
            self.issue(k + 1)
        if shift == 1 and self.after is not None:
            self.after()
        for index in (0, 3, 1, 2):
            self.across(k, shift, index, False).start()

    def relay(self, k, shift):
        self.across(k, shift, 0, True).wait_recv()
        self.across(k, shift, 4, False).start()
        self.across(k, shift, 3, True).wait_recv()
        self.across(k, shift, 5, False).start()

    def pair(self, k, shift):
        for index in (1, 2, 4, 5):
            self.across(k, shift, index, True).wait_recv()
        self.beside(k, shift, False).start()

    def finish(self):
        for k in range(len(self.targets)):
            for shift in range(1, SEQ):
                self.beside(k, shift, True).wait_recv()
                self.along(k, shift, False).wait_send()
                self.beside(k, shift, False).wait_send()
                for index in range(6):
                    self.across(k, shift, index, False).wait_send()
            self.stored(k).wait()


class Rounds:
    def __init__(self, sources, targets, sems):
        self.link = Link()
        self.sources, self.targets, self.sems, self.local_sems = sources, targets, *sems

    @staticmethod
    def scratch(count):
        dma = pltpu.SemaphoreType.DMA
        return [dma((2, count, 3)), dma((count,))]

    def along(self, k, shift, incoming):
        link = self.link
        return link.copy(
            self.sources[k].at[link.ahead(shift)],
            self.targets[k].at[link.behind(shift) if incoming else link.z],
            (self.sems.at[0, k, shift - 1], self.sems.at[1, k, shift - 1]),
            "seq",
            link.ahead(shift),
        )

    def local(self, k):
        z = self.link.z
        return pltpu.make_async_copy(
            self.sources[k].at[z], self.targets[k].at[z], self.local_sems.at[k]
        )

    def start(self):
        for k in range(len(self.targets)):
            for shift in (2, 1, 3):
                self.along(k, shift, False).start()
            self.local(k).start()

    def finish(self):
        for k in range(len(self.targets)):
            for shift in range(1, SEQ):
                self.along(k, shift, True).wait_recv()
                self.along(k, shift, False).wait_send()
            self.local(k).wait()


class Sum:
    def __init__(self, sources, results, refs):
        self.link = Link()
        self.sources, self.results = sources, results
        self.bufs = refs[: len(sources)]
        self.sems, self.local_sems = refs[len(sources) :]

    @staticmethod
    def scratch(sources):
        dma = pltpu.SemaphoreType.DMA
        bufs = [pltpu.VMEM((5,) + source.shape[1:], source.dtype) for source in sources]
        return bufs + [dma((2, len(sources), 3)), dma((len(sources), 2))]

    def along(self, k, shift):
        link = self.link
        return link.copy(
            self.sources[k].at[link.ahead(shift)],
            self.bufs[k].at[shift - 1],
            (self.sems.at[0, k, shift - 1], self.sems.at[1, k, shift - 1]),
            "seq",
            link.ahead(shift),
        )

    def mine(self, k):
        return pltpu.make_async_copy(
            self.sources[k].at[self.link.z], self.bufs[k].at[3], self.local_sems.at[k, 0]
        )

    def stored(self, k):
        return pltpu.make_async_copy(
            self.bufs[k].at[4], self.results[k], self.local_sems.at[k, 1]
        )

    def start(self):
        for k in range(len(self.sources)):
            for shift in (2, 1, 3):
                self.along(k, shift).start()
            self.mine(k).start()

    def add(self, k):
        for shift in range(1, SEQ):
            self.along(k, shift).wait_recv()
        self.mine(k).wait()
        buf = self.bufs[k]
        total = buf[0].astype(F32) + buf[1].astype(F32) + buf[2].astype(F32) + buf[3].astype(F32)
        buf[4] = total.astype(buf.dtype)
        self.stored(k).start()

    def finish(self):
        for k in range(len(self.sources)):
            for shift in range(1, SEQ):
                self.along(k, shift).wait_send()
            self.stored(k).wait()


class Share:
    def __init__(self, sources, targets, refs):
        self.link = Link()
        self.sources, self.targets = sources, targets
        self.bufs = refs[: len(sources)]
        self.p_sems, self.c_sems, self.local_sems = refs[len(sources) :]

    @staticmethod
    def scratch(sources, shared):
        dma = pltpu.SemaphoreType.DMA
        count = len(sources)
        bufs = [
            pltpu.VMEM((5 if one else 1,) + source.shape[-2:], source.dtype)
            for source, one in zip(sources, shared)
        ]
        return bufs + [dma((2, count, 3)), dma((2, count, 4)), dma((count, 2))]

    def shared(self, k):
        return len(self.targets[k].shape) == 3

    def loaded(self, k):
        return pltpu.make_async_copy(self.sources[k], self.bufs[k].at[0], self.local_sems.at[k, 0])

    def across(self, k, bit, incoming):
        link = self.link
        plane = link.across(bit)
        if self.shared(k):
            target = self.bufs[k].at[bit]
        else:
            target = self.targets[k].at[plane if incoming else link.p, link.c]
        return link.copy(
            self.bufs[k].at[0],
            target,
            (self.p_sems.at[0, k, bit - 1], self.p_sems.at[1, k, bit - 1]),
            "plane",
            plane,
        )

    def beside(self, k, bit, incoming):
        link = self.link
        core = 1 - link.c if incoming else link.c
        if self.shared(k):
            source, target = self.bufs[k].at[4], self.targets[k].at[core]
        else:
            plane = link.across(bit)
            target = self.targets[k].at[plane, core]
            source = self.bufs[k].at[0] if bit == 0 else self.targets[k].at[plane, link.c]
        return link.copy(
            source,
            target,
            (self.c_sems.at[0, k, bit], self.c_sems.at[1, k, bit]),
            "core",
            1 - link.c,
        )

    def own(self, k):
        link = self.link
        if self.shared(k):
            source, target = self.bufs[k].at[4], self.targets[k].at[link.c]
        else:
            source, target = self.bufs[k].at[0], self.targets[k].at[link.p, link.c]
        return pltpu.make_async_copy(source, target, self.local_sems.at[k, 1])

    def send(self, k):
        for bit in range(1, PLANES):
            self.across(k, bit, False).start()
        if not self.shared(k):
            self.own(k).start()
            self.beside(k, 0, False).start()

    def pass_on(self, k):
        for bit in range(1, PLANES):
            self.across(k, bit, True).wait_recv()
            if not self.shared(k):
                self.beside(k, bit, False).start()
        if self.shared(k):
            buf = self.bufs[k]
            total = buf[0].astype(F32) + buf[1].astype(F32) + buf[2].astype(F32) + buf[3].astype(F32)
            buf[4] = total.astype(buf.dtype)
            self.own(k).start()
            self.beside(k, 0, False).start()

    def finish(self):
        for k in range(len(self.targets)):
            for bit in range(1 if self.shared(k) else PLANES):
                self.beside(k, bit, True).wait_recv()
                self.beside(k, bit, False).wait_send()
            for bit in range(1, PLANES):
                self.across(k, bit, False).wait_send()
            self.own(k).wait()


def bring_kernel(*refs, bundles, rounds):
    refs = list(refs)
    take = lambda count: [refs.pop(0) for _ in range(count)]
    shards = [take(count) for count in bundles]
    sources = take(rounds)
    targets = take(len(bundles))
    arrived = take(rounds)
    gather_refs = take(Gather.room(len(bundles)))
    tokens = Rounds(sources, arrived, take(2))
    gather = Gather(shards, targets, gather_refs, after=tokens.start)
    gather.link.greet()
    gather.start()
    for step in gather.steps():
        step()
    tokens.finish()
    gather.finish()


def gathered(cuts, shards):
    shapes = []
    for cut, shard in zip(cuts, shards):
        if shard[0].ndim == 3:
            blocks, per = shard[0].shape[:2]
        else:
            blocks, per = sum(array.shape[1] for array in shard) // cut, shard[0].shape[0]
        shapes.append(jax.ShapeDtypeStruct((SEQ, blocks, per, cut), BF))
    return shapes


def bring(cuts, shards, sources, collective):
    flat = [array for shard in shards for array in shard]
    shapes = gathered(cuts, shards) + [jax.ShapeDtypeStruct(array.shape, array.dtype) for array in sources]
    args = flat + list(sources)
    return pl.pallas_call(
        functools.partial(
            bring_kernel, bundles=[len(shard) for shard in shards], rounds=len(sources)
        ),
        in_specs=[ANY] * len(args),
        out_specs=[ANY] * len(shapes),
        out_shape=shapes,
        scratch_shapes=Gather.scratch(gathered(cuts, shards)) + Rounds.scratch(len(sources)),
        compiler_params=pltpu.CompilerParams(
            collective_id=collective, has_side_effects=True, vmem_limit_bytes=60 * MIB
        ),
        cost_estimate=pl.CostEstimate(flops=0, bytes_accessed=300_000_000, transcendentals=0),
        name="bring",
    )(*args)


def settle_kernel(*refs, sums, shares, rounds, through):
    refs = list(refs)
    take = lambda number: [refs.pop(0) for _ in range(number)]
    sum_in, share_in, round_in = take(sums), take(shares), take(rounds)
    sum_out, share_out, round_out = take(sums), take(shares + sums * through), take(rounds)
    add = Sum(sum_in, sum_out, take(sums + 2))
    share = Share(share_in + sum_in * through, share_out, take(len(share_out) + 3))
    tokens = Rounds(round_in, round_out, take(2)) if rounds else None
    add.link.greet()
    add.start()
    if rounds:
        tokens.start()
    for k in range(shares):
        share.loaded(k).start()
    for k in range(shares):
        share.loaded(k).wait()
        share.send(k)
    for k in range(shares):
        share.pass_on(k)
    for k in range(sums):
        add.add(k)
        if through:
            share.bufs[shares + k][0] = add.bufs[k][4]
            share.send(shares + k)
    if through:
        for k in range(sums):
            share.pass_on(shares + k)
    add.finish()
    share.finish()
    if rounds:
        tokens.finish()


def summed(array):
    return jax.ShapeDtypeStruct(array.shape[1:], array.dtype)


def shared_out(array, shared):
    return jax.ShapeDtypeStruct(
        ((2,) if shared else (PLANES, 2)) + array.shape[-2:], array.dtype
    )


def settle(sums, shares, rounds, shared, collective, through=False):
    args = list(sums) + list(shares) + list(rounds)
    given = list(shares) + (list(sums) if through else [])
    shapes = (
        [summed(array) for array in sums]
        + [shared_out(array, one) for array, one in zip(given, shared)]
        + [jax.ShapeDtypeStruct(array.shape, array.dtype) for array in rounds]
    )
    return pl.pallas_call(
        functools.partial(
            settle_kernel,
            sums=len(sums),
            shares=len(shares),
            rounds=len(rounds),
            through=int(through),
        ),
        in_specs=[ANY] * len(args),
        out_specs=[ANY] * len(shapes),
        out_shape=shapes,
        scratch_shapes=Sum.scratch(sums)
        + Share.scratch(given, shared)
        + (Rounds.scratch(len(rounds)) if rounds else []),
        compiler_params=pltpu.CompilerParams(
            collective_id=collective, has_side_effects=True, vmem_limit_bytes=60 * MIB
        ),
        cost_estimate=pl.CostEstimate(flops=0, bytes_accessed=200_000_000, transcendentals=0),
        name="settle",
    )(*args)


def local(
    block_input,
    modulation,
    segment_ids,
    qkv_weight,
    query_value_bias,
    attn_out_weight,
    attn_out_bias,
    mlp_in_weight,
    mlp_in_bias,
    mlp_out_weight,
    mlp_out_bias,
    proj_in_weight,
    proj_in_bias,
    proj_mid_weight,
    proj_mid_bias,
    proj_out_weight,
    proj_out_bias,
    targets,
):
    rows, span, width = block_input.shape
    segs = modulation.shape[1]
    seq = lax.axis_size("seq")
    place = Rows(seq, rows)
    heads = width // HEAD_DIM
    hidden = mlp_in_weight.shape[1]
    inner = proj_mid_weight.shape[1]
    goal_width = targets.shape[2]
    tokens = rows * span
    share = place.share

    x_in = jnp.concatenate(place.to_rows(block_input), axis=0)
    seg_pieces = place.to_rows(segment_ids)
    segs_own = jnp.concatenate(seg_pieces, axis=0)
    seg_query = segs_own[:, None]
    seg_keys = place.gather_parts(seg_query) if share > 1 else seg_query
    goals = jnp.concatenate(place.to_rows(targets), axis=0)
    mod_row = lax.dynamic_index_in_dim(modulation, place.row, 0, keepdims=False)

    per = qkv_weight.shape[0]
    half = inner // 2
    first = gather_slices(own_slice([qkv_weight, attn_out_weight], width))
    second = gather_slices(own_slice([mlp_in_weight], width), first)
    third = gather_slices(own_slice([mlp_out_weight], width), second)
    fourth = gather_slices(own_slice([proj_in_weight], half), third)
    fifth = gather_slices(own_slice([proj_mid_weight], inner), fourth)
    sixth = gather_slices(own_slice([proj_out_weight], goal_width), fifth)
    w_q, w_k, w_v, w_attn = split_rows(first, per)
    w_qkv = jnp.concatenate([w_q, w_k, w_v], axis=1)
    w_mlp_in = jnp.concatenate(split_rows(second, per), axis=1)
    w_mlp_out = third.reshape(hidden, width)
    w_proj_in = jnp.concatenate(split_rows(fourth, per), axis=1)
    w_proj_mid = fifth.reshape(inner, inner)
    w_proj_out = sixth.reshape(inner, goal_width)

    one_hot = (segs_own[:, None] == jnp.arange(segs, dtype=jnp.int32)[None, :]).astype(BF)
    inputs = x_in.astype(F32)
    mod_tok = dot_nn(one_hot, mod_row)
    shift1, scale1, gate1, shift2, scale2, gate2 = (
        mod_tok[:, part * width : (part + 1) * width] for part in range(6)
    )
    normed1, inv_std1 = norm_stats(inputs)
    modulated1 = (normed1 * (1.0 + scale1) + shift1).astype(BF)
    bias_float = query_value_bias.astype(F32)
    full_bias = jnp.concatenate(
        [bias_float[:width], jnp.zeros((width,), F32), bias_float[width:]]
    )
    qkv = (dot_nn(modulated1, w_qkv) + full_bias).astype(BF)
    if share > 1:
        kv_all = place.gather_parts(qkv[:, width:])
        parts = ((qkv, 0), (kv_all, 0), (kv_all, 1))
    else:
        parts = ((qkv, 0), (qkv, 1), (qkv, 2))
    attended, totals = attend_forward(parts, seg_query, seg_keys, heads)
    branch = dot_nn(attended, w_attn) + attn_out_bias.astype(F32)
    middle = inputs + gate1 * branch
    normed2, inv_std2 = norm_stats(middle)
    modulated2 = (normed2 * (1.0 + scale2) + shift2).astype(BF)
    hmid = dot_nn(modulated2, w_mlp_in) + mlp_in_bias.astype(F32)
    act_mid = jax.nn.gelu(hmid, approximate=True).astype(BF)
    mlp_branch = dot_nn(act_mid, w_mlp_out) + mlp_out_bias.astype(F32)
    out_low = (middle + gate2 * mlp_branch).astype(BF)
    hidden1 = dot_nn(out_low, w_proj_in) + proj_in_bias.astype(F32)
    act1 = jax.nn.silu(hidden1).astype(BF)
    hidden2 = dot_nn(act1, w_proj_mid) + proj_mid_bias.astype(F32)
    act2 = jax.nn.silu(hidden2).astype(BF)
    feats = dot_nn(act2, w_proj_out) + proj_out_bias.astype(F32)
    goals = goals.astype(F32)
    inv_feat = lax.rsqrt(jnp.sum(feats * feats, axis=-1, keepdims=True) + EPSILON)
    feat_unit = feats * inv_feat
    goal_unit = goals * lax.rsqrt(jnp.sum(goals * goals, axis=-1, keepdims=True) + EPSILON)
    cosine = jnp.sum(feat_unit * goal_unit, axis=-1, keepdims=True)
    loss_weight = 0.5 * goal_width
    grad_feats = (-loss_weight * inv_feat * (goal_unit - cosine * feat_unit)).astype(BF)

    def blocks(grad, cut):
        low = grad.astype(BF).reshape(seq, grad.shape[0] // seq, grad.shape[1])
        return [low[:, :, start : start + cut] for start in range(0, grad.shape[1], cut)]

    sixth_sum = reduce_bundle(
        jnp.concatenate(blocks(dot_tn(act2, grad_feats), goal_width), axis=1)
    )
    bias_out = jnp.sum(grad_feats.astype(F32), axis=0)
    grad_hidden2 = (dot_nt(grad_feats, w_proj_out) * silu_grad(hidden2)).astype(BF)
    fifth_sum = reduce_bundle(jnp.concatenate(blocks(dot_tn(act1, grad_hidden2), inner), axis=1))
    bias_mid = jnp.sum(grad_hidden2.astype(F32), axis=0)
    grad_hidden1 = (dot_nt(grad_hidden2, w_proj_mid) * silu_grad(hidden1)).astype(BF)
    fourth_sum = reduce_bundle(jnp.concatenate(blocks(dot_tn(out_low, grad_hidden1), half), axis=1))
    bias_in = jnp.sum(grad_hidden1.astype(F32), axis=0)
    grad_output = dot_nt(grad_hidden1, w_proj_in)
    grad_gate2 = grad_output * mlp_branch
    grad_mlp = (grad_output * gate2).astype(BF)
    third_sum = reduce_bundle(jnp.concatenate(blocks(dot_tn(act_mid, grad_mlp), width), axis=1))
    bias_ff_out = jnp.sum(grad_mlp.astype(F32), axis=0)
    grad_hmid = (dot_nt(grad_mlp, w_mlp_out) * gelu_grad(hmid)).astype(BF)
    second_sum = reduce_bundle(jnp.concatenate(blocks(dot_tn(modulated2, grad_hmid), width), axis=1))
    bias_ff_in = jnp.sum(grad_hmid.astype(F32), axis=0)
    grad_modulated2 = dot_nt(grad_hmid, w_mlp_in)
    grad_middle = grad_output + norm_back(grad_modulated2 * (1.0 + scale2), normed2, inv_std2)
    grad_gate1 = grad_middle * branch
    grad_branch = (grad_middle * gate1).astype(BF)
    grad_attn_w = dot_tn(attended, grad_branch)
    bias_attn = jnp.sum(grad_branch.astype(F32), axis=0)
    grad_attended = dot_nt(grad_branch, w_attn).astype(BF)
    grads = attend_backward(parts, seg_query, seg_keys, totals, attended, grad_attended, heads)
    if share > 1:
        grad_qkv = jnp.concatenate(
            [grads[0], place.sum_parts(grads[1]), place.sum_parts(grads[2])], axis=1
        )
    else:
        grad_qkv = grads[0][:, : 3 * width]
    first_sum = reduce_bundle(
        jnp.concatenate(
            blocks(dot_tn(modulated1, grad_qkv), width) + blocks(grad_attn_w, width), axis=1
        )
    )
    column_sums = jnp.sum(grad_qkv.astype(F32), axis=0)
    bias_qv = jnp.concatenate([column_sums[:width], column_sums[2 * width :]])
    grad_modulated1 = dot_nt(grad_qkv, w_qkv)
    grad_input = grad_middle + norm_back(grad_modulated1 * (1.0 + scale1), normed1, inv_std1)

    def by_segment(value):
        return dot_tn(one_hot, value.astype(BF))

    grad_mod = jnp.concatenate(
        [
            by_segment(grad_modulated1),
            by_segment(grad_modulated1 * normed1),
            by_segment(grad_gate1),
            by_segment(grad_modulated2),
            by_segment(grad_modulated2 * normed2),
            by_segment(grad_gate2),
        ],
        axis=-1,
    )
    grad_mod = place.all_parts(grad_mod)
    grad_modulation = lax.all_gather(grad_mod.astype(BF), "seq", axis=0)[:: share].astype(F32)

    def back(value):
        return place.to_spans(
            [value[shift * span : (shift + 1) * span] for shift in range(rows)]
        )

    block_out = back(out_low)
    grad_input = back(grad_input.astype(BF)).astype(F32)

    biases = [bias_qv, bias_attn, bias_ff_in, bias_ff_out, bias_in, bias_mid, bias_out]
    packed = jnp.concatenate([bias.reshape(seq, -1) for bias in biases], axis=1)
    packed = lax.psum(packed, EVERY)
    packed = lax.dynamic_index_in_dim(packed, lax.axis_index("seq"), 0, keepdims=False)
    shares = []
    start = 0
    for bias in biases:
        stop = start + bias.shape[0] // seq
        shares.append(packed[start:stop])
        start = stop

    def columns_of(total, count):
        return [total[start : start + count].astype(F32) for start in range(0, total.shape[0], count)]

    first_parts = columns_of(first_sum, per)
    return (
        block_out,
        grad_input,
        grad_modulation,
        jnp.concatenate(first_parts[:3], axis=1),
        shares[0],
        first_parts[3],
        shares[1],
        jnp.concatenate(columns_of(second_sum, per), axis=1),
        shares[2],
        third_sum.astype(F32),
        shares[3],
        jnp.concatenate(columns_of(fourth_sum, per), axis=1),
        shares[4],
        fifth_sum.astype(F32),
        shares[5],
        sixth_sum.astype(F32),
        shares[6],
    )


def tie(value, *others):
    return lax.optimization_barrier((value,) + others)[0]


def swap_cores(value):
    return lax.ppermute(value, "core", [(0, 1), (1, 0)])


def swap_planes(value, bit):
    return lax.ppermute(value, "plane", [(p, p ^ bit) for p in range(lax.axis_size("plane"))])


def scatter_planes(both, after=None):
    planes, seq, count, columns = both.shape
    flat = both.reshape(planes * seq * count, columns)
    if after is not None:
        flat = tie(flat, after)
    own = lax.psum_scatter(flat, "plane", scatter_dimension=0, tiled=True)
    return own.reshape(seq, count, columns)


def scatter_seq(both):
    seq, count, columns = both.shape
    return lax.psum_scatter(
        both.reshape(seq * count, columns), "seq", scatter_dimension=0, tiled=True
    )


def gather_copies(own):
    full = lax.all_gather(own, COPIES, axis=0, tiled=True)
    return full.reshape(lax.axis_size("plane"), 2, own.shape[0], own.shape[1])


def unpack_kernel(*refs):
    count = len(refs) // 2
    for full_ref, out_ref in zip(refs[:count], refs[count:]):
        out_ref[...] = square(full_ref[...]).astype(F32)


def unpack(*fulls):
    planes = fulls[0][0].shape[0]
    inputs, outputs = [], []
    for full, columns in fulls:
        _, _, count, cut = full.shape
        inputs.append(spec((1, 2, count, cut), lambda p: (p, 0, 0, 0)))
        if columns is None:
            outputs.append(
                ((planes * 2 * count, cut), F32, spec((2 * count, cut), lambda p: (p, 0)))
            )
        else:
            outputs.append(((2 * count, columns), F32, spec((2 * count, cut), lambda p: (0, p))))
    return call(
        unpack_kernel, (planes,), inputs, outputs, [full for full, _ in fulls], "unpack", 0
    )


def local_row(
    block_input, modulation, segment_ids,
    qkv_weight, query_value_bias,
    attn_out_weight, attn_out_bias,
    mlp_in_weight, mlp_in_bias,
    mlp_out_weight, mlp_out_bias,
    proj_in_weight, proj_in_bias,
    proj_mid_weight, proj_mid_bias,
    proj_out_weight, proj_out_bias,
    targets,
):
    rows, span, width = block_input.shape
    seq, planes = lax.axis_size("seq"), lax.axis_size("plane")
    heads = width // HEAD_DIM
    hidden = mlp_in_weight.shape[1]
    inner = proj_mid_weight.shape[1]
    goal_width = targets.shape[2]
    tokens = rows * span
    where = lax.axis_index("core").reshape(1).astype(jnp.int32)

    w1, x, seg_own = bring(
        [width],
        [[qkv_weight, attn_out_weight]],
        [block_input, segment_ids.reshape(rows, -1, LANES)],
        0,
    )
    x = x.reshape(tokens, width)
    seg_own = seg_own.reshape(tokens)
    mod_row = lax.dynamic_index_in_dim(modulation, lax.axis_index("seq"), 0, keepdims=False)
    mod = jnp.pad(mod_row, ((0, 16 - mod_row.shape[0]), (0, 0)))
    hot = (seg_own[:, None] == jnp.arange(16, dtype=jnp.int32)[None, :]).astype(BF)
    hott = (seg_own[None, :] == jnp.arange(16, dtype=jnp.int32)[:, None]).astype(BF)
    seg_column = seg_own[:, None]
    vector = lambda bias: bias.astype(F32)[None, :]

    per = qkv_weight.shape[0]
    bias_float = query_value_bias.astype(F32)
    full_bias = jnp.concatenate(
        [bias_float[:width], jnp.zeros((width,), F32), bias_float[width:]]
    )
    by_rows = lambda weight: weight.reshape(planes, -1, weight.shape[1])
    qkv, mod1t, attended, totals, w2, w3, goals = project(
        x, hot, mod, w1, full_bias[None, :], seg_column, heads,
        [width, width], [[mlp_in_weight], [by_rows(mlp_out_weight)]], targets, 3,
    )
    goals = goals.reshape(tokens, goal_width)
    parts = ((qkv, 0), (qkv, 1), (qkv, 2))
    branch, mid, low2, mod2t, attt = merge(attended, x, hot, mod, w1, vector(attn_out_bias))
    w3 = w3.reshape(hidden, width)
    actt, slope, out_low, outt, mlp_branch, w4, w5, w6 = feed(
        low2, w2, vector(mlp_in_bias), w3, vector(mlp_out_bias), mid, hot, mod,
        [inner // planes, inner, goal_width],
        [[proj_in_weight], [by_rows(proj_mid_weight)], [by_rows(proj_out_weight)]],
        5,
    )
    w5, w6 = w5.reshape(inner, inner), w6.reshape(inner, goal_width)
    act1t, act2t, gfeat, gh2, gh1, gout, block_out = align(
        out_low, w4, vector(proj_in_bias), w5, vector(proj_mid_bias), w6, vector(proj_out_bias),
        goals, 7,
    )
    half = functools.partial(weight_half, where, seq=seq, planes=planes)
    other6, column6 = half(act2t, tie(gfeat, gout), by_columns=False)
    got6 = swap_cores(other6)
    other5, column5 = half(act1t, tie(gh2, other6), by_columns=True)
    got5 = swap_cores(other5)
    other4, column4 = half(outt, tie(gh1, other5), by_columns=True)
    got4 = swap_cores(other4)
    (own6,) = half(act2t, tie(gfeat, other4), by_columns=False, got=got6)
    (own5,) = half(act1t, tie(gh2, own6), by_columns=True, got=got5)
    (own4,) = half(outt, tie(gh1, own5), by_columns=True, got=got4)
    plane6 = scatter_planes(own6)
    plane5 = scatter_planes(own5)
    plane4 = scatter_planes(own4)
    gmlp, ghmid, gmod2, ggate2 = feed_back(
        tie(gout, own4), mlp_branch, hot, hott, mod, w3, slope, w2
    )
    other3, column3 = half(actt, tie(gmlp, gmod2), by_columns=False)
    got3 = swap_cores(other3)
    other2, column2 = half(mod2t, tie(ghmid, other3), by_columns=True)
    got2 = swap_cores(other2)
    (own3,) = half(actt, tie(gmlp, other2), by_columns=False, got=got3)
    plane3 = scatter_planes(own3)
    gmid, gbranch, gatt, gshift2, gscale2, ggate1 = merge_back(
        gout, tie(gmod2, own3), mid, branch, hot, hott, mod, w1
    )
    half1 = functools.partial(weight_half, where, seq=seq, planes=1)
    other0, column0 = half1(attt, tie(gbranch, gatt), by_columns=True)
    got0 = swap_cores(other0)
    (own2,) = half(mod2t, tie(ghmid, other0), by_columns=True, got=got2)
    plane2 = scatter_planes(own2)
    (own0,) = half1(attt, tie(gbranch, own2), by_columns=True, got=got0)
    gqkv, sum6, sum4, sum5, own_attn = attend_backward(
        parts, seg_column, seg_column, totals, attended, tie(gatt, own0), heads,
        [plane6, plane4, plane5, own0[0]], 4,
    )
    other1, column1 = half(mod1t, tie(gqkv, other0), by_columns=True)
    got1 = swap_cores(other1)
    gin, gshift1, gscale1, sum3 = project_back(
        tie(gqkv, other1), x, gmid, hot, hott, mod, w1, [plane3], 6
    )
    (own1,) = half(mod1t, tie(gqkv, gin), by_columns=True, got=got1)
    plane1 = scatter_planes(own1)

    segs = modulation.shape[1]
    grad_mod = jnp.concatenate(
        [gshift1, gscale1, ggate1, gshift2, gscale2, ggate2], axis=1
    )[:segs].astype(BF)
    grad_mod = jnp.pad(grad_mod.reshape(-1, LANES), ((0, 8), (0, 0)))
    grad_mod = jnp.broadcast_to(grad_mod[None], (rows,) + grad_mod.shape)
    columns1 = column1[0]
    biases = [
        jnp.concatenate([columns1[:width], columns1[2 * width : 3 * width]]),
        column0[0], column2[0], column3[0], column4[0], column5[0], column6[0],
    ]
    packed = jnp.concatenate([bias.reshape(seq, -1) for bias in biases], axis=1)
    count = -(-packed.shape[1] // (8 * LANES)) * 8 * LANES
    packed = jnp.pad(packed, ((0, 0), (0, count - packed.shape[1]))).reshape(seq, -1, LANES)
    sum2, full6, full5, full4, full3, full0, grad_input = settle(
        [plane2],
        [sum6, sum5, sum4, sum3, tie(own_attn, own1)],
        [gin.reshape(block_input.shape)],
        [False] * 4 + [True],
        1,
    )
    _, _, full2, full1, all_bias, all_mod = settle(
        [tie(plane1, sum2), packed], [sum2], [grad_mod], [False, False, True], 2, True
    )
    grad_input = grad_input.astype(F32)
    grad3, grad4, grad5, grad6 = unpack(
        (full3, None), (full4, inner), (full5, inner), (full6, None)
    )
    grad2, grad1 = unpack((full2, hidden), (full1, 3 * width))
    grad_modulation = all_mod[:, :-8].reshape(rows, segs, 6 * width).astype(F32)

    packed = (all_bias[0] + all_bias[1]).reshape(-1)
    shares = []
    start = 0
    for bias in biases:
        stop = start + bias.shape[0] // seq
        shares.append(packed[start:stop])
        start = stop

    return (
        block_out,
        grad_input,
        grad_modulation,
        grad1,
        shares[0],
        full0.reshape(per, width).astype(F32),
        shares[1],
        grad2,
        shares[2],
        grad3,
        shares[3],
        grad4,
        shares[4],
        grad5,
        shares[5],
        grad6,
        shares[6],
    )


def solution(mesh):
    copies, seq = mesh.shape["dp"], mesh.shape["seq"]
    grid = jax.sharding.Mesh(
        mesh.devices.reshape(copies // 2, 2, seq), ("plane", "core", "seq")
    )
    rows, weight = P(COPIES, "seq", None), P("seq", None)
    placed = (rows, P(COPIES, None, None), P(COPIES, "seq")) + (weight, P()) * 7 + (rows,)

    def step(*args):
        per_device = args[0].shape[0] // copies
        one_row = per_device == seq and copies // 2 == seq and args[0].shape[1] == 1024
        return jax.shard_map(
            local_row if one_row else local,
            mesh=grid,
            in_specs=placed,
            out_specs=(rows, rows, P(COPIES, None, None)) + (weight, P("seq")) * 7,
            check_vma=False,
        )(*args)

    return step
```

```python
import functools
import math

import jax
import jax.numpy as jnp
from jax import lax
from jax.experimental import pallas as pl
from jax.experimental.pallas import tpu as pltpu
from jax.sharding import PartitionSpec as P

HEAD_DIM = 72
EPSILON = 1e-06
GELU_COEF = 0.044715
MASKED = -1e30
LOG2E = 1.4426950408889634
LANES = 128
BF = jnp.bfloat16
F32 = jnp.float32


def dot_nn(left, right):
    return jnp.dot(left, right, preferred_element_type=F32)


def dot_tn(left, right):
    return lax.dot_general(left, right, (((0,), (0,)), ((), ())), preferred_element_type=F32)


def dot_nt(left, right):
    return lax.dot_general(left, right, (((1,), (1,)), ((), ())), preferred_element_type=F32)


def silu_grad(value):
    sigmoid_val = jax.nn.sigmoid(value)
    return sigmoid_val * (1.0 + value * (1.0 - sigmoid_val))


def gelu_grad(value):
    factor = math.sqrt(2.0 / math.pi)
    tangent = jnp.tanh(factor * (value + GELU_COEF * value * value * value))
    return 0.5 * (1.0 + tangent) + 0.5 * value * (1.0 - tangent * tangent) * factor * (
        1.0 + 3.0 * GELU_COEF * value * value
    )


def norm_stats(values):
    centred = values - jnp.mean(values, axis=-1, keepdims=True)
    inv_std = lax.rsqrt(jnp.mean(centred * centred, axis=-1, keepdims=True) + EPSILON)
    return (centred * inv_std, inv_std)


def norm_back(grad_normed, normed, inv_std):
    return inv_std * (
        grad_normed
        - jnp.mean(grad_normed, axis=-1, keepdims=True)
        - normed * jnp.mean(grad_normed * normed, axis=-1, keepdims=True)
    )


GATHER_AT = (7, 7, 7, 16, 17, 17, 11, 11, 11, 18, 18, 18, 14, 14, 14, 18, 18, 18)
SECOND_AT, THIRD_AT = 6, 15
FEED_AT = (1, 1, 4, 5, 5, 8, 7, 7, 8, 3, 3, 6, 7, 7, 8, 8, 8, 8, 5, 5, 7, 8, 8, 8, 8, 8, 8)


def head_window(head, width):
    tile = jnp.minimum((head * HEAD_DIM) // LANES, width // LANES - 2)
    base = pl.multiple_of(tile * LANES, LANES)
    offset = head * HEAD_DIM - base
    lane = lax.broadcasted_iota(jnp.int32, (1, 2 * LANES), 1)
    mine = (lane >= offset) & (lane < offset + HEAD_DIM)
    spare = jnp.where(offset >= 4, 0, LANES)
    return base, mine, lane - spare, offset >= 4


def with_segments(block, mine, lane, seg, hit, miss):
    code = jnp.where(lane == seg, hit, miss)
    code = jnp.where((lane >= 0) & (lane < 4), code, 0.0)
    return jnp.where(mine, block.astype(F32), code).astype(BF)


def attend_head(head, refs, seg_refs, out_ref, total_ref, block):
    (q_ref, qcol), (k_ref, kcol), (v_ref, vcol) = refs
    segq_ref, segk_ref = seg_refs
    base, mine, lane, low = head_window(head, out_ref.shape[1])
    window = lambda column: pl.ds(pl.multiple_of(base + column, LANES), 2 * LANES)
    factor = HEAD_DIM ** (-0.5) * LOG2E
    keys = with_segments(k_ref[:, window(kcol)], mine, lane, segk_ref[...], 0.0, 1.0)
    values = jnp.where(
        mine, v_ref[:, window(vcol)].astype(F32), jnp.where(lane == 0, 1.0, 0.0)
    ).astype(BF)
    values_t = values.T
    for start in range(0, out_ref.shape[0], block):
        rows = pl.ds(start, block)
        query = with_segments(
            q_ref[rows, window(qcol)], mine, lane, segq_ref[rows, :], MASKED, 0.0
        )
        scores = dot_nt(keys, query) * factor
        top = jnp.max(scores, axis=0, keepdims=True)
        weights = jnp.exp2(scores - top).astype(BF)
        gathered = dot_nn(values_t, weights)
        total = jnp.where(low, gathered[0:1], gathered[LANES : LANES + 1])
        result = (gathered * (1.0 / total)).T
        out_ref[rows, window(0)] = jnp.where(
            mine, result, out_ref[rows, window(0)].astype(F32)
        ).astype(BF)
        total_ref[pl.ds(head, 1), rows] = top + jnp.log2(total)


def attend_forward_kernel(q_ref, k_ref, v_ref, segq_ref, segk_ref, out_ref, total_ref, *, block):
    parts = ((q_ref, 0), (k_ref, 0), (v_ref, 0))
    attend_head(pl.program_id(0), parts, (segq_ref, segk_ref), out_ref, total_ref, block)


def whole(shape):
    return pl.BlockSpec(shape, lambda *_: (0,) * len(shape))


def attend_forward(parts, seg_query, seg_keys, heads):
    (query, qcol), (keys, kcol), (values, vcol) = parts
    count, tokens = seg_query.shape[0], seg_keys.shape[0]
    width = heads * HEAD_DIM
    return pl.pallas_call(
        functools.partial(attend_forward_kernel, block=min(256, count)),
        grid=(heads,),
        in_specs=[
            pl.BlockSpec((count, width), lambda h: (0, qcol)),
            pl.BlockSpec((tokens, width), lambda h: (0, kcol)),
            pl.BlockSpec((tokens, width), lambda h: (0, vcol)),
            whole((count, 1)),
            whole((tokens, 1)),
        ],
        out_specs=[whole((count, width)), whole((heads, count))],
        out_shape=[
            jax.ShapeDtypeStruct((count, width), BF),
            jax.ShapeDtypeStruct((heads, count), F32),
        ],
        compiler_params=pltpu.CompilerParams(vmem_limit_bytes=56 * 1024 * 1024),
        cost_estimate=pl.CostEstimate(
            flops=heads * count * tokens * 4 * 256,
            bytes_accessed=2 * width * (2 * count + 2 * tokens),
            transcendentals=heads * count * tokens,
        ),
        name="attend_forward",
    )(query, keys, values, seg_query, seg_keys)


def attend_backward_kernel(
    q_ref, k_ref, v_ref, segq_ref, segk_ref, total_ref, out_ref, grad_ref, *rest, block, columns,
    carried=0
):
    work = None
    if carried:
        rest = list(rest)
        take = lambda number: [rest.pop(0) for _ in range(number)]
        sums = take(carried)
        grads = take(1)
        targets = take(carried)
        dots = rest.pop(0)
        work = Sum(sums, targets, rest)
        head = pl.program_id(0)

        @pl.when(head == 0)
        def _():
            work.link.greet()
            work.start()

    else:
        grads, dots = rest[:-1], rest[-1]
    dq_ref, dk_ref, dv_ref = grads if len(grads) == 3 else grads * 3
    head = pl.program_id(0)
    width = q_ref.shape[1]
    count = q_ref.shape[0]
    factor = HEAD_DIM ** (-0.5) * LOG2E

    @pl.when(head == 0)
    def _():
        if len(grads) == 1:
            spare = pl.ds(3 * width, dq_ref.shape[1] - 3 * width)
            dq_ref[:, spare] = jnp.zeros((count, dq_ref.shape[1] - 3 * width), BF)
        row = lax.broadcasted_iota(jnp.int32, dots.shape[:1] + (width,), 0)
        col = lax.broadcasted_iota(jnp.int32, dots.shape[:1] + (width,), 1)
        pick = ((col >= row * HEAD_DIM) & (col < (row + 1) * HEAD_DIM)).astype(F32).astype(BF)
        for start in range(0, count, block):
            rows = pl.ds(start, block)
            product = out_ref[rows, :].astype(F32) * grad_ref[rows, :].astype(F32)
            high = product.astype(BF)
            rest_part = (product - high.astype(F32)).astype(BF)
            dots[:, rows] = dot_nt(pick, high) + dot_nt(pick, rest_part)

    base, mine, lane, _ = head_window(head, width)
    window = pl.ds(base, 2 * LANES)
    keys = with_segments(k_ref[:, window], mine, lane, segk_ref[...], 0.0, 1.0)
    keys_t = keys.T
    values = v_ref[:, window]
    grad_keys = None
    for start in range(0, count, block):
        rows = pl.ds(start, block)
        query = with_segments(q_ref[rows, window], mine, lane, segq_ref[rows, :], MASKED, 0.0)
        grad = jnp.where(mine, grad_ref[rows, window].astype(F32), 0.0).astype(BF)
        scores = dot_nt(keys, query) * factor
        probs = jnp.exp2(scores - total_ref[pl.ds(head, 1), rows])
        grad_probs = dot_nt(values, grad)
        grad_scores = (probs * (grad_probs - dots[pl.ds(head, 1), rows])).astype(BF)
        part_v = dot_nn(probs.astype(BF), grad)
        part_k = dot_nn(grad_scores, query)
        if grad_keys is None:
            grad_keys, grad_values = part_k, part_v
        else:
            grad_keys, grad_values = grad_keys + part_k, grad_values + part_v
        grad_query = (dot_nn(keys_t, grad_scores) * HEAD_DIM ** (-0.5)).T
        put(dq_ref, rows, base + columns[0], mine, grad_query)
    every = pl.ds(0, k_ref.shape[0])
    put(dk_ref, every, base + columns[1], mine, grad_keys * HEAD_DIM ** (-0.5))
    put(dv_ref, every, base + columns[2], mine, grad_values)
    if work is not None:

        @pl.when(head == pl.num_programs(0) - 1)
        def _():
            for k in range(carried):
                work.add(k)
            work.finish()


def put(ref, rows, base, mine, value):
    window = pl.ds(pl.multiple_of(base, LANES), 2 * LANES)
    ref[rows, window] = jnp.where(mine, value, ref[rows, window].astype(F32)).astype(BF)


def attend_backward(
    parts, seg_query, seg_keys, totals, out, grad, heads, sums=(), collective=None
):
    (query, qcol), (keys, kcol), (values, vcol) = parts
    count, tokens = seg_query.shape[0], seg_keys.shape[0]
    width = heads * HEAD_DIM
    if count == tokens:
        shapes = [(count, -(-3 * width // (4 * LANES)) * 4 * LANES)]
        columns = (0, width, 2 * width)
    else:
        shapes = [(count, width), (tokens, width), (tokens, width)]
        columns = (0, 0, 0)
    return pl.pallas_call(
        functools.partial(
            attend_backward_kernel, block=min(256, count), columns=columns, carried=len(sums)
        ),
        grid=(heads,),
        in_specs=[
            pl.BlockSpec((count, width), lambda h: (0, qcol)),
            pl.BlockSpec((tokens, width), lambda h: (0, kcol)),
            pl.BlockSpec((tokens, width), lambda h: (0, vcol)),
            whole((count, 1)),
            whole((tokens, 1)),
            whole((heads, count)),
            whole((count, width)),
            whole((count, width)),
        ]
        + [ANY] * len(sums),
        out_specs=[whole(shape) for shape in shapes] + [ANY] * len(sums),
        out_shape=[jax.ShapeDtypeStruct(shape, BF) for shape in shapes]
        + [summed(total) for total in sums],
        scratch_shapes=[pltpu.VMEM((heads, count), F32)]
        + (Sum.scratch(sums) if sums else []),
        compiler_params=pltpu.CompilerParams(
            vmem_limit_bytes=60 * 1024 * 1024,
            collective_id=collective,
            has_side_effects=bool(sums),
        ),
        cost_estimate=pl.CostEstimate(
            flops=heads * count * tokens * 10 * 256,
            bytes_accessed=2 * width * (4 * count + 4 * tokens),
            transcendentals=heads * count * tokens,
        ),
        name="attend_backward",
    )(query, keys, values, seg_query, seg_keys, totals, out, grad, *sums)


class Rows:
    def __init__(self, seq, rows):
        self.seq, self.rows = seq, rows
        self.share = seq // rows
        here = lax.axis_index("seq")
        self.row, self.part = here // self.share, here % self.share

    def device(self, row, part):
        return (row % self.rows) * self.share + part % self.share

    def shift_rows(self, shift):
        return [
            (self.device(r, p), self.device(r + shift, p))
            for r in range(self.rows)
            for p in range(self.share)
        ]

    def shift_parts(self, shift):
        return [
            (self.device(r, p), self.device(r, p + shift))
            for r in range(self.rows)
            for p in range(self.share)
        ]

    def to_rows(self, array):
        pieces = []
        for shift in range(self.rows):
            piece = lax.dynamic_index_in_dim(
                array, (self.row + shift) % self.rows, 0, keepdims=False
            )
            if shift:
                piece = lax.ppermute(piece, "seq", self.shift_rows(shift))
            pieces.append(piece)
        return pieces

    def to_spans(self, pieces):
        result = jnp.zeros((self.rows,) + pieces[0].shape, pieces[0].dtype)
        for shift, piece in enumerate(pieces):
            if shift:
                piece = lax.ppermute(piece, "seq", self.shift_rows(-shift))
            result = lax.dynamic_update_index_in_dim(
                result, piece, (self.row + shift) % self.rows, 0
            )
        return result

    def gather_parts(self, array):
        return jnp.concatenate(
            [array]
            + [
                lax.ppermute(array, "seq", self.shift_parts(shift))
                for shift in range(1, self.share)
            ],
            axis=0,
        )

    def sum_parts(self, array):
        count = array.shape[0] // self.share
        total = array[:count].astype(F32)
        for shift in range(1, self.share):
            piece = array[shift * count : (shift + 1) * count]
            total = total + lax.ppermute(piece, "seq", self.shift_parts(-shift)).astype(F32)
        return total.astype(array.dtype)

    def all_parts(self, array):
        total = array
        for shift in range(1, self.share):
            total = total + lax.ppermute(array, "seq", self.shift_parts(shift))
        return total


COPIES = ("plane", "core")
EVERY = ("seq", "plane", "core")


def own_slice(weights, cut):
    copies = lax.axis_size(COPIES)
    here = lax.axis_index(COPIES)
    blocks = [weight.shape[1] // cut for weight in weights]
    per = weights[0].shape[0]
    count = per * sum(blocks) // copies
    piece, row = here * count // per, here * count % per
    own = None
    first = 0
    for weight, number in zip(weights, blocks):
        column = jnp.clip(piece - first, 0, number - 1) * cut
        part = lax.dynamic_slice(weight, (row, column), (count, cut))
        own = part if own is None else jnp.where(piece >= first, part, own)
        first += number
    return own, (lax.axis_size("seq"), sum(blocks) * per, cut)


def gather_slices(slices, after=None):
    own, shape = slices
    if after is not None:
        own, _ = lax.optimization_barrier((own, after))
    return lax.all_gather(own, EVERY, axis=0, tiled=True).reshape(shape)


def reduce_bundle(bundle):
    seq, count, columns = bundle.shape
    planes = lax.axis_size("plane")
    core = lax.axis_index("core")
    parts = bundle.reshape(seq, planes, 2, count // planes // 2, columns)
    keep = lax.dynamic_index_in_dim(parts, core, 2, keepdims=False).swapaxes(0, 1)
    send = lax.dynamic_index_in_dim(parts, 1 - core, 2, keepdims=False).swapaxes(0, 1)
    got = lax.ppermute(send, "core", [(0, 1), (1, 0)])
    both = (keep.astype(F32) + got.astype(F32)).astype(BF)
    mine = lax.psum_scatter(both, "plane", scatter_dimension=0, tiled=True)[0]
    own = lax.psum_scatter(mine, "seq", scatter_dimension=0, tiled=True)[0]
    return lax.all_gather(own, COPIES, axis=0, tiled=True)


def split_rows(full, count):
    return [
        full[:, start : start + count].reshape(-1, full.shape[2])
        for start in range(0, full.shape[1], count)
    ]


MIB = 1024 * 1024


def spec(shape, index, once=False):
    if once:
        return pl.BlockSpec(shape, index, pipeline_mode=pl.Buffered(1))
    return pl.BlockSpec(shape, index)


def fixed(shape):
    return spec(shape, lambda *_: (0,) * len(shape), once=True)


def call(
    kernel, grid, inputs, outputs, args, name, flops, scratch=(), scalars=None, collective=None
):
    moved = sum(math.prod(arg.shape) * arg.dtype.itemsize for arg in args)
    moved += sum(math.prod(shape) * jnp.dtype(kind).itemsize for shape, kind, _ in outputs)
    grid_spec = pltpu.PrefetchScalarGridSpec(
        num_scalar_prefetch=0 if scalars is None else 1,
        grid=grid,
        in_specs=inputs,
        out_specs=[block for _, _, block in outputs],
        scratch_shapes=list(scratch),
    )
    given = args if scalars is None else [scalars] + list(args)
    return pl.pallas_call(
        kernel,
        grid_spec=grid_spec,
        out_shape=[jax.ShapeDtypeStruct(shape, kind) for shape, kind, _ in outputs],
        compiler_params=pltpu.CompilerParams(
            vmem_limit_bytes=60 * MIB,
            collective_id=collective,
            has_side_effects=collective is not None,
        ),
        cost_estimate=pl.CostEstimate(flops=flops, bytes_accessed=moved, transcendentals=0),
        name=name,
    )(*given)


def square(block):
    return block.reshape(-1, block.shape[-1])


def chunks(count, size=256):
    return [pl.ds(start, min(size, count)) for start in range(0, count, min(size, count))]


def carry(refs, bundles):
    refs = list(refs)
    take = lambda count: [refs.pop(0) for _ in range(count)]
    return take, [take(count) for count in bundles]


def project_kernel(
    x_ref, hot_ref, shift_ref, scale_ref, w_ref, bias_ref, seg_ref, *refs, block, bundles
):
    take, given = carry(refs, bundles)
    (goal_in,) = take(1)
    qkv_ref, modt_ref, out_ref, total_ref = take(4)
    targets = take(len(bundles))
    (goal_out,) = take(1)
    (low_ref,) = take(1)
    gather = Gather(given, targets, take(Gather.room(len(bundles))))
    tokens = Rounds([goal_in], [goal_out], take(2))
    head = pl.program_id(0)
    width = x_ref.shape[1]
    steps = gather.steps()

    def point(number):
        if number == SECOND_AT:
            gather.issue(1)
        if number == THIRD_AT:
            tokens.start()
        for step, when in zip(steps, GATHER_AT):
            if when == number:
                step()

    @pl.when(head == 0)
    def _():
        gather.link.greet()
        gather.start()
        for rows in chunks(x_ref.shape[0]):
            normed, _ = norm_stats(x_ref[rows, :].astype(F32))
            hot = hot_ref[rows, :]
            low = normed * (1.0 + dot_nn(hot, scale_ref[...])) + dot_nn(hot, shift_ref[...])
            low_ref[rows, :] = low.astype(BF)
            modt_ref[:, rows] = low.astype(BF).T
        point(0)
        for j in range(3):
            columns = pl.ds(j * width, width)
            weight = square(w_ref[:, j])
            for rows in chunks(x_ref.shape[0]):
                qkv_ref[rows, columns] = (
                    dot_nn(low_ref[rows, :], weight) + bias_ref[:, columns]
                ).astype(BF)
            point(j + 1)

    for number in range(4, max(GATHER_AT) + 1):
        if number in GATHER_AT + (SECOND_AT, THIRD_AT):
            pl.when(head == number - 3)(functools.partial(point, number))
    parts = ((qkv_ref, 0), (qkv_ref, width), (qkv_ref, 2 * width))
    attend_head(head, parts, (seg_ref, seg_ref), out_ref, total_ref, block)

    @pl.when(head == pl.num_programs(0) - 1)
    def _():
        gather.finish()
        tokens.finish()


def project(x, hot, mod, weights, bias, seg, heads, cuts, shards, goals, collective):
    tokens, width = x.shape
    seq, _, per, _ = weights.shape
    part = lambda index: spec((mod.shape[0], width), lambda h: (0, index), once=True)
    flat = [array for shard in shards for array in shard]
    return call(
        functools.partial(
            project_kernel, block=min(256, tokens), bundles=[len(shard) for shard in shards]
        ),
        (heads,),
        [
            fixed((tokens, width)),
            fixed(hot.shape),
            part(0),
            part(1),
            spec((seq, 3, per, width), lambda h: (0, 0, 0, 0), once=True),
            fixed((1, 3 * width)),
            fixed(seg.shape),
        ]
        + [ANY] * (len(flat) + 1),
        [
            ((tokens, 3 * width), BF, fixed((tokens, 3 * width))),
            ((width, tokens), BF, fixed((width, tokens))),
            ((tokens, width), BF, fixed((tokens, width))),
            ((heads, tokens), F32, fixed((heads, tokens))),
        ]
        + [(shape.shape, BF, ANY) for shape in gathered(cuts, shards)]
        + [(goals.shape, BF, ANY)],
        [x, hot, mod, mod, weights, bias, seg] + flat + [goals],
        "project",
        6 * tokens * width * width + heads * tokens * tokens * 4 * 256,
        [pltpu.VMEM((tokens, width), BF)]
        + Gather.scratch(gathered(cuts, shards))
        + Rounds.scratch(1),
        collective=collective,
    )


def merge_kernel(
    out_ref, x_ref, hot_ref, gate_ref, shift_ref, scale_ref, w_ref, bias_ref,
    branch_ref, mid_ref, low_ref, lowt_ref, outt_ref,
):
    hot = hot_ref[...]
    branch = dot_nn(out_ref[...], square(w_ref[...])) + bias_ref[...]
    middle = x_ref[...].astype(F32) + dot_nn(hot, gate_ref[...]) * branch
    normed, _ = norm_stats(middle)
    low = normed * (1.0 + dot_nn(hot, scale_ref[...])) + dot_nn(hot, shift_ref[...])
    low = low.astype(BF)
    branch_ref[...] = branch.astype(BF)
    mid_ref[...] = middle
    low_ref[...] = low
    lowt_ref[...] = low.T
    outt_ref[...] = out_ref[...].T


def merge(attended, x, hot, mod, weights, bias):
    tokens, width = x.shape
    seq, _, per, _ = weights.shape
    size = min(256, tokens)
    part = lambda index: spec((mod.shape[0], width), lambda i: (0, index), once=True)
    rows = spec((size, width), lambda i: (i, 0))
    turned = spec((width, size), lambda i: (0, i))
    return call(
        merge_kernel,
        (tokens // size,),
        [
            rows,
            rows,
            spec((size, hot.shape[1]), lambda i: (i, 0)),
            part(2),
            part(3),
            part(4),
            spec((seq, 1, per, width), lambda i: (0, 3, 0, 0), once=True),
            fixed((1, width)),
        ],
        [
            ((tokens, width), BF, rows),
            ((tokens, width), F32, rows),
            ((tokens, width), BF, rows),
            ((width, tokens), BF, turned),
            ((width, tokens), BF, turned),
        ],
        [attended, x, hot, mod, mod, mod, weights, bias],
        "merge",
        2 * tokens * width * width,
    )


def gelu_pair(value):
    factor = math.sqrt(2.0 / math.pi)
    squared = value * value
    tangent = jnp.tanh(factor * value * (1.0 + GELU_COEF * squared))
    half = 0.5 * (1.0 + tangent)
    slope = half + (0.5 * factor) * value * (1.0 - tangent * tangent) * (
        1.0 + 3.0 * GELU_COEF * squared
    )
    return value * half, slope


def feed_kernel(
    low_ref, w_in_ref, b_in_ref, w_out_ref, b_out_ref, mid_ref, hot_ref, gate_ref, *refs, bundles
):
    take, given = carry(refs, bundles)
    actt_ref, slope_ref, res_ref, rest_ref, branch_ref = take(5)
    targets = take(len(bundles))
    (total,) = take(1)
    gather = Gather(given, targets, take(Gather.room(len(bundles))), eager=True)
    steps = gather.steps()
    blocks = targets[0].shape[1]
    step = pl.program_id(0)

    @pl.when(step == 0)
    def _():
        gather.link.greet()
        gather.start()
        total[...] = jnp.zeros_like(total)

    w_in, w_out = square(w_in_ref[...]), w_out_ref[...]
    pieces = chunks(low_ref.shape[0])
    for number, rows in enumerate(pieces):
        if number % 2 == 0:
            for index, action in enumerate(steps):
                if FEED_AT[index] % 2 == number // 2:
                    pl.when(step == FEED_AT[index] // 2)(action)
        hmid = dot_nn(low_ref[rows, :], w_in) + b_in_ref[...]
        act, slope = gelu_pair(hmid)
        act = act.astype(BF)
        slope_ref[rows, :] = slope.astype(BF)
        actt_ref[:, rows] = act.T
        total[rows, :] += dot_nn(act, w_out)

    @pl.when(step == pl.num_programs(0) - 1)
    def _():
        for rows in pieces:
            branch = total[rows, :] + b_out_ref[...]
            result = mid_ref[rows, :] + dot_nn(hot_ref[rows, :], gate_ref[...]) * branch
            result = result.astype(BF)
            res_ref[rows, :] = result
            rest_ref[:, rows] = result.T
            branch_ref[rows, :] = branch.astype(BF)
        for index, action in enumerate(steps):
            if FEED_AT[index] == 2 * blocks:
                action()
        gather.finish()


def feed(low, w_in, b_in, w_out, b_out, mid, hot, mod, cuts, shards, collective):
    tokens, width = low.shape
    seq, blocks, per, cut = w_in.shape
    hidden = blocks * cut
    flat = [array for shard in shards for array in shard]
    return call(
        functools.partial(feed_kernel, bundles=[len(shard) for shard in shards]),
        (blocks,),
        [
            fixed((tokens, width)),
            spec((seq, 1, per, cut), lambda j: (0, j, 0, 0)),
            spec((1, cut), lambda j: (0, j)),
            spec((cut, width), lambda j: (j, 0)),
            fixed((1, width)),
            fixed((tokens, width)),
            fixed(hot.shape),
            spec((mod.shape[0], width), lambda j: (0, 5), once=True),
        ]
        + [ANY] * len(flat),
        [
            ((hidden, tokens), BF, spec((cut, tokens), lambda j: (j, 0))),
            ((tokens, hidden), BF, spec((tokens, cut), lambda j: (0, j))),
            ((tokens, width), BF, fixed((tokens, width))),
            ((width, tokens), BF, fixed((width, tokens))),
            ((tokens, width), BF, fixed((tokens, width))),
        ]
        + [(shape.shape, BF, ANY) for shape in gathered(cuts, shards)],
        [low, w_in, b_in, w_out, b_out, mid, hot, mod] + flat,
        "feed",
        4 * tokens * width * hidden,
        [pltpu.VMEM((tokens, width), F32)] + Gather.scratch(gathered(cuts, shards)),
        collective=collective,
    )


def silu_pair(value):
    gate = jax.nn.sigmoid(value)
    return value * gate, gate * (1.0 + value * (1.0 - gate))


def align_kernel(
    res_ref, w_in_ref, b_in_ref, w_mid_ref, b_mid_ref, w_out_ref, b_out_ref, goal_ref, rows_ref,
    act1t_ref, act2t_ref, gfeat_ref, gh2_ref, gh1_ref, gout_ref, back_ref, act1_ref, slope1_ref,
    *sems,
):
    tokens = Rounds([rows_ref], [back_ref], sems)

    @pl.when(pl.program_id(0) == 0)
    def _():
        tokens.link.greet()
        tokens.start()

    blocks, cut = w_in_ref.shape[1], w_in_ref.shape[3]
    res = res_ref[...]
    for j in range(blocks):
        columns = pl.ds(j * cut, cut)
        hidden1 = dot_nn(res, square(w_in_ref[:, j])) + b_in_ref[:, columns]
        act, slope = silu_pair(hidden1)
        act1_ref[:, columns] = act.astype(BF)
        slope1_ref[:, columns] = slope
    act1 = act1_ref[...]
    act1t_ref[...] = act1.T
    hidden2 = dot_nn(act1, w_mid_ref[...]) + b_mid_ref[...]
    act2, slope2 = silu_pair(hidden2)
    act2 = act2.astype(BF)
    act2t_ref[...] = act2.T
    feats = dot_nn(act2, w_out_ref[...]) + b_out_ref[...]
    goals = goal_ref[...].astype(F32)
    inv_feat = lax.rsqrt(jnp.sum(feats * feats, axis=-1, keepdims=True) + EPSILON)
    feat_unit = feats * inv_feat
    goal_unit = goals * lax.rsqrt(jnp.sum(goals * goals, axis=-1, keepdims=True) + EPSILON)
    cosine = jnp.sum(feat_unit * goal_unit, axis=-1, keepdims=True)
    weight = -0.5 * feats.shape[1]
    gfeat = (weight * inv_feat * (goal_unit - cosine * feat_unit)).astype(BF)
    gfeat_ref[...] = gfeat
    gh2 = (dot_nt(gfeat, w_out_ref[...]) * slope2).astype(BF)
    gh2_ref[...] = gh2
    gh1 = (dot_nt(gh2, w_mid_ref[...]) * slope1_ref[...]).astype(BF)
    gh1_ref[...] = gh1
    total = None
    for j in range(blocks):
        part = dot_nt(gh1_ref[:, pl.ds(j * cut, cut)], square(w_in_ref[:, j]))
        total = part if total is None else total + part
    gout_ref[...] = total
    pl.when(pl.program_id(0) == pl.num_programs(0) - 1)(tokens.finish)


def align(res, w_in, b_in, w_mid, b_mid, w_out, b_out, goals, collective):
    tokens, width = res.shape
    inner, goal_width = w_out.shape
    size = min(256, tokens)
    rows = lambda n: spec((size, n), lambda i: (i, 0))
    turned = lambda n: spec((n, size), lambda i: (0, i))
    return call(
        align_kernel,
        (tokens // size,),
        [
            rows(width),
            fixed(w_in.shape),
            fixed((1, inner)),
            fixed(w_mid.shape),
            fixed((1, inner)),
            fixed(w_out.shape),
            fixed((1, goal_width)),
            rows(goal_width),
            ANY,
        ],
        [
            ((inner, tokens), BF, turned(inner)),
            ((inner, tokens), BF, turned(inner)),
            ((tokens, goal_width), BF, rows(goal_width)),
            ((tokens, inner), BF, rows(inner)),
            ((tokens, inner), BF, rows(inner)),
            ((tokens, width), F32, rows(width)),
            ((SEQ, tokens // SEQ, width), BF, ANY),
        ],
        [res, w_in, b_in, w_mid, b_mid, w_out, b_out, goals, res.reshape(SEQ, -1, width)],
        "align",
        4 * tokens * inner * (width + inner + goal_width),
        [pltpu.VMEM((size, inner), BF), pltpu.VMEM((size, inner), F32)] + Rounds.scratch(1),
        collective=collective,
    )


def feed_back_kernel(
    gout_ref, branch_ref, hot_ref, hott_ref, gate_ref, w_out_ref, slope_ref, w_in_ref,
    gmlp_ref, ghmid_ref, gmod_ref, ggate_ref,
):
    step = pl.program_id(0)

    @pl.when(step == 0)
    def _():
        sums = None
        for rows in chunks(gout_ref.shape[0]):
            gout = gout_ref[rows, :]
            gmlp_ref[rows, :] = (gout * dot_nn(hot_ref[rows, :], gate_ref[...])).astype(BF)
            part = dot_nn(hott_ref[:, rows], (gout * branch_ref[rows, :].astype(F32)).astype(BF))
            sums = part if sums is None else sums + part
        ggate_ref[...] = sums
        gmod_ref[...] = jnp.zeros_like(gmod_ref)

    w_out, w_in = w_out_ref[...], square(w_in_ref[...])
    for rows in chunks(gout_ref.shape[0]):
        ghmid = (dot_nt(gmlp_ref[rows, :], w_out) * slope_ref[rows, :].astype(F32)).astype(BF)
        ghmid_ref[rows, :] = ghmid
        gmod_ref[rows, :] += dot_nt(ghmid, w_in)


def feed_back(gout, branch, hot, hott, mod, w_out, slope, w_in):
    tokens, width = gout.shape
    seq, blocks, per, cut = w_in.shape
    hidden = blocks * cut
    return call(
        feed_back_kernel,
        (blocks,),
        [
            fixed((tokens, width)),
            fixed((tokens, width)),
            fixed(hot.shape),
            fixed(hott.shape),
            spec((mod.shape[0], width), lambda j: (0, 5), once=True),
            spec((cut, width), lambda j: (j, 0)),
            spec((tokens, cut), lambda j: (0, j)),
            spec((seq, 1, per, cut), lambda j: (0, j, 0, 0)),
        ],
        [
            ((tokens, width), BF, fixed((tokens, width))),
            ((tokens, hidden), BF, spec((tokens, cut), lambda j: (0, j))),
            ((tokens, width), F32, fixed((tokens, width))),
            ((hott.shape[0], width), F32, fixed((hott.shape[0], width))),
        ],
        [gout, branch, hot, hott, mod, w_out, slope, w_in],
        "feed_back",
        4 * tokens * width * hidden,
    )


def add_rows(ref, value):
    @pl.when(pl.program_id(0) == 0)
    def _():
        ref[...] = value

    @pl.when(pl.program_id(0) > 0)
    def _():
        ref[...] += value


def merge_back_kernel(
    gout_ref, gmod_ref, mid_ref, branch_ref, hot_ref, hott_ref, gate_ref, scale_ref, w_ref,
    gmid_ref, gbranch_ref, gatt_ref, gshift_ref, gscale_ref, ggate_ref,
):
    hot, hott = hot_ref[...], hott_ref[...]
    gmod = gmod_ref[...]
    normed, inv_std = norm_stats(mid_ref[...])
    gmid = gout_ref[...] + norm_back(
        gmod * (1.0 + dot_nn(hot, scale_ref[...])), normed, inv_std
    )
    gmid_ref[...] = gmid
    gbranch = (gmid * dot_nn(hot, gate_ref[...])).astype(BF)
    gbranch_ref[...] = gbranch
    gatt_ref[...] = dot_nt(gbranch, square(w_ref[...])).astype(BF)
    add_rows(gshift_ref, dot_nn(hott, gmod.astype(BF)))
    add_rows(gscale_ref, dot_nn(hott, (gmod * normed).astype(BF)))
    add_rows(ggate_ref, dot_nn(hott, (gmid * branch_ref[...].astype(F32)).astype(BF)))


def merge_back(gout, gmod, mid, branch, hot, hott, mod, weights):
    tokens, width = gout.shape
    seq, _, per, _ = weights.shape
    size = min(256, tokens)
    part = lambda index: spec((mod.shape[0], width), lambda i: (0, index), once=True)
    rows = spec((size, width), lambda i: (i, 0))
    sums = ((hott.shape[0], width), F32, fixed((hott.shape[0], width)))
    return call(
        merge_back_kernel,
        (tokens // size,),
        [
            rows,
            rows,
            rows,
            rows,
            spec((size, hot.shape[1]), lambda i: (i, 0)),
            spec((hott.shape[0], size), lambda i: (0, i)),
            part(2),
            part(4),
            spec((seq, 1, per, width), lambda i: (0, 3, 0, 0), once=True),
        ],
        [
            ((tokens, width), F32, rows),
            ((tokens, width), BF, rows),
            ((tokens, width), BF, rows),
            sums,
            sums,
            sums,
        ],
        [gout, gmod, mid, branch, hot, hott, mod, mod, weights],
        "merge_back",
        2 * tokens * width * width,
    )


def project_back_kernel(
    gqkv_ref, x_ref, gmid_ref, hot_ref, hott_ref, scale_ref, w_ref, *refs, carried
):
    refs = list(refs)
    take = lambda number: [refs.pop(0) for _ in range(number)]
    sums = take(carried)
    gin_ref, gshift_ref, gscale_ref = take(3)
    work = Sum(sums, take(carried), refs)

    @pl.when(pl.program_id(0) == 0)
    def _():
        work.link.greet()
        work.start()

    width = x_ref.shape[1]
    hott = hott_ref[...]
    gmod = None
    for j in range(3):
        part = dot_nt(gqkv_ref[:, pl.ds(j * width, width)], square(w_ref[:, j]))
        gmod = part if gmod is None else gmod + part
    normed, inv_std = norm_stats(x_ref[...].astype(F32))
    gin = gmid_ref[...] + norm_back(
        gmod * (1.0 + dot_nn(hot_ref[...], scale_ref[...])), normed, inv_std
    )
    gin_ref[...] = gin.astype(BF)
    add_rows(gshift_ref, dot_nn(hott, gmod.astype(BF)))
    add_rows(gscale_ref, dot_nn(hott, (gmod * normed).astype(BF)))

    @pl.when(pl.program_id(0) == pl.num_programs(0) - 1)
    def _():
        for k in range(carried):
            work.add(k)
        work.finish()


def project_back(gqkv, x, gmid, hot, hott, mod, weights, carried, collective):
    tokens, width = x.shape
    seq, _, per, _ = weights.shape
    size = min(256, tokens)
    rows = spec((size, width), lambda i: (i, 0))
    sums = ((hott.shape[0], width), F32, fixed((hott.shape[0], width)))
    return call(
        functools.partial(project_back_kernel, carried=len(carried)),
        (tokens // size,),
        [
            spec((size, 3 * width), lambda i: (i, 0)),
            rows,
            rows,
            spec((size, hot.shape[1]), lambda i: (i, 0)),
            spec((hott.shape[0], size), lambda i: (0, i)),
            spec((mod.shape[0], width), lambda i: (0, 1), once=True),
            spec((seq, 3, per, width), lambda i: (0, 0, 0, 0), once=True),
        ]
        + [ANY] * len(carried),
        [((tokens, width), BF, rows), sums, sums]
        + [(total.shape[1:], total.dtype, ANY) for total in carried],
        [gqkv, x, gmid, hot, hott, mod, weights] + list(carried),
        "project_back",
        6 * tokens * width * width,
        Sum.scratch(carried),
        collective=collective,
    )


def weight_kernel(where_ref, left_ref, right_ref, *refs, first):
    left = left_ref[...].reshape(-1, left_ref.shape[-1])
    got_ref = None if first else refs[0]
    out_ref = refs[0] if first else refs[1]
    result = dot_nn(left, right_ref[...]).reshape(out_ref.shape)
    if first:
        ones = jnp.ones((16, right_ref.shape[0]), BF)
        refs[1][...] = dot_nn(ones, right_ref[...])
    else:
        result = result + got_ref[...].astype(F32)
    out_ref[...] = result.astype(BF)


def weight_half(where, turned, right, seq, planes, by_columns, got=None):
    count, tokens = turned.shape
    columns = right.shape[1]
    first = got is None
    half = (lambda w: 1 - w[0]) if first else (lambda w: w[0])
    if by_columns:
        per, cut = count // seq // 2, columns // planes
        left = turned.reshape(seq, 2, per, tokens)
        left_spec = spec((seq, 1, per, tokens), lambda j, w: (0, half(w), 0, 0))
        right_spec = spec((tokens, cut), lambda j, w: (0, j))
        sum_spec = spec((16, cut), lambda j, w: (0, j))
    else:
        per, cut = count // seq // planes // 2, columns
        left = turned.reshape(seq, planes, 2, per, tokens)
        left_spec = spec((seq, 1, 1, per, tokens), lambda j, w: (0, j, half(w), 0, 0))
        right_spec = spec((tokens, cut), lambda j, w: (0, 0))
        sum_spec = spec((16, cut), lambda j, w: (0, 0))
    block = spec((1, seq, per, cut), lambda j, w: (j, 0, 0, 0))
    outputs = [((planes, seq, per, cut), BF, block)]
    inputs, args = [left_spec, right_spec], [left, right]
    if first:
        outputs.append(((16, columns), F32, sum_spec))
    else:
        inputs.append(block)
        args.append(got)
    return call(
        functools.partial(weight_kernel, first=first),
        (planes,),
        inputs,
        outputs,
        args,
        "weight_other" if first else "weight_own",
        count * tokens * columns,
        scalars=where,
    )


ANY = pl.BlockSpec(memory_space=pl.ANY)
SEQ, PLANES = 4, 4


class Link:
    def __init__(self):
        self.z, self.p, self.c = (lax.axis_index(name) for name in ("seq", "plane", "core"))

    def ahead(self, shift):
        return lax.rem(self.z + shift, SEQ)

    def behind(self, shift):
        return lax.rem(self.z + SEQ - shift, SEQ)

    def across(self, bit):
        low = lax.rem(self.p, 2)
        high = self.p // 2
        low = 1 - low if bit % 2 else low
        high = 1 - high if bit // 2 else high
        return high * 2 + low

    def copy(self, source, target, sems, axis, index):
        return pltpu.make_async_remote_copy(
            src_ref=source,
            dst_ref=target,
            send_sem=sems[0],
            recv_sem=sems[1],
            device_id={axis: index},
            device_id_type=pl.DeviceIdType.MESH,
        )

    def greet(self):
        barrier = pltpu.get_barrier_semaphore()
        for step in range(1, SEQ):
            signal = functools.partial(
                pl.semaphore_signal, barrier, inc=1, device_id_type=pl.DeviceIdType.MESH
            )
            signal(device_id={"seq": self.ahead(step)})
            signal(device_id={"plane": self.across(step)})
        pl.semaphore_signal(
            barrier, inc=1, device_id={"core": 1 - self.c}, device_id_type=pl.DeviceIdType.MESH
        )
        pl.semaphore_wait(barrier, 2 * SEQ - 1)


class Gather:
    def __init__(self, shards, targets, sems, eager=False, after=None):
        self.link = Link()
        self.shards, self.targets = shards, targets
        self.eager, self.after = eager, after
        self.z_sems, self.p_sems, self.c_sems, self.local_sems, self.out_sems = sems[:5]
        self.bufs = sems[5:]

    @staticmethod
    def scratch(targets):
        dma = pltpu.SemaphoreType.DMA
        count = len(targets)
        return [
            dma((2, count, 3)),
            dma((2, count, 3, 6)),
            dma((2, count, 3)),
            dma((count, 4)),
            dma((count,)),
        ] + [pltpu.VMEM(target.shape[1:], BF) for target in targets]

    @staticmethod
    def room(count):
        return 5 + count

    def rows(self, target):
        half = target.shape[2] // 2
        return pl.ds(pl.multiple_of(self.link.c * half, half), half)

    def locals(self, k):
        target = self.targets[k]
        width = target.shape[3]
        block = 0
        for array in self.shards[k]:
            if len(array.shape) == 3:
                parts = [array.at[index] for index in range(array.shape[0])]
            else:
                parts = [
                    array.at[:, pl.ds(start, width)] for start in range(0, array.shape[1], width)
                ]
            for part in parts:
                yield pltpu.make_async_copy(
                    part, self.bufs[k].at[block], self.local_sems.at[k, block]
                )
                block += 1

    def stored(self, k):
        return pltpu.make_async_copy(
            self.bufs[k], self.targets[k].at[self.link.z], self.out_sems.at[k]
        )

    def along(self, k, shift, incoming):
        link, target = self.link, self.targets[k]
        place = link.behind(shift) if incoming else link.z
        return link.copy(
            self.bufs[k].at[link.p, self.rows(target), :],
            target.at[place, link.p, self.rows(target), :],
            (self.z_sems.at[0, k, shift - 1], self.z_sems.at[1, k, shift - 1]),
            "seq",
            link.ahead(shift),
        )

    def across(self, k, shift, index, incoming):
        link, target = self.link, self.targets[k]
        half = target.shape[2] // 2
        first = -(-half // 32) * 16
        start, size = ((0, first), (first, half - first))[index % 2]
        peer = (1, 1, 2, 2, 2, 1)[index]
        plane = link.p
        if incoming:
            plane = link.across(3 if index >= 4 else peer)
        elif index >= 4:
            plane = link.across(3 - peer)
        rows = pl.ds(pl.multiple_of(link.c * half + start, 16), size)
        place = target.at[link.behind(shift), plane, rows, :]
        return link.copy(
            place,
            place,
            (self.p_sems.at[0, k, shift - 1, index], self.p_sems.at[1, k, shift - 1, index]),
            "plane",
            link.across(peer),
        )

    def beside(self, k, shift, incoming):
        link, target = self.link, self.targets[k]
        half = target.shape[2] // 2
        core = 1 - link.c if incoming else link.c
        rows = pl.ds(pl.multiple_of(core * half, half), half)
        place = target.at[link.behind(shift), :, rows, :]
        return link.copy(
            place,
            place,
            (self.c_sems.at[0, k, shift - 1], self.c_sems.at[1, k, shift - 1]),
            "core",
            1 - link.c,
        )

    def start(self):
        count = range(len(self.targets))
        for k in count:
            for copy in self.locals(k):
                copy.start()
        for k in count:
            for copy in self.locals(k):
                copy.wait()
            if k == 0:
                self.issue(0)
            self.stored(k).start()

    def issue(self, k):
        if k < len(self.targets):
            for shift in (1, 3) if self.eager else (1, 3, 2):
                self.along(k, shift, False).start()

    def steps(self):
        return [
            functools.partial(stage, k, shift)
            for stage in (self.spread, self.relay, self.pair)
            for k in range(len(self.targets))
            for shift in (1, 3, 2)
        ]

    def spread(self, k, shift):
        self.along(k, shift, True).wait_recv()
        if self.eager and shift == 1:
            self.along(k, 2, False).start()
        if self.eager and shift == 3:
            self.issue(k + 1)
        if shift == 1 and self.after is not None:
            self.after()
        for index in (0, 3, 1, 2):
            self.across(k, shift, index, False).start()

    def relay(self, k, shift):
        self.across(k, shift, 0, True).wait_recv()
        self.across(k, shift, 4, False).start()
        self.across(k, shift, 3, True).wait_recv()
        self.across(k, shift, 5, False).start()

    def pair(self, k, shift):
        for index in (1, 2, 4, 5):
            self.across(k, shift, index, True).wait_recv()
        self.beside(k, shift, False).start()

    def finish(self):
        for k in range(len(self.targets)):
            for shift in range(1, SEQ):
                self.beside(k, shift, True).wait_recv()
                self.along(k, shift, False).wait_send()
                self.beside(k, shift, False).wait_send()
                for index in range(6):
                    self.across(k, shift, index, False).wait_send()
            self.stored(k).wait()


class Rounds:
    def __init__(self, sources, targets, sems):
        self.link = Link()
        self.sources, self.targets, self.sems, self.local_sems = sources, targets, *sems

    @staticmethod
    def scratch(count):
        dma = pltpu.SemaphoreType.DMA
        return [dma((2, count, 3)), dma((count,))]

    def along(self, k, shift, incoming):
        link = self.link
        return link.copy(
            self.sources[k].at[link.ahead(shift)],
            self.targets[k].at[link.behind(shift) if incoming else link.z],
            (self.sems.at[0, k, shift - 1], self.sems.at[1, k, shift - 1]),
            "seq",
            link.ahead(shift),
        )

    def local(self, k):
        z = self.link.z
        return pltpu.make_async_copy(
            self.sources[k].at[z], self.targets[k].at[z], self.local_sems.at[k]
        )

    def start(self):
        for k in range(len(self.targets)):
            for shift in (2, 1, 3):
                self.along(k, shift, False).start()
            self.local(k).start()

    def finish(self):
        for k in range(len(self.targets)):
            for shift in range(1, SEQ):
                self.along(k, shift, True).wait_recv()
                self.along(k, shift, False).wait_send()
            self.local(k).wait()


class Sum:
    def __init__(self, sources, results, refs):
        self.link = Link()
        self.sources, self.results = sources, results
        self.bufs = refs[: len(sources)]
        self.sems, self.local_sems = refs[len(sources) :]

    @staticmethod
    def scratch(sources):
        dma = pltpu.SemaphoreType.DMA
        bufs = [pltpu.VMEM((5,) + source.shape[1:], source.dtype) for source in sources]
        return bufs + [dma((2, len(sources), 3)), dma((len(sources), 2))]

    def along(self, k, shift):
        link = self.link
        return link.copy(
            self.sources[k].at[link.ahead(shift)],
            self.bufs[k].at[shift - 1],
            (self.sems.at[0, k, shift - 1], self.sems.at[1, k, shift - 1]),
            "seq",
            link.ahead(shift),
        )

    def mine(self, k):
        return pltpu.make_async_copy(
            self.sources[k].at[self.link.z], self.bufs[k].at[3], self.local_sems.at[k, 0]
        )

    def stored(self, k):
        return pltpu.make_async_copy(
            self.bufs[k].at[4], self.results[k], self.local_sems.at[k, 1]
        )

    def start(self):
        for k in range(len(self.sources)):
            for shift in (2, 1, 3):
                self.along(k, shift).start()
            self.mine(k).start()

    def add(self, k):
        for shift in range(1, SEQ):
            self.along(k, shift).wait_recv()
        self.mine(k).wait()
        buf = self.bufs[k]
        total = buf[0].astype(F32) + buf[1].astype(F32) + buf[2].astype(F32) + buf[3].astype(F32)
        buf[4] = total.astype(buf.dtype)
        self.stored(k).start()

    def finish(self):
        for k in range(len(self.sources)):
            for shift in range(1, SEQ):
                self.along(k, shift).wait_send()
            self.stored(k).wait()


class Share:
    def __init__(self, sources, targets, refs):
        self.link = Link()
        self.sources, self.targets = sources, targets
        self.bufs = refs[: len(sources)]
        self.p_sems, self.c_sems, self.local_sems = refs[len(sources) :]

    @staticmethod
    def scratch(sources, shared):
        dma = pltpu.SemaphoreType.DMA
        count = len(sources)
        bufs = [
            pltpu.VMEM((5 if one else 1,) + source.shape[-2:], source.dtype)
            for source, one in zip(sources, shared)
        ]
        return bufs + [dma((2, count, 3)), dma((2, count, 4)), dma((count, 2))]

    def shared(self, k):
        return len(self.targets[k].shape) == 3

    def loaded(self, k):
        return pltpu.make_async_copy(self.sources[k], self.bufs[k].at[0], self.local_sems.at[k, 0])

    def across(self, k, bit, incoming):
        link = self.link
        plane = link.across(bit)
        if self.shared(k):
            target = self.bufs[k].at[bit]
        else:
            target = self.targets[k].at[plane if incoming else link.p, link.c]
        return link.copy(
            self.bufs[k].at[0],
            target,
            (self.p_sems.at[0, k, bit - 1], self.p_sems.at[1, k, bit - 1]),
            "plane",
            plane,
        )

    def beside(self, k, bit, incoming):
        link = self.link
        core = 1 - link.c if incoming else link.c
        if self.shared(k):
            source, target = self.bufs[k].at[4], self.targets[k].at[core]
        else:
            plane = link.across(bit)
            target = self.targets[k].at[plane, core]
            source = self.bufs[k].at[0] if bit == 0 else self.targets[k].at[plane, link.c]
        return link.copy(
            source,
            target,
            (self.c_sems.at[0, k, bit], self.c_sems.at[1, k, bit]),
            "core",
            1 - link.c,
        )

    def own(self, k):
        link = self.link
        if self.shared(k):
            source, target = self.bufs[k].at[4], self.targets[k].at[link.c]
        else:
            source, target = self.bufs[k].at[0], self.targets[k].at[link.p, link.c]
        return pltpu.make_async_copy(source, target, self.local_sems.at[k, 1])

    def send(self, k):
        for bit in range(1, PLANES):
            self.across(k, bit, False).start()
        if not self.shared(k):
            self.own(k).start()
            self.beside(k, 0, False).start()

    def pass_on(self, k):
        for bit in range(1, PLANES):
            self.across(k, bit, True).wait_recv()
            if not self.shared(k):
                self.beside(k, bit, False).start()
        if self.shared(k):
            buf = self.bufs[k]
            total = buf[0].astype(F32) + buf[1].astype(F32) + buf[2].astype(F32) + buf[3].astype(F32)
            buf[4] = total.astype(buf.dtype)
            self.own(k).start()
            self.beside(k, 0, False).start()

    def finish(self):
        for k in range(len(self.targets)):
            for bit in range(1 if self.shared(k) else PLANES):
                self.beside(k, bit, True).wait_recv()
                self.beside(k, bit, False).wait_send()
            for bit in range(1, PLANES):
                self.across(k, bit, False).wait_send()
            self.own(k).wait()


def bring_kernel(*refs, bundles, rounds):
    refs = list(refs)
    take = lambda count: [refs.pop(0) for _ in range(count)]
    shards = [take(count) for count in bundles]
    sources = take(rounds)
    targets = take(len(bundles))
    arrived = take(rounds)
    gather_refs = take(Gather.room(len(bundles)))
    tokens = Rounds(sources, arrived, take(2))
    gather = Gather(shards, targets, gather_refs, after=tokens.start)
    gather.link.greet()
    gather.start()
    for step in gather.steps():
        step()
    tokens.finish()
    gather.finish()


def gathered(cuts, shards):
    shapes = []
    for cut, shard in zip(cuts, shards):
        if shard[0].ndim == 3:
            blocks, per = shard[0].shape[:2]
        else:
            blocks, per = sum(array.shape[1] for array in shard) // cut, shard[0].shape[0]
        shapes.append(jax.ShapeDtypeStruct((SEQ, blocks, per, cut), BF))
    return shapes


def bring(cuts, shards, sources, collective):
    flat = [array for shard in shards for array in shard]
    shapes = gathered(cuts, shards) + [jax.ShapeDtypeStruct(array.shape, array.dtype) for array in sources]
    args = flat + list(sources)
    return pl.pallas_call(
        functools.partial(
            bring_kernel, bundles=[len(shard) for shard in shards], rounds=len(sources)
        ),
        in_specs=[ANY] * len(args),
        out_specs=[ANY] * len(shapes),
        out_shape=shapes,
        scratch_shapes=Gather.scratch(gathered(cuts, shards)) + Rounds.scratch(len(sources)),
        compiler_params=pltpu.CompilerParams(
            collective_id=collective, has_side_effects=True, vmem_limit_bytes=60 * MIB
        ),
        cost_estimate=pl.CostEstimate(flops=0, bytes_accessed=300_000_000, transcendentals=0),
        name="bring",
    )(*args)


def settle_kernel(*refs, sums, shares, rounds, through):
    refs = list(refs)
    take = lambda number: [refs.pop(0) for _ in range(number)]
    sum_in, share_in, round_in = take(sums), take(shares), take(rounds)
    sum_out, share_out, round_out = take(sums), take(shares + sums * through), take(rounds)
    add = Sum(sum_in, sum_out, take(sums + 2))
    share = Share(share_in + sum_in * through, share_out, take(len(share_out) + 3))
    tokens = Rounds(round_in, round_out, take(2)) if rounds else None
    add.link.greet()
    add.start()
    if rounds:
        tokens.start()
    for k in range(shares):
        share.loaded(k).start()
    for k in range(shares):
        share.loaded(k).wait()
        share.send(k)
    for k in range(shares):
        share.pass_on(k)
    for k in range(sums):
        add.add(k)
        if through:
            share.bufs[shares + k][0] = add.bufs[k][4]
            share.send(shares + k)
    if through:
        for k in range(sums):
            share.pass_on(shares + k)
    add.finish()
    share.finish()
    if rounds:
        tokens.finish()


def summed(array):
    return jax.ShapeDtypeStruct(array.shape[1:], array.dtype)


def shared_out(array, shared):
    return jax.ShapeDtypeStruct(
        ((2,) if shared else (PLANES, 2)) + array.shape[-2:], array.dtype
    )


def settle(sums, shares, rounds, shared, collective, through=False):
    args = list(sums) + list(shares) + list(rounds)
    given = list(shares) + (list(sums) if through else [])
    shapes = (
        [summed(array) for array in sums]
        + [shared_out(array, one) for array, one in zip(given, shared)]
        + [jax.ShapeDtypeStruct(array.shape, array.dtype) for array in rounds]
    )
    return pl.pallas_call(
        functools.partial(
            settle_kernel,
            sums=len(sums),
            shares=len(shares),
            rounds=len(rounds),
            through=int(through),
        ),
        in_specs=[ANY] * len(args),
        out_specs=[ANY] * len(shapes),
        out_shape=shapes,
        scratch_shapes=Sum.scratch(sums)
        + Share.scratch(given, shared)
        + (Rounds.scratch(len(rounds)) if rounds else []),
        compiler_params=pltpu.CompilerParams(
            collective_id=collective, has_side_effects=True, vmem_limit_bytes=60 * MIB
        ),
        cost_estimate=pl.CostEstimate(flops=0, bytes_accessed=200_000_000, transcendentals=0),
        name="settle",
    )(*args)


def local(
    block_input,
    modulation,
    segment_ids,
    qkv_weight,
    query_value_bias,
    attn_out_weight,
    attn_out_bias,
    mlp_in_weight,
    mlp_in_bias,
    mlp_out_weight,
    mlp_out_bias,
    proj_in_weight,
    proj_in_bias,
    proj_mid_weight,
    proj_mid_bias,
    proj_out_weight,
    proj_out_bias,
    targets,
):
    rows, span, width = block_input.shape
    segs = modulation.shape[1]
    seq = lax.axis_size("seq")
    place = Rows(seq, rows)
    heads = width // HEAD_DIM
    hidden = mlp_in_weight.shape[1]
    inner = proj_mid_weight.shape[1]
    goal_width = targets.shape[2]
    tokens = rows * span
    share = place.share

    x_in = jnp.concatenate(place.to_rows(block_input), axis=0)
    seg_pieces = place.to_rows(segment_ids)
    segs_own = jnp.concatenate(seg_pieces, axis=0)
    seg_query = segs_own[:, None]
    seg_keys = place.gather_parts(seg_query) if share > 1 else seg_query
    goals = jnp.concatenate(place.to_rows(targets), axis=0)
    mod_row = lax.dynamic_index_in_dim(modulation, place.row, 0, keepdims=False)

    per = qkv_weight.shape[0]
    half = inner // 2
    first = gather_slices(own_slice([qkv_weight, attn_out_weight], width))
    second = gather_slices(own_slice([mlp_in_weight], width), first)
    third = gather_slices(own_slice([mlp_out_weight], width), second)
    fourth = gather_slices(own_slice([proj_in_weight], half), third)
    fifth = gather_slices(own_slice([proj_mid_weight], inner), fourth)
    sixth = gather_slices(own_slice([proj_out_weight], goal_width), fifth)
    w_q, w_k, w_v, w_attn = split_rows(first, per)
    w_qkv = jnp.concatenate([w_q, w_k, w_v], axis=1)
    w_mlp_in = jnp.concatenate(split_rows(second, per), axis=1)
    w_mlp_out = third.reshape(hidden, width)
    w_proj_in = jnp.concatenate(split_rows(fourth, per), axis=1)
    w_proj_mid = fifth.reshape(inner, inner)
    w_proj_out = sixth.reshape(inner, goal_width)

    one_hot = (segs_own[:, None] == jnp.arange(segs, dtype=jnp.int32)[None, :]).astype(BF)
    inputs = x_in.astype(F32)
    mod_tok = dot_nn(one_hot, mod_row)
    shift1, scale1, gate1, shift2, scale2, gate2 = (
        mod_tok[:, part * width : (part + 1) * width] for part in range(6)
    )
    normed1, inv_std1 = norm_stats(inputs)
    modulated1 = (normed1 * (1.0 + scale1) + shift1).astype(BF)
    bias_float = query_value_bias.astype(F32)
    full_bias = jnp.concatenate(
        [bias_float[:width], jnp.zeros((width,), F32), bias_float[width:]]
    )
    qkv = (dot_nn(modulated1, w_qkv) + full_bias).astype(BF)
    if share > 1:
        kv_all = place.gather_parts(qkv[:, width:])
        parts = ((qkv, 0), (kv_all, 0), (kv_all, 1))
    else:
        parts = ((qkv, 0), (qkv, 1), (qkv, 2))
    attended, totals = attend_forward(parts, seg_query, seg_keys, heads)
    branch = dot_nn(attended, w_attn) + attn_out_bias.astype(F32)
    middle = inputs + gate1 * branch
    normed2, inv_std2 = norm_stats(middle)
    modulated2 = (normed2 * (1.0 + scale2) + shift2).astype(BF)
    hmid = dot_nn(modulated2, w_mlp_in) + mlp_in_bias.astype(F32)
    act_mid = jax.nn.gelu(hmid, approximate=True).astype(BF)
    mlp_branch = dot_nn(act_mid, w_mlp_out) + mlp_out_bias.astype(F32)
    out_low = (middle + gate2 * mlp_branch).astype(BF)
    hidden1 = dot_nn(out_low, w_proj_in) + proj_in_bias.astype(F32)
    act1 = jax.nn.silu(hidden1).astype(BF)
    hidden2 = dot_nn(act1, w_proj_mid) + proj_mid_bias.astype(F32)
    act2 = jax.nn.silu(hidden2).astype(BF)
    feats = dot_nn(act2, w_proj_out) + proj_out_bias.astype(F32)
    goals = goals.astype(F32)
    inv_feat = lax.rsqrt(jnp.sum(feats * feats, axis=-1, keepdims=True) + EPSILON)
    feat_unit = feats * inv_feat
    goal_unit = goals * lax.rsqrt(jnp.sum(goals * goals, axis=-1, keepdims=True) + EPSILON)
    cosine = jnp.sum(feat_unit * goal_unit, axis=-1, keepdims=True)
    loss_weight = 0.5 * goal_width
    grad_feats = (-loss_weight * inv_feat * (goal_unit - cosine * feat_unit)).astype(BF)

    def blocks(grad, cut):
        low = grad.astype(BF).reshape(seq, grad.shape[0] // seq, grad.shape[1])
        return [low[:, :, start : start + cut] for start in range(0, grad.shape[1], cut)]

    sixth_sum = reduce_bundle(
        jnp.concatenate(blocks(dot_tn(act2, grad_feats), goal_width), axis=1)
    )
    bias_out = jnp.sum(grad_feats.astype(F32), axis=0)
    grad_hidden2 = (dot_nt(grad_feats, w_proj_out) * silu_grad(hidden2)).astype(BF)
    fifth_sum = reduce_bundle(jnp.concatenate(blocks(dot_tn(act1, grad_hidden2), inner), axis=1))
    bias_mid = jnp.sum(grad_hidden2.astype(F32), axis=0)
    grad_hidden1 = (dot_nt(grad_hidden2, w_proj_mid) * silu_grad(hidden1)).astype(BF)
    fourth_sum = reduce_bundle(jnp.concatenate(blocks(dot_tn(out_low, grad_hidden1), half), axis=1))
    bias_in = jnp.sum(grad_hidden1.astype(F32), axis=0)
    grad_output = dot_nt(grad_hidden1, w_proj_in)
    grad_gate2 = grad_output * mlp_branch
    grad_mlp = (grad_output * gate2).astype(BF)
    third_sum = reduce_bundle(jnp.concatenate(blocks(dot_tn(act_mid, grad_mlp), width), axis=1))
    bias_ff_out = jnp.sum(grad_mlp.astype(F32), axis=0)
    grad_hmid = (dot_nt(grad_mlp, w_mlp_out) * gelu_grad(hmid)).astype(BF)
    second_sum = reduce_bundle(jnp.concatenate(blocks(dot_tn(modulated2, grad_hmid), width), axis=1))
    bias_ff_in = jnp.sum(grad_hmid.astype(F32), axis=0)
    grad_modulated2 = dot_nt(grad_hmid, w_mlp_in)
    grad_middle = grad_output + norm_back(grad_modulated2 * (1.0 + scale2), normed2, inv_std2)
    grad_gate1 = grad_middle * branch
    grad_branch = (grad_middle * gate1).astype(BF)
    grad_attn_w = dot_tn(attended, grad_branch)
    bias_attn = jnp.sum(grad_branch.astype(F32), axis=0)
    grad_attended = dot_nt(grad_branch, w_attn).astype(BF)
    grads = attend_backward(parts, seg_query, seg_keys, totals, attended, grad_attended, heads)
    if share > 1:
        grad_qkv = jnp.concatenate(
            [grads[0], place.sum_parts(grads[1]), place.sum_parts(grads[2])], axis=1
        )
    else:
        grad_qkv = grads[0][:, : 3 * width]
    first_sum = reduce_bundle(
        jnp.concatenate(
            blocks(dot_tn(modulated1, grad_qkv), width) + blocks(grad_attn_w, width), axis=1
        )
    )
    column_sums = jnp.sum(grad_qkv.astype(F32), axis=0)
    bias_qv = jnp.concatenate([column_sums[:width], column_sums[2 * width :]])
    grad_modulated1 = dot_nt(grad_qkv, w_qkv)
    grad_input = grad_middle + norm_back(grad_modulated1 * (1.0 + scale1), normed1, inv_std1)

    def by_segment(value):
        return dot_tn(one_hot, value.astype(BF))

    grad_mod = jnp.concatenate(
        [
            by_segment(grad_modulated1),
            by_segment(grad_modulated1 * normed1),
            by_segment(grad_gate1),
            by_segment(grad_modulated2),
            by_segment(grad_modulated2 * normed2),
            by_segment(grad_gate2),
        ],
        axis=-1,
    )
    grad_mod = place.all_parts(grad_mod)
    grad_modulation = lax.all_gather(grad_mod.astype(BF), "seq", axis=0)[:: share].astype(F32)

    def back(value):
        return place.to_spans(
            [value[shift * span : (shift + 1) * span] for shift in range(rows)]
        )

    block_out = back(out_low)
    grad_input = back(grad_input.astype(BF)).astype(F32)

    biases = [bias_qv, bias_attn, bias_ff_in, bias_ff_out, bias_in, bias_mid, bias_out]
    packed = jnp.concatenate([bias.reshape(seq, -1) for bias in biases], axis=1)
    packed = lax.psum(packed, EVERY)
    packed = lax.dynamic_index_in_dim(packed, lax.axis_index("seq"), 0, keepdims=False)
    shares = []
    start = 0
    for bias in biases:
        stop = start + bias.shape[0] // seq
        shares.append(packed[start:stop])
        start = stop

    def columns_of(total, count):
        return [total[start : start + count].astype(F32) for start in range(0, total.shape[0], count)]

    first_parts = columns_of(first_sum, per)
    return (
        block_out,
        grad_input,
        grad_modulation,
        jnp.concatenate(first_parts[:3], axis=1),
        shares[0],
        first_parts[3],
        shares[1],
        jnp.concatenate(columns_of(second_sum, per), axis=1),
        shares[2],
        third_sum.astype(F32),
        shares[3],
        jnp.concatenate(columns_of(fourth_sum, per), axis=1),
        shares[4],
        fifth_sum.astype(F32),
        shares[5],
        sixth_sum.astype(F32),
        shares[6],
    )


def tie(value, *others):
    return lax.optimization_barrier((value,) + others)[0]


def swap_cores(value):
    return lax.ppermute(value, "core", [(0, 1), (1, 0)])


def swap_planes(value, bit):
    return lax.ppermute(value, "plane", [(p, p ^ bit) for p in range(lax.axis_size("plane"))])


def scatter_planes(both, after=None):
    planes, seq, count, columns = both.shape
    flat = both.reshape(planes * seq * count, columns)
    if after is not None:
        flat = tie(flat, after)
    own = lax.psum_scatter(flat, "plane", scatter_dimension=0, tiled=True)
    return own.reshape(seq, count, columns)


def scatter_seq(both):
    seq, count, columns = both.shape
    return lax.psum_scatter(
        both.reshape(seq * count, columns), "seq", scatter_dimension=0, tiled=True
    )


def gather_copies(own):
    full = lax.all_gather(own, COPIES, axis=0, tiled=True)
    return full.reshape(lax.axis_size("plane"), 2, own.shape[0], own.shape[1])


def unpack_kernel(*refs):
    count = len(refs) // 2
    for full_ref, out_ref in zip(refs[:count], refs[count:]):
        out_ref[...] = square(full_ref[...]).astype(F32)


def unpack(*fulls):
    planes = fulls[0][0].shape[0]
    inputs, outputs = [], []
    for full, columns in fulls:
        _, _, count, cut = full.shape
        inputs.append(spec((1, 2, count, cut), lambda p: (p, 0, 0, 0)))
        if columns is None:
            outputs.append(
                ((planes * 2 * count, cut), F32, spec((2 * count, cut), lambda p: (p, 0)))
            )
        else:
            outputs.append(((2 * count, columns), F32, spec((2 * count, cut), lambda p: (0, p))))
    return call(
        unpack_kernel, (planes,), inputs, outputs, [full for full, _ in fulls], "unpack", 0
    )


def local_row(
    block_input, modulation, segment_ids,
    qkv_weight, query_value_bias,
    attn_out_weight, attn_out_bias,
    mlp_in_weight, mlp_in_bias,
    mlp_out_weight, mlp_out_bias,
    proj_in_weight, proj_in_bias,
    proj_mid_weight, proj_mid_bias,
    proj_out_weight, proj_out_bias,
    targets,
):
    rows, span, width = block_input.shape
    seq, planes = lax.axis_size("seq"), lax.axis_size("plane")
    heads = width // HEAD_DIM
    hidden = mlp_in_weight.shape[1]
    inner = proj_mid_weight.shape[1]
    goal_width = targets.shape[2]
    tokens = rows * span
    where = lax.axis_index("core").reshape(1).astype(jnp.int32)

    w1, x, seg_own = bring(
        [width],
        [[qkv_weight, attn_out_weight]],
        [block_input, segment_ids.reshape(rows, -1, LANES)],
        0,
    )
    x = x.reshape(tokens, width)
    seg_own = seg_own.reshape(tokens)
    mod_row = lax.dynamic_index_in_dim(modulation, lax.axis_index("seq"), 0, keepdims=False)
    mod = jnp.pad(mod_row, ((0, 16 - mod_row.shape[0]), (0, 0)))
    hot = (seg_own[:, None] == jnp.arange(16, dtype=jnp.int32)[None, :]).astype(BF)
    hott = (seg_own[None, :] == jnp.arange(16, dtype=jnp.int32)[:, None]).astype(BF)
    seg_column = seg_own[:, None]
    vector = lambda bias: bias.astype(F32)[None, :]

    per = qkv_weight.shape[0]
    bias_float = query_value_bias.astype(F32)
    full_bias = jnp.concatenate(
        [bias_float[:width], jnp.zeros((width,), F32), bias_float[width:]]
    )
    by_rows = lambda weight: weight.reshape(planes, -1, weight.shape[1])
    qkv, mod1t, attended, totals, w2, w3, goals = project(
        x, hot, mod, w1, full_bias[None, :], seg_column, heads,
        [width, width], [[mlp_in_weight], [by_rows(mlp_out_weight)]], targets, 3,
    )
    goals = goals.reshape(tokens, goal_width)
    parts = ((qkv, 0), (qkv, 1), (qkv, 2))
    branch, mid, low2, mod2t, attt = merge(attended, x, hot, mod, w1, vector(attn_out_bias))
    w3 = w3.reshape(hidden, width)
    actt, slope, out_low, outt, mlp_branch, w4, w5, w6 = feed(
        low2, w2, vector(mlp_in_bias), w3, vector(mlp_out_bias), mid, hot, mod,
        [inner // planes, inner, goal_width],
        [[proj_in_weight], [by_rows(proj_mid_weight)], [by_rows(proj_out_weight)]],
        5,
    )
    w5, w6 = w5.reshape(inner, inner), w6.reshape(inner, goal_width)
    act1t, act2t, gfeat, gh2, gh1, gout, block_out = align(
        out_low, w4, vector(proj_in_bias), w5, vector(proj_mid_bias), w6, vector(proj_out_bias),
        goals, 7,
    )
    half = functools.partial(weight_half, where, seq=seq, planes=planes)
    other6, column6 = half(act2t, tie(gfeat, gout), by_columns=False)
    got6 = swap_cores(other6)
    other5, column5 = half(act1t, tie(gh2, other6), by_columns=True)
    got5 = swap_cores(other5)
    other4, column4 = half(outt, tie(gh1, other5), by_columns=True)
    got4 = swap_cores(other4)
    (own6,) = half(act2t, tie(gfeat, other4), by_columns=False, got=got6)
    (own5,) = half(act1t, tie(gh2, own6), by_columns=True, got=got5)
    (own4,) = half(outt, tie(gh1, own5), by_columns=True, got=got4)
    plane6 = scatter_planes(own6)
    plane5 = scatter_planes(own5)
    plane4 = scatter_planes(own4)
    gmlp, ghmid, gmod2, ggate2 = feed_back(
        tie(gout, own4), mlp_branch, hot, hott, mod, w3, slope, w2
    )
    other3, column3 = half(actt, tie(gmlp, gmod2), by_columns=False)
    got3 = swap_cores(other3)
    other2, column2 = half(mod2t, tie(ghmid, other3), by_columns=True)
    got2 = swap_cores(other2)
    (own3,) = half(actt, tie(gmlp, other2), by_columns=False, got=got3)
    plane3 = scatter_planes(own3)
    gmid, gbranch, gatt, gshift2, gscale2, ggate1 = merge_back(
        gout, tie(gmod2, own3), mid, branch, hot, hott, mod, w1
    )
    half1 = functools.partial(weight_half, where, seq=seq, planes=1)
    other0, column0 = half1(attt, tie(gbranch, gatt), by_columns=True)
    got0 = swap_cores(other0)
    (own2,) = half(mod2t, tie(ghmid, other0), by_columns=True, got=got2)
    plane2 = scatter_planes(own2)
    (own0,) = half1(attt, tie(gbranch, own2), by_columns=True, got=got0)
    gqkv, sum6, sum4, sum5, own_attn = attend_backward(
        parts, seg_column, seg_column, totals, attended, tie(gatt, own0), heads,
        [plane6, plane4, plane5, own0[0]], 4,
    )
    other1, column1 = half(mod1t, tie(gqkv, other0), by_columns=True)
    got1 = swap_cores(other1)
    gin, gshift1, gscale1, sum3 = project_back(
        tie(gqkv, other1), x, gmid, hot, hott, mod, w1, [plane3], 6
    )
    (own1,) = half(mod1t, tie(gqkv, gin), by_columns=True, got=got1)
    plane1 = scatter_planes(own1)

    segs = modulation.shape[1]
    grad_mod = jnp.concatenate(
        [gshift1, gscale1, ggate1, gshift2, gscale2, ggate2], axis=1
    )[:segs].astype(BF)
    grad_mod = jnp.pad(grad_mod.reshape(-1, LANES), ((0, 8), (0, 0)))
    grad_mod = jnp.broadcast_to(grad_mod[None], (rows,) + grad_mod.shape)
    columns1 = column1[0]
    biases = [
        jnp.concatenate([columns1[:width], columns1[2 * width : 3 * width]]),
        column0[0], column2[0], column3[0], column4[0], column5[0], column6[0],
    ]
    packed = jnp.concatenate([bias.reshape(seq, -1) for bias in biases], axis=1)
    count = -(-packed.shape[1] // (8 * LANES)) * 8 * LANES
    packed = jnp.pad(packed, ((0, 0), (0, count - packed.shape[1]))).reshape(seq, -1, LANES)
    sum2, full6, full5, full4, full3, full0, grad_input = settle(
        [plane2],
        [sum6, sum5, sum4, sum3, tie(own_attn, own1)],
        [gin.reshape(block_input.shape)],
        [False] * 4 + [True],
        1,
    )
    _, _, full2, full1, all_bias, all_mod = settle(
        [tie(plane1, sum2), packed], [sum2], [grad_mod], [False, False, True], 2, True
    )
    grad_input = grad_input.astype(F32)
    grad3, grad4, grad5, grad6 = unpack(
        (full3, None), (full4, inner), (full5, inner), (full6, None)
    )
    grad2, grad1 = unpack((full2, hidden), (full1, 3 * width))
    grad_modulation = all_mod[:, :-8].reshape(rows, segs, 6 * width).astype(F32)

    packed = (all_bias[0] + all_bias[1]).reshape(-1)
    shares = []
    start = 0
    for bias in biases:
        stop = start + bias.shape[0] // seq
        shares.append(packed[start:stop])
        start = stop

    return (
        block_out,
        grad_input,
        grad_modulation,
        grad1,
        shares[0],
        full0.reshape(per, width).astype(F32),
        shares[1],
        grad2,
        shares[2],
        grad3,
        shares[3],
        grad4,
        shares[4],
        grad5,
        shares[5],
        grad6,
        shares[6],
    )


def solution(mesh):
    copies, seq = mesh.shape["dp"], mesh.shape["seq"]
    grid = jax.sharding.Mesh(
        mesh.devices.reshape(copies // 2, 2, seq), ("plane", "core", "seq")
    )
    rows, weight = P(COPIES, "seq", None), P("seq", None)
    placed = (rows, P(COPIES, None, None), P(COPIES, "seq")) + (weight, P()) * 7 + (rows,)

    def step(*args):
        per_device = args[0].shape[0] // copies
        one_row = per_device == seq and copies // 2 == seq and args[0].shape[1] == 1024
        return jax.shard_map(
            local_row if one_row else local,
            mesh=grid,
            in_specs=placed,
            out_specs=(rows, rows, P(COPIES, None, None)) + (weight, P("seq")) * 7,
            check_vma=False,
        )(*args)

    return step
```
